32 devices in a mesh: band: 4 (over y, x), tok: 8 (over z, core).
Axes of the slice: x: 2, y: 2, z: 4, core: 2. Of those that a mesh axis runs over, the one named last changes fastest.
Arguments:
- pixels: bfloat16 [4, 8, 1024, 768], P(None, 'tok', None, 'band'), may hold values from -6 to 6
- wavelengths: float32 [32], replicated, may hold values from 0.4 to 2.5
- wave_index: int32 [7, 12], replicated, may hold values from 0 to 31
- band_counts: int32 [7], replicated, may hold values from 1 to 12, as said below
- sensors: int32 [4, 8, 4], P(None, 'tok'), may hold values from 0 to 6
- chip_lengths: int32 [4, 8, 4], P(None, 'tok'), may hold values from 0 to 1024, as said below
- meta_rows: bfloat16 [4, 8, 4, 768], P('band', 'tok'), may hold values from -6 to 6
- w_qkv: bfloat16 [768, 2304], P(('band', 'tok')), may hold values from -0.21875 to 0.21875
- w_out: bfloat16 [768, 768], P(('band', 'tok')), may hold values from -0.875 to 0.875
- w_up: bfloat16 [768, 3072], P(('band', 'tok')), may hold values from -0.21875 to 0.21875
- b_up: bfloat16 [3072], P(('band', 'tok')), may hold values from -3 to 3
- w_down: bfloat16 [3072, 768], P(('band', 'tok')), may hold values from -0.109375 to 0.109375
- norm_gains: bfloat16 [2, 768], P(None, ('band', 'tok')), may hold values from 0.5 to 1.5
- shifts: bfloat16 [4, 768], P(None, ('band', 'tok')), may hold values from -3 to 3
- gen_qkv: float32 [128, 384], replicated, may hold values from -0.5 to 0.5
- gen_out: float32 [128, 128], replicated, may hold values from -0.5 to 0.5
- gen_ff1: float32 [128, 2048], replicated, may hold values from -0.5 to 0.5
- gen_ff2: float32 [2048, 128], replicated, may hold values from -0.125 to 0.125
- gen_gains: float32 [2, 128], replicated, may hold values from 0.5 to 1.5
- gen_shifts: float32 [2, 128], replicated, may hold values from -2 to 2
- latent_tokens: float32 [128, 128], replicated, may hold values from -6 to 6
- bias_token: float32 [128], replicated, may hold values from -6 to 6
- fc_kernel: float32 [128, 49152], P(None, 'tok'), may hold values from -0.0234375 to 0.0234375
- fc_bias: float32 [128, 768], replicated, may hold values from -0.25 to 0.25
- d_out: bfloat16 [4, 8, 1032, 768], P('band', 'tok'), may hold values from -6 to 6
Outputs:
- out: float32 [4, 8, 1032, 768], P('band', 'tok')
- d_pixels: float32 [4, 8, 1024, 768], P(None, 'tok', None, 'band')
- d_meta: float32 [4, 8, 4, 768], P('band', 'tok')
- d_w_qkv: float32 [768, 2304], P(('band', 'tok'))
- d_w_out: float32 [768, 768], P(('band', 'tok'))
- d_w_up: float32 [768, 3072], P(('band', 'tok'))
- d_b_up: float32 [3072], P(('band', 'tok'))
- d_w_down: float32 [3072, 768], P(('band', 'tok'))
- d_norm_gains: float32 [2, 768], P(None, ('band', 'tok'))
- d_shifts: float32 [4, 768], P(None, ('band', 'tok'))
- d_gen_qkv: float32 [128, 384], replicated
- d_gen_out: float32 [128, 128], replicated
- d_gen_ff1: float32 [128, 2048], replicated
- d_gen_ff2: float32 [2048, 128], replicated
- d_gen_gains: float32 [2, 128], replicated
- d_gen_shifts: float32 [2, 128], replicated
- d_latent: float32 [128, 128], replicated
- d_bias_token: float32 [128], replicated
- d_fc_kernel: float32 [128, 49152], P(None, 'tok')
- d_fc_bias: float32 [128, 768], replicated
The draws below stay inside these ranges and needn't reach their ends.
Inputs may be any that keep to these rules, and one draw needn't show every extreme that they name: `band_counts`: some sensor uses all 12 band slots. `chip_lengths`: each frame holds either one chip of 1024 patches in slot 0 with zeros in the other slots, or 4 chips of 256 patches; both kinds occur.
All inputs are finite; a program needn't handle non-finite values.
Results may differ from the reference program's by a relative error of at most 0.019.
Values may be sent and summed in bfloat16 or wider, within the bound.
No kernel may reach another device: no remote copies, remote signals or barrier semaphores. Data moves between devices by JAX's collectives and lax.ppermute only.
A program may use at most 256 MiB of HBM per device.

```python
import math
import jax
import jax.numpy as jnp
from jax import lax

D = 768
HEADS = 12
HD = 64
FF = 3072
WG = 128
GHEADS = 4
GHD = 32
GFF = 2048
NLAT = 128
PIX = 64
SENSORS = 7
BMAX = 12
NWAVE = 32
CHIP = 256
CAP = 4
FRAME = 1024
ROWS = 1032
TFRAMES = 8
N_BAND = 4


def draw_band_counts(key, part):
    counts_drawn = jax.random.randint(key, (SENSORS,), 1, BMAX + 1, dtype=jnp.int32)
    widest = jax.random.randint(jax.random.fold_in(key, 7), (), 0, SENSORS, dtype=jnp.int32)
    return jnp.where(jnp.arange(SENSORS, dtype=jnp.int32) == widest, BMAX, counts_drawn).astype(jnp.int32)


def draw_chip_lengths(key, part):
    single = jax.random.randint(key, (N_BAND, TFRAMES), 0, 2, dtype=jnp.int32)
    single = single.at[0, 0].set(1).at[0, 1].set(0)
    slot_index = jnp.arange(CAP, dtype=jnp.int32)
    one_chip = jnp.where(slot_index == 0, FRAME, 0).astype(jnp.int32)
    return jnp.where(single[:, :, None] == 1, one_chip[None, None, :], CHIP).astype(jnp.int32)


def set_ends(values, rng, least, largest):
    extent = values.shape
    place = [jax.random.randint(jax.random.fold_in(rng, axis), (), 0, extent[axis]) for axis in range(len(extent))]
    values = values.at[tuple(place)].set(least)
    longest = extent.index(max(extent))
    place[longest] = (place[longest] + 1) % extent[longest]
    return values.at[tuple(place)].set(largest)


def block_scale(stream_key, shape, pieces, least, high):
    def one(position, blocks):
        heights = jax.random.uniform(jax.random.fold_in(jax.random.fold_in(stream_key, 6), position), (blocks,), jnp.float32, least / len(pieces), high / len(pieces))
        return jnp.repeat(jnp.exp(heights), shape[position] // blocks).reshape((-1,) + (1,) * (len(shape) - position - 1))

    gain = one(*pieces[0])
    for cut in pieces[1:]:
        gain = gain * one(*cut)
    return gain


def bell_draw(rng, shape, width, bound, split=(), kind=jnp.bfloat16):
    values = width * jax.random.normal(rng, shape, jnp.float32)
    if split:
        values = values * block_scale(rng, shape, split, -0.22, 0.18)
    return jnp.clip(values, -bound, bound).astype(kind)


def setup_inputs(seed: int = 0) -> dict:
    seeds = jax.random.split(jax.random.key(seed), 26)
    return {
        "pixels": bell_draw(seeds[0], (N_BAND, TFRAMES, FRAME, BMAX * PIX), 1.0, 6.0, ((1, 8), (3, 4))),
        "wavelengths": jnp.clip(jnp.exp(jax.random.uniform(seeds[1], (NWAVE,), jnp.float32, math.log(0.4), math.log(2.5))), 0.4, 2.5),
        "wave_index": set_ends(jax.random.randint(seeds[2], (SENSORS, BMAX), 0, NWAVE), jax.random.fold_in(seeds[2], 1), 0, NWAVE - 1).astype(jnp.int32),
        "band_counts": draw_band_counts(jax.random.fold_in(seeds[25], 71), 0),
        "sensors": set_ends(jax.random.randint(seeds[4], (N_BAND, TFRAMES, CAP), 0, SENSORS), jax.random.fold_in(seeds[4], 1), 0, SENSORS - 1).astype(jnp.int32),
        "chip_lengths": draw_chip_lengths(jax.random.fold_in(seeds[25], 71), 0),
        "meta_rows": bell_draw(seeds[6], (N_BAND, TFRAMES, CAP, D), 1.0, 6.0, ((0, 4), (1, 8))),
        "w_qkv": bell_draw(seeds[7], (D, 3 * D), D ** -0.5, 0.21875, ((0, 32),)),
        "w_out": bell_draw(seeds[8], (D, D), (D // 16) ** -0.5, 0.875, ((0, 32),)),
        "w_up": bell_draw(seeds[9], (D, FF), D ** -0.5, 0.21875, ((0, 32),)),
        "b_up": bell_draw(seeds[10], (FF,), 0.5, 3.0, ((0, 32),)),
        "w_down": bell_draw(seeds[11], (FF, D), FF ** -0.5, 0.109375, ((0, 32),)),
        "norm_gains": jnp.clip(1.0 + 0.1 * jax.random.normal(seeds[12], (2, D), jnp.float32), 0.5, 1.5).astype(jnp.bfloat16),
        "shifts": bell_draw(seeds[13], (4, D), 0.5, 3.0, ((1, 32),)),
        "gen_qkv": bell_draw(seeds[14], (WG, 3 * WG), WG ** -0.5, 0.5, (), jnp.float32),
        "gen_out": bell_draw(seeds[15], (WG, WG), WG ** -0.5, 0.5, (), jnp.float32),
        "gen_ff1": bell_draw(seeds[16], (WG, GFF), WG ** -0.5, 0.5, (), jnp.float32),
        "gen_ff2": bell_draw(seeds[17], (GFF, WG), GFF ** -0.5, 0.125, (), jnp.float32),
        "gen_gains": jnp.clip(1.0 + 0.1 * jax.random.normal(seeds[18], (2, WG), jnp.float32), 0.5, 1.5),
        "gen_shifts": bell_draw(seeds[19], (2, WG), 0.3, 2.0, (), jnp.float32),
        "latent_tokens": bell_draw(seeds[20], (NLAT, WG), 1.0, 6.0, (), jnp.float32),
        "bias_token": bell_draw(seeds[21], (WG,), 1.0, 6.0, (), jnp.float32),
        "fc_kernel": bell_draw(seeds[22], (WG, PIX * D), (600 * WG) ** -0.5, 0.0234375, ((1, 8),), jnp.float32),
        "fc_bias": bell_draw(seeds[23], (WG, D), (4 * WG) ** -0.5, 0.25, (), jnp.float32),
        "d_out": bell_draw(seeds[24], (N_BAND, TFRAMES, ROWS, D), 1.0, 6.0, ((0, 4), (1, 8))),
    }


@jax.custom_vjp
def low(v):
    return lax.optimization_barrier(v.astype(jnp.bfloat16)).astype(jnp.float32)

@jax.custom_vjp
def low_back(v):
    return v

def low_keep(v):
    return (low(v), None)

def low_pass(kept, grad):
    return (grad,)

def back_keep(v):
    return (v, None)

def back_low(kept, grad):
    return (low(grad),)
low.defvjp(low_keep, low_pass)
low_back.defvjp(back_keep, back_low)
exact_precision = lax.Precision.HIGHEST
norm_epsilon = 1e-05
masked_score = -1000000000.0

def layer_norm(values, gain_row, shift_row):
    average = lax.optimization_barrier(jnp.mean(values, axis=-1, keepdims=True))
    centered = values - average
    variance = lax.optimization_barrier(jnp.mean(centered * centered, axis=-1, keepdims=True))
    return centered * lax.rsqrt(variance + norm_epsilon) * gain_row + shift_row

def wave_features(wavelengths, wave_index):
    table_size = wavelengths.shape[0]
    picked = (wave_index[..., None] == jnp.arange(table_size, dtype=jnp.int32)).astype(jnp.float32)
    wave_values = lax.optimization_barrier(jnp.sum(picked * wavelengths, axis=-1))
    half_width = WG // 2
    frequency = 1.0 / 10000.0 ** (jnp.arange(half_width, dtype=jnp.float32) / half_width)
    angles = 1000.0 * wave_values[..., None] * frequency
    return jnp.concatenate([jnp.sin(angles), jnp.cos(angles)], axis=-1)

def generator(gen_params, features, band_valid):
    gen_qkv, gen_out, gen_ff1, gen_ff2, gen_gains, gen_shifts, latent_tokens, bias_token = gen_params
    sensor_count = features.shape[0]
    sequence = jnp.concatenate([jnp.broadcast_to(latent_tokens, (sensor_count, NLAT, WG)), features, jnp.broadcast_to(bias_token, (sensor_count, 1, WG))], axis=1)
    key_valid = jnp.concatenate([jnp.ones((sensor_count, NLAT), jnp.bool_), band_valid, jnp.ones((sensor_count, 1), jnp.bool_)], axis=1)
    seq_length = sequence.shape[1]
    projected = jnp.einsum('slw,wk->slk', sequence, gen_qkv, precision=exact_precision)
    projected = projected.reshape(sensor_count, seq_length, 3, GHEADS, GHD)
    scores = jnp.einsum('sqhd,skhd->shqk', projected[:, :, 0], projected[:, :, 1], precision=exact_precision) / math.sqrt(GHD)
    scores = jnp.where(key_valid[:, None, None, :], scores, masked_score)
    attention = jax.nn.softmax(scores, axis=-1)
    mixed_heads = jnp.einsum('shqk,skhd->sqhd', attention, projected[:, :, 2], precision=exact_precision)
    mixed_heads = mixed_heads.reshape(sensor_count, seq_length, WG)
    first_norm = layer_norm(sequence + jnp.einsum('slw,wk->slk', mixed_heads, gen_out, precision=exact_precision), gen_gains[0], gen_shifts[0])
    inner_act = jax.nn.gelu(jnp.einsum('slw,wf->slf', first_norm, gen_ff1, precision=exact_precision), approximate=False)
    second = layer_norm(first_norm + jnp.einsum('slf,fw->slw', inner_act, gen_ff2, precision=exact_precision), gen_gains[1], gen_shifts[1])
    band_rows = second[:, NLAT:NLAT + BMAX] + features
    return (band_rows, second[:, -1])

def frame_forward(weights, frame_inputs):
    kernel, bias_vec, w_qkv, w_out, w_up, b_up, w_down, norm_gains, shifts = weights
    pixel_frame, block_sensor, row_segment, meta_frame = frame_inputs
    block_kernel_matrix = jnp.take(kernel, block_sensor, axis=0)
    embedded = jnp.einsum('crk,ckd->crd', pixel_frame.reshape(CAP, CHIP, BMAX * PIX), block_kernel_matrix, precision=exact_precision)
    embedded = low_back(embedded + jnp.take(bias_vec, block_sensor, axis=0)[:, None, :]).reshape(FRAME, D)
    class_rows = jnp.broadcast_to(shifts[3], (CAP, D))
    stream = jnp.concatenate([embedded, class_rows, meta_frame], axis=0)
    normed = low(layer_norm(stream, norm_gains[0], shifts[0]))
    projected = low_back(low(jnp.dot(normed, w_qkv, precision=exact_precision))).reshape(ROWS, 3, HEADS, HD)
    same_chip = row_segment[:, None] == row_segment[None, :]
    scores = low_back(jnp.einsum('qhd,khd->hqk', projected[:, 0], projected[:, 1], precision=exact_precision) * (1.0 / math.sqrt(HD)))
    scores = jnp.where(same_chip[None], scores, masked_score)
    probabilities = low(jax.nn.softmax(scores, axis=-1))
    attended = jnp.einsum('hqk,khd->qhd', probabilities, projected[:, 2], precision=exact_precision).reshape(ROWS, D)
    attended = low_back(low(attended))
    middle = stream + low_back(jnp.dot(attended, w_out, precision=exact_precision))
    normed_two = low(layer_norm(middle, norm_gains[1], shifts[1]))
    hidden_pre = low_back(jnp.dot(normed_two, w_up, precision=exact_precision) + b_up)
    activated = low_back(low(jax.nn.gelu(hidden_pre, approximate=False)))
    return middle + low_back(jnp.dot(activated, w_down, precision=exact_precision) + shifts[2])

def reference(pixels, wavelengths, wave_index, band_counts, sensors, chip_lengths, meta_rows, w_qkv, w_out, w_up, b_up, w_down, norm_gains, shifts, gen_qkv, gen_out, gen_ff1, gen_ff2, gen_gains, gen_shifts, latent_tokens, bias_token, fc_kernel, fc_bias, d_out):
    frames = N_BAND * TFRAMES
    features = wave_features(wavelengths, wave_index)
    band_valid = jnp.arange(BMAX, dtype=jnp.int32)[None, :] < band_counts[:, None]
    chip_ends = jnp.cumsum(chip_lengths.reshape(frames, CAP), axis=-1)
    positions = jnp.arange(FRAME, dtype=jnp.int32)
    patch_segment = lax.optimization_barrier(jnp.sum((chip_ends[:, None, :] <= positions[None, :, None]).astype(jnp.int32), axis=-1))
    block_starts = jnp.arange(CAP, dtype=jnp.int32) * CHIP
    block_segment = lax.optimization_barrier(jnp.sum((chip_ends[:, None, :] <= block_starts[None, :, None]).astype(jnp.int32), axis=-1))
    block_sensor = jnp.take_along_axis(sensors.reshape(frames, CAP), block_segment, axis=1)
    extra_segment = jnp.broadcast_to(jnp.arange(CAP, dtype=jnp.int32), (frames, CAP))
    row_segment = jnp.concatenate([patch_segment, extra_segment, extra_segment], axis=1)

    def forward(pixel_all, meta_all, qkv_weight, out_weight, up_weight, up_bias, down_weight, gains_all, shifts_all, gen_qkv_f, gen_out_f, gen_ff1_f, gen_ff2_f, gen_gains_f, gen_shifts_f, latent_f, bias_token_f, fc_kernel_f, fc_bias_f):
        band_rows, last_rows = generator((gen_qkv_f, gen_out_f, gen_ff1_f, gen_ff2_f, gen_gains_f, gen_shifts_f, latent_f, bias_token_f), features, band_valid)
        kernel = jnp.dot(band_rows.reshape(SENSORS * BMAX, WG), fc_kernel_f, precision=exact_precision)
        kernel = kernel * band_valid.reshape(SENSORS * BMAX, 1).astype(jnp.float32)
        kernel = low(kernel).reshape(SENSORS, BMAX * PIX, D)
        bias_vec = jnp.dot(last_rows, fc_bias_f, precision=exact_precision)
        weights = (kernel, bias_vec, qkv_weight, out_weight, up_weight, up_bias, down_weight, gains_all, shifts_all)
        checked = jax.checkpoint(frame_forward)

        def frame_step(frame_inputs):
            return checked(weights, frame_inputs)
        inputs = (pixel_all.reshape(frames, FRAME, BMAX * PIX), block_sensor, row_segment, meta_all.reshape(frames, CAP, D))
        outputs = lax.map(frame_step, inputs)
        return outputs.reshape(N_BAND, TFRAMES, ROWS, D)
    primals = (pixels.astype(jnp.float32), meta_rows.astype(jnp.float32), w_qkv.astype(jnp.float32), w_out.astype(jnp.float32), w_up.astype(jnp.float32), b_up.astype(jnp.float32), w_down.astype(jnp.float32), norm_gains.astype(jnp.float32), shifts.astype(jnp.float32), gen_qkv, gen_out, gen_ff1, gen_ff2, gen_gains, gen_shifts, latent_tokens, bias_token, fc_kernel, fc_bias)
    result, pullback = jax.vjp(forward, *primals)
    gradients = pullback(d_out.astype(jnp.float32))
    return (result, gradients[0], gradients[1], gradients[2], gradients[3], gradients[4], gradients[5], gradients[6], gradients[7], gradients[8], gradients[9], gradients[10], gradients[11], gradients[12], gradients[13], gradients[14], gradients[15], gradients[16], gradients[17], gradients[18])
```

```python
import math

import jax
import jax.numpy as jnp
from jax import lax
from jax.experimental import pallas as pl
from jax.experimental.pallas import tpu as pltpu
from jax.sharding import PartitionSpec as P

D = 768
HEADS = 12
HD = 64
FF = 3072
WG = 128
GHEADS = 4
GHD = 32
GFF = 2048
NLAT = 128
PIX = 64
SENSORS = 7
BMAX = 12
CHIP = 256
CAP = 4
FRAME = 1024
ROWS = 1032
RP = 1040
CH = 208
BANDS = 4
SLOTS = BMAX // BANDS
OWN = SENSORS * SLOTS
QX = 96

f32 = jnp.float32
bf16 = jnp.bfloat16
BT = ("band", "tok")
HIGH = lax.Precision.HIGHEST
EPS = 1e-05
MASKED = -1000000000.0
MIB = 2**20


def mm(a, b):
    return lax.dot_general(a, b, (((1,), (0,)), ((), ())), preferred_element_type=f32)


def mm_nt(a, b):
    return lax.dot_general(a, b, (((1,), (1,)), ((), ())), preferred_element_type=f32)


def mm_tn(a, b):
    return lax.dot_general(a, b, (((0,), (0,)), ((), ())), preferred_element_type=f32)


def xmm(a, b, dims=((1,), (0,))):
    return lax.dot_general(a, b, (dims, ((), ())), precision=HIGH, preferred_element_type=f32)


def whole(shape):
    return pl.BlockSpec(shape, lambda *_: (0,) * len(shape))


def like(shape, dtype):
    return jax.ShapeDtypeStruct(shape, dtype)


def params(mib):
    return pltpu.CompilerParams(vmem_limit_bytes=mib * MIB)


def center(x):
    xc = x - jnp.mean(x, axis=1, keepdims=True)
    r = lax.rsqrt(jnp.mean(xc * xc, axis=1, keepdims=True) + EPS)
    return xc * r, r


def gelu_parts(u):
    phi = 0.5 + 0.5 * lax.erf(u * math.sqrt(0.5))
    slope = phi + u * (math.sqrt(0.5 / math.pi) * jnp.exp(-0.5 * u * u))
    return u * phi, slope


def col8(v):
    return jnp.sum(v.reshape(v.shape[0] // 8, 8, v.shape[1]), axis=0)


def total(v):
    return jnp.sum(v, axis=0, keepdims=True)


def head_lanes(h):
    lane = lax.broadcasted_iota(jnp.int32, (1, WG), 1)
    return (lane // GHD == h).astype(f32)


def gen_forward(x, latent, bias, w_qkv, w_out, ff1, ff2, gains, shifts):
    scale = 1.0 / math.sqrt(GHD)
    qkv = xmm(x, w_qkv)
    kv = xmm(latent, w_qkv[:, WG:])
    q = qkv[:, :WG] * scale
    k = jnp.concatenate([kv[:, :WG], qkv[:, WG : 2 * WG]], axis=0)
    v = jnp.concatenate([kv[:, WG:], qkv[:, 2 * WG :]], axis=0)
    mixed = jnp.zeros((QX, WG), f32)
    probs = []
    for h in range(GHEADS):
        lanes = head_lanes(h)
        s = xmm(q * lanes, k, ((1,), (1,))) + bias
        e = jnp.exp(s - jnp.max(s, axis=1, keepdims=True))
        p = e / jnp.sum(e, axis=1, keepdims=True)
        probs.append(p)
        mixed = mixed + xmm(p, v * lanes)
    hat1, r1 = center(x + xmm(mixed, w_out))
    z1 = hat1 * gains[0:1] + shifts[0:1]
    act, slope = gelu_parts(xmm(z1, ff1))
    hat2, r2 = center(z1 + xmm(act, ff2))
    z2 = hat2 * gains[1:2] + shifts[1:2]
    return z2, (q, k, v, probs, mixed, hat1, r1, z1, act, slope, hat2, r2)


def gen_fwd_kernel(x, latent, bias, w_qkv, w_out, ff1, ff2, gains, shifts, fc_bias, z2_o, bias_o):
    z2, _ = gen_forward(
        x[...], latent[...], bias[...], w_qkv[...], w_out[...], ff1[...], ff2[...], gains[...], shifts[...]
    )
    z2_o[...] = z2
    bias_o[...] = xmm(z2[QX - 8 :], fc_bias[...])


def gen_fwd(x, latent, bias, w_qkv, w_out, ff1, ff2, gains, shifts, fc_bias):
    args = (x, latent, bias, w_qkv, w_out, ff1, ff2, gains, shifts, fc_bias)
    return pl.pallas_call(
        gen_fwd_kernel,
        in_specs=[whole(a.shape) for a in args],
        out_specs=[whole((QX, WG)), whole((8, D))],
        out_shape=[like((QX, WG), f32), like((8, D), f32)],
        compiler_params=params(40),
        name="gen_fwd",
    )(*args)


def norm_back(g, hat, r, gain):
    s = g * gain
    return r * (s - jnp.mean(s, axis=1, keepdims=True) - hat * jnp.mean(s * hat, axis=1, keepdims=True))


def gen_bwd_kernel(
    x, latent, bias, w_qkv, w_out, ff1, ff2, gains, shifts, fc_bias, dh, dbias,
    dqkv_o, dout_o, dff1_o, dff2_o, dgains_o, dshifts_o, dlat_o, dtok_o, dfcb_o,
):
    scale = 1.0 / math.sqrt(GHD)
    xv, lat, gainv = x[...], latent[...], gains[...]
    z2, (q, k, v, probs, mixed, hat1, r1, z1, act, slope, hat2, r2) = gen_forward(
        xv, lat, bias[...], w_qkv[...], w_out[...], ff1[...], ff2[...], gainv, shifts[...]
    )
    db = dbias[...]
    dfcb_o[...] = xmm(z2[QX - 8 :], db, ((0,), (0,)))
    dz2 = jnp.concatenate([dh[...], xmm(db, fc_bias[...], ((1,), (1,)))], axis=0)
    dw2 = norm_back(dz2, hat2, r2, gainv[1:2])
    dff2_o[...] = xmm(act, dw2, ((0,), (0,)))
    du = xmm(dw2, ff2[...], ((1,), (1,))) * slope
    dff1_o[...] = xmm(z1, du, ((0,), (0,)))
    dz1 = dw2 + xmm(du, ff1[...], ((1,), (1,)))
    dw1 = norm_back(dz1, hat1, r1, gainv[0:1])
    dgains_o[...] = jnp.concatenate([total(dz1 * hat1), total(dz2 * hat2)], axis=0)
    dshifts_o[...] = jnp.concatenate([total(dz1), total(dz2)], axis=0)
    dout_o[...] = xmm(mixed, dw1, ((0,), (0,)))
    dmix = xmm(dw1, w_out[...], ((1,), (1,)))
    dq = jnp.zeros((QX, WG), f32)
    dk = jnp.zeros((NLAT + QX, WG), f32)
    dv = jnp.zeros((NLAT + QX, WG), f32)
    for h in range(GHEADS):
        lanes = head_lanes(h)
        p = probs[h]
        dm = dmix * lanes
        dp = xmm(dm, v, ((1,), (1,)))
        ds = p * (dp - jnp.sum(p * dp, axis=1, keepdims=True))
        dv = dv + xmm(p, dm, ((0,), (0,)))
        dq = dq + xmm(ds, k * lanes)
        dk = dk + xmm(ds, q * lanes, ((0,), (0,)))
    dq = dq * scale
    dx = jnp.concatenate([dq, dk[NLAT:], dv[NLAT:]], axis=1)
    dl = jnp.concatenate([dk[:NLAT], dv[:NLAT]], axis=1)
    wv = w_qkv[...]
    from_x = xmm(xv, dx, ((0,), (0,)))
    from_l = xmm(lat, dl, ((0,), (0,)))
    dqkv_o[:, :WG] = from_x[:, :WG]
    dqkv_o[:, WG:] = from_x[:, WG:] + from_l
    dlat_o[...] = xmm(dl, wv[:, WG:], ((1,), (1,)))
    dx_full = dw1 + xmm(dx, wv, ((1,), (1,)))
    dtok_o[...] = total(dx_full[QX - 8 : QX - 8 + SENSORS])


def gen_bwd(x, latent, bias, w_qkv, w_out, ff1, ff2, gains, shifts, fc_bias, dh, dbias):
    args = (x, latent, bias, w_qkv, w_out, ff1, ff2, gains, shifts, fc_bias, dh, dbias)
    shapes = [(WG, 3 * WG), (WG, WG), (WG, GFF), (GFF, WG), (2, WG), (2, WG), (NLAT, WG), (1, WG), (WG, D)]
    return pl.pallas_call(
        gen_bwd_kernel,
        in_specs=[whole(a.shape) for a in args],
        out_specs=[whole(s) for s in shapes],
        out_shape=[like(s, f32) for s in shapes],
        compiler_params=params(48),
        name="gen_bwd",
    )(*args)


def embed_kernel(sens, pix, kmat, bias, extra, gains, shifts, x0_o, n1_o):
    c = pl.program_id(0)
    rows = pl.ds(c * CHIP, CHIP)
    row = bias[pl.ds(sens[c], 1), :]
    x = mm_tn(pix[...], kmat[0]) + row
    x0_o[rows, :] = x
    hat, _ = center(x)
    n1_o[rows, :] = (hat * gains[0:1] + shifts[0:1]).astype(bf16)

    @pl.when(c == CAP - 1)
    def _():
        e = extra[...]
        x0_o[FRAME:, :] = e
        h, _ = center(e)
        n1_o[FRAME:, :] = (h * gains[0:1] + shifts[0:1]).astype(bf16)


def embed(sens, pix, kmat, bias, extra, gains, shifts):
    return pl.pallas_call(
        embed_kernel,
        grid_spec=pltpu.PrefetchScalarGridSpec(
            num_scalar_prefetch=1,
            grid=(CAP,),
            in_specs=[
                pl.BlockSpec((D, CHIP), lambda c, s: (0, c)),
                pl.BlockSpec((1, D, D), lambda c, s: (s[c], 0, 0)),
                whole((8, D)),
                whole((RP - FRAME, D)),
                whole((8, D)),
                whole((8, D)),
            ],
            out_specs=[whole((RP, D)), whole((RP, D))],
        ),
        out_shape=[like((RP, D), f32), like((RP, D), bf16)],
        compiler_params=params(40),
        name="embed",
    )(sens, pix, kmat, bias, extra, gains, shifts)


def pixel_grad_kernel(sens, band, de, kmat, pix, dpix_o, dker_o, acc):
    n = pl.program_id(0)
    g = de[0]
    dpix_o[0] = mm_nt(kmat[0], g)

    @pl.when(n == 0)
    def _():
        acc[...] = jnp.zeros_like(acc)

    s = sens[n]
    acc[s] = acc[s] + mm(pix[0], g)

    @pl.when(n == pl.num_programs(0) - 1)
    def _():
        dker_o[...] = acc[...]


def pixel_grad(sens, band, de, kmat, pix):
    blocks = BANDS * CAP
    width = SLOTS * PIX
    return pl.pallas_call(
        pixel_grad_kernel,
        grid_spec=pltpu.PrefetchScalarGridSpec(
            num_scalar_prefetch=2,
            grid=(blocks,),
            in_specs=[
                pl.BlockSpec((1, CHIP, D), lambda n, s, b: (n, 0, 0)),
                pl.BlockSpec((1, width, D), lambda n, s, b: (s[n], b[0], 0)),
                pl.BlockSpec((1, width, CHIP), lambda n, s, b: (n // CAP, 0, n % CAP)),
            ],
            out_specs=[
                pl.BlockSpec((1, width, CHIP), lambda n, s, b: (n // CAP, 0, n % CAP)),
                whole((SENSORS, width, D)),
            ],
            scratch_shapes=[pltpu.VMEM((SENSORS, width, D), f32)],
        ),
        out_shape=[like((BANDS, width, FRAME), f32), like((SENSORS, width, D), f32)],
        compiler_params=params(40),
        name="pixel_grad",
    )(sens, band, de, kmat, pix)


GH = 4
GW = GH * HD
GROUPS = HEADS // GH


def attn_fwd_kernel(n1, wq, wk, wv, wo, x0, qa, ka, gains, shifts, q_o, k_o, v_o, o_o, p_o, x1_o, n2_o):
    g = pl.program_id(0)

    @pl.when(g == 0)
    def _():
        x1_o[...] = x0[...]

    for c in range(RP // CH):
        s = pl.ds(c * CH, CH)
        q_o[s, :] = mm(n1[s, :], wq[...]).astype(bf16)
        k_o[s, :] = mm(n1[s, :], wk[...]).astype(bf16)
        v_o[s, :] = mm(n1[s, :], wv[...]).astype(bf16)
    qav = qa[...]
    kav = ka[...]
    for h in range(GH):
        hs = slice(h * HD, (h + 1) * HD)
        kh = jnp.concatenate([k_o[:, hs], kav], axis=1)
        vh = v_o[:, hs]
        for c in range(RP // CH):
            s = pl.ds(c * CH, CH)
            qh = jnp.concatenate([q_o[s, hs] * jnp.bfloat16(0.125), qav[c * CH : (c + 1) * CH]], axis=1)
            sc = mm_nt(qh, kh)
            e = jnp.exp(sc - jnp.max(sc, axis=1, keepdims=True))
            p = (e * (1.0 / jnp.sum(e, axis=1, keepdims=True))).astype(bf16)
            p_o[h, s, :] = p
            o_o[s, hs] = mm(p, vh).astype(bf16)
    for c in range(RP // CH):
        s = pl.ds(c * CH, CH)
        x1_o[s, :] += mm(o_o[s, :], wo[...])

    @pl.when(g == pl.num_programs(0) - 1)
    def _():
        for c in range(RP // CH):
            s = pl.ds(c * CH, CH)
            hat, _ = center(x1_o[s, :])
            n2_o[s, :] = (hat * gains[1:2, :] + shifts[1:2, :]).astype(bf16)


def attn_fwd(n1, w_qkv, w_out, x0, qa, ka, gains, shifts):
    G = GROUPS
    return pl.pallas_call(
        attn_fwd_kernel,
        grid=(G,),
        in_specs=[
            whole((RP, D)),
            pl.BlockSpec((D, GW), lambda g: (0, g)),
            pl.BlockSpec((D, GW), lambda g: (0, G + g)),
            pl.BlockSpec((D, GW), lambda g: (0, 2 * G + g)),
            pl.BlockSpec((GW, D), lambda g: (g, 0)),
            whole((RP, D)),
            whole((RP, HD)),
            whole((RP, HD)),
            whole((8, D)),
            whole((8, D)),
        ],
        out_specs=[pl.BlockSpec((RP, GW), lambda g: (0, g))] * 4
        + [pl.BlockSpec((GH, RP, RP), lambda g: (g, 0, 0)), whole((RP, D)), whole((RP, D))],
        out_shape=[like((RP, D), bf16)] * 4
        + [like((HEADS, RP, RP), bf16), like((RP, D), f32), like((RP, D), bf16)],
        compiler_params=params(60),
        name="attn_fwd",
    )(n1, w_qkv, w_qkv, w_qkv, w_out, x0, qa, ka, gains, shifts)


def attn_bwd_kernel(
    dx1b, wo, q, k, v, o, p, wq, wk, wv, n1, x0, dx1, gains,
    dwo, dwq, dwk, dwv, de_o, tail_o, small_o, dn1_s, do_s, dq_s, dk_s, dv_s, ds_s,
):
    g = pl.program_id(0)

    @pl.when(g == 0)
    def _():
        dn1_s[...] = jnp.zeros_like(dn1_s)

    for c in range(RP // CH):
        s = pl.ds(c * CH, CH)
        do_s[s, :] = mm_nt(dx1b[s, :], wo[...]).astype(bf16)
    dwo[...] = mm_tn(o[...], dx1b[...]).astype(bf16)
    for h in range(GH):
        hs = slice(h * HD, (h + 1) * HD)
        vh = v[:, hs]
        kh = k[:, hs]
        qh = q[:, hs]
        doh = do_s[:, hs]
        for c in range(RP // CH):
            s = pl.ds(c * CH, CH)
            dc = do_s[s, hs]
            inner = jnp.sum(dc.astype(f32) * o[s, hs].astype(f32), axis=1, keepdims=True)
            ds = (p[h, s, :].astype(f32) * (mm_nt(dc, vh) - inner)).astype(bf16)
            ds_s[s, :] = ds
            dq_s[s, hs] = (mm(ds, kh) * 0.125).astype(bf16)
        dk_s[:, hs] = (mm_tn(ds_s[...], qh) * 0.125).astype(bf16)
        dv_s[:, hs] = mm_tn(p[h], doh).astype(bf16)
    for c in range(RP // CH):
        s = pl.ds(c * CH, CH)
        dn1_s[s, :] += mm_nt(dq_s[s, :], wq[...]) + mm_nt(dk_s[s, :], wk[...]) + mm_nt(dv_s[s, :], wv[...])
    dwq[...] = mm_tn(n1[...], dq_s[...]).astype(bf16)
    dwk[...] = mm_tn(n1[...], dk_s[...]).astype(bf16)
    dwv[...] = mm_tn(n1[...], dv_s[...]).astype(bf16)

    @pl.when(g == pl.num_programs(0) - 1)
    def _():
        gg = jnp.zeros((8, D), f32)
        gs = jnp.zeros((8, D), f32)
        for c in range(RP // CH):
            s = pl.ds(c * CH, CH)
            hat, r = center(x0[s, :])
            gr = dn1_s[s, :]
            gg = gg + col8(gr * hat)
            gs = gs + col8(gr)
            dn1_s[s, :] = dx1[s, :] + norm_back(gr, hat, r, gains[0:1, :])
        de_o[...] = dn1_s[:FRAME, :].astype(bf16)
        tail_o[...] = dn1_s[FRAME:, :]
        small_o[0:1, :] = total(gg)
        small_o[1:2, :] = total(gs)
        small_o[2:8, :] = jnp.zeros((6, D), f32)


def attn_bwd(dx1b, w_out, q, k, v, o, p, w_qkv, n1, x0, dx1, gains):
    G = GROUPS
    col = pl.BlockSpec((RP, GW), lambda g: (0, g))
    return pl.pallas_call(
        attn_bwd_kernel,
        grid=(G,),
        in_specs=[
            whole((RP, D)),
            pl.BlockSpec((GW, D), lambda g: (g, 0)),
            col,
            col,
            col,
            col,
            pl.BlockSpec((GH, RP, RP), lambda g: (g, 0, 0)),
            pl.BlockSpec((D, GW), lambda g: (0, g)),
            pl.BlockSpec((D, GW), lambda g: (0, G + g)),
            pl.BlockSpec((D, GW), lambda g: (0, 2 * G + g)),
            whole((RP, D)),
            whole((RP, D)),
            whole((RP, D)),
            whole((8, D)),
        ],
        out_specs=[pl.BlockSpec((GW, D), lambda g: (g, 0))]
        + [pl.BlockSpec((D, GW), lambda g: (0, g))] * 3
        + [whole((FRAME, D)), whole((RP - FRAME, D)), whole((8, D))],
        out_shape=[like((D, D), bf16)] * 4
        + [like((FRAME, D), bf16), like((RP - FRAME, D), f32), like((8, D), f32)],
        scratch_shapes=[pltpu.VMEM((RP, D), f32)]
        + [pltpu.VMEM((RP, GW), bf16)] * 4
        + [pltpu.VMEM((RP, RP), bf16)],
        compiler_params=params(62),
        name="attn_bwd",
    )(dx1b, w_out, q, k, v, o, p, w_qkv, w_qkv, w_qkv, n1, x0, dx1, gains)


FB = 512


def ffn_kernel(
    n2, dout, x1, wup, bup, wdown, gains, shifts,
    out, dwup, dwdown, dbup, dx1_o, dx1b_o, small_o, act_s, du_s, dn2_s, out_s,
):
    j = pl.program_id(0)

    @pl.when(j == 0)
    def _():
        out_s[...] = x1[...] + shifts[2:3, :]
        dn2_s[...] = jnp.zeros_like(dn2_s)

    cs = jnp.zeros((8, FB), f32)
    for c in range(RP // CH):
        s = pl.ds(c * CH, CH)
        u = mm(n2[s, :], wup[...]) + bup[...]
        da = mm_nt(dout[s, :], wdown[...]).astype(bf16).astype(f32)
        act, slope = gelu_parts(u)
        act = act.astype(bf16)
        act_s[s, :] = act
        du = (da * slope).astype(bf16)
        du_s[s, :] = du
        cs = cs + col8(du.astype(f32))
        out_s[s, :] += mm(act, wdown[...])
        dn2_s[s, :] += mm_nt(du, wup[...])
    dbup[...] = jnp.broadcast_to(total(cs), (8, FB))
    dwup[...] = mm_tn(n2[...], du_s[...]).astype(bf16)
    dwdown[...] = mm_tn(act_s[...], dout[...]).astype(bf16)

    @pl.when(j == pl.num_programs(0) - 1)
    def _():
        out[...] = out_s[:ROWS, :]
        gg = jnp.zeros((8, D), f32)
        gs = jnp.zeros((8, D), f32)
        gd = jnp.zeros((8, D), f32)
        for c in range(RP // CH):
            s = pl.ds(c * CH, CH)
            hat, r = center(x1[s, :])
            g = dn2_s[s, :]
            do = dout[s, :].astype(f32)
            gg = gg + col8(g * hat)
            gs = gs + col8(g)
            gd = gd + col8(do)
            dx1 = do + norm_back(g, hat, r, gains[1:2, :])
            dx1_o[s, :] = dx1
            dx1b_o[s, :] = dx1.astype(bf16)
        small_o[0:1, :] = total(gg)
        small_o[1:2, :] = total(gs)
        small_o[2:3, :] = total(gd)
        small_o[3:8, :] = jnp.zeros((5, D), f32)


def ffn(n2, dout, x1, w_up, b_up, w_down, gains, shifts):
    return pl.pallas_call(
        ffn_kernel,
        grid=(FF // FB,),
        in_specs=[
            whole((RP, D)),
            whole((RP, D)),
            whole((RP, D)),
            pl.BlockSpec((D, FB), lambda g: (0, g)),
            pl.BlockSpec((1, FB), lambda g: (0, g)),
            pl.BlockSpec((FB, D), lambda g: (g, 0)),
            whole((8, D)),
            whole((8, D)),
        ],
        out_specs=[
            whole((ROWS, D)),
            pl.BlockSpec((D, FB), lambda g: (0, g)),
            pl.BlockSpec((FB, D), lambda g: (g, 0)),
            pl.BlockSpec((8, FB), lambda g: (0, g)),
            whole((RP, D)),
            whole((RP, D)),
            whole((8, D)),
        ],
        out_shape=[
            like((ROWS, D), f32),
            like((D, FF), bf16),
            like((FF, D), bf16),
            like((8, FF), f32),
            like((RP, D), f32),
            like((RP, D), bf16),
            like((8, D), f32),
        ],
        scratch_shapes=[pltpu.VMEM((RP, FB), bf16)] * 2 + [pltpu.VMEM((RP, D), f32)] * 2,
        compiler_params=params(60),
        name="ffn",
    )(n2, dout, x1, w_up, b_up, w_down, gains, shifts)


def wave_features(wavelengths, wave_index):
    table_size = wavelengths.shape[0]
    picked = (wave_index[..., None] == jnp.arange(table_size, dtype=jnp.int32)).astype(f32)
    wave_values = jnp.sum(picked * wavelengths, axis=-1)
    half_width = WG // 2
    frequency = 1.0 / 10000.0 ** (jnp.arange(half_width, dtype=f32) / half_width)
    angles = 1000.0 * wave_values[..., None] * frequency
    return jnp.concatenate([jnp.sin(angles), jnp.cos(angles)], axis=-1)


def shards(
    pixels, wavelengths, wave_index, band_counts, sensors, chip_lengths, meta_rows,
    w_qkv, w_out, w_up, b_up, w_down, norm_gains, shifts,
    gen_qkv, gen_out, gen_ff1, gen_ff2, gen_gains, gen_shifts, latent_tokens, bias_token,
    fc_kernel, fc_bias, d_out,
):
    band = lax.axis_index("band")
    tok = lax.axis_index("tok")
    toks = lax.axis_size("tok")
    devices = BANDS * toks
    me = band * toks + tok
    share = D // devices
    ff_share = FF // devices
    pix_share = PIX // toks
    width = SLOTS * PIX

    extras = jnp.concatenate(
        [norm_gains.T, shifts.T, b_up.reshape(share, ff_share // share), jnp.zeros((share, 118), bf16)], axis=1
    )
    gathered = lax.all_gather(jnp.concatenate([w_qkv, w_out, extras, w_up], axis=1), BT, axis=0, tiled=True)
    qkv_all = gathered[:, : 3 * D]
    out_all = gathered[:, 3 * D : 4 * D]
    rest = gathered[:, 4 * D : 4 * D + WG].astype(f32)
    up_all = gathered[:, 4 * D + WG :]
    down_all = lax.all_gather(w_down, BT, axis=0, tiled=True)
    gains = jnp.pad(rest[:, :2].T, ((0, 6), (0, 0)))
    shift_rows = jnp.pad(rest[:, 2:6].T, ((0, 4), (0, 0)))
    bias_up = rest[:, 6:10].reshape(1, FF)

    pix_t = pixels.reshape(BANDS, FRAME, width).transpose(0, 2, 1)
    pix_own = lax.all_to_all(pix_t, "band", 0, 0, tiled=True).reshape(BMAX * PIX, FRAME)

    features = wave_features(wavelengths, wave_index).reshape(SENSORS * BMAX, WG)
    valid = jnp.arange(BMAX, dtype=jnp.int32)[None, :] < band_counts[:, None]
    seq = jnp.concatenate([features, jnp.zeros((4, WG), f32), jnp.broadcast_to(bias_token, (8, WG))], axis=0)
    sensor_ids = jnp.arange(SENSORS, dtype=jnp.int32)
    row_sensor = jnp.concatenate(
        [jnp.repeat(sensor_ids, BMAX), jnp.full((4,), 8, jnp.int32), sensor_ids, jnp.full((1,), 9, jnp.int32)]
    )
    key_ok = jnp.concatenate([valid.reshape(-1), jnp.zeros((4,), jnp.bool_), jnp.ones((8,), jnp.bool_)])
    allowed = (row_sensor[:, None] == row_sensor[None, :]) & key_ok[None, :]
    gen_bias = jnp.concatenate([jnp.zeros((QX, NLAT), f32), jnp.where(allowed, 0.0, MASKED)], axis=1)
    gen_args = (seq, latent_tokens, gen_bias, gen_qkv, gen_out, gen_ff1, gen_ff2, gen_gains, gen_shifts, fc_bias)
    z2, bias_vec = gen_fwd(*gen_args)
    h_all = (z2[: SENSORS * BMAX] + features).reshape(SENSORS, BMAX, WG)
    valid_f = valid.astype(f32)

    h_own = lax.dynamic_slice_in_dim(h_all, band * SLOTS, SLOTS, 1).reshape(OWN, WG)
    valid_own = lax.dynamic_slice_in_dim(valid_f, band * SLOTS, SLOTS, 1).reshape(OWN, 1)
    part = (jnp.dot(h_own, fc_kernel, precision=HIGH) * valid_own).astype(bf16).reshape(OWN, pix_share, D)
    kernels = lax.all_gather(part, BT, axis=0, tiled=False)
    kmat = (
        kernels.reshape(BANDS, toks, SENSORS, SLOTS, pix_share, D)
        .transpose(2, 0, 3, 1, 4, 5)
        .reshape(SENSORS, BMAX * PIX, D)
    )

    ends = jnp.cumsum(chip_lengths.reshape(BANDS, CAP), axis=-1)
    starts = jnp.arange(CAP, dtype=jnp.int32) * CHIP
    block_segment = jnp.sum((ends[:, None, :] <= starts[None, :, None]).astype(jnp.int32), axis=-1)
    block_sensor = jnp.take_along_axis(sensors.reshape(BANDS, CAP), block_segment, axis=1)
    own_ends = lax.dynamic_slice_in_dim(ends, band, 1, 0).reshape(CAP)
    own_sensor = lax.dynamic_slice_in_dim(block_sensor, band, 1, 0).reshape(CAP)
    positions = jnp.arange(FRAME, dtype=jnp.int32)
    patch_segment = jnp.sum((own_ends[None, :] <= positions[:, None]).astype(jnp.int32), axis=-1)
    slot_ids = jnp.arange(CAP, dtype=jnp.int32)
    segment = jnp.concatenate([patch_segment, slot_ids, slot_ids, jnp.full((RP - ROWS,), CAP + 1, jnp.int32)])
    onehot = segment[:, None] == jnp.arange(HD, dtype=jnp.int32)[None, :]
    ka = onehot.astype(bf16)
    qa = jnp.where(onehot, 0.0, -(2.0**30)).astype(bf16)

    extra_rows = jnp.concatenate(
        [
            jnp.broadcast_to(shift_rows[3], (CAP, D)),
            meta_rows.reshape(CAP, D).astype(f32),
            jnp.zeros((RP - ROWS, D), f32),
        ],
        axis=0,
    )
    x0, n1 = embed(own_sensor, pix_own, kmat, bias_vec, extra_rows, gains, shift_rows)
    q, k, v, o, probs, x1, n2 = attn_fwd(n1, qkv_all, out_all, x0, qa, ka, gains, shift_rows)
    dout = jnp.pad(d_out.reshape(ROWS, D), ((0, RP - ROWS), (0, 0)))
    out, d_up, d_down, d_bup, dx1, dx1b, small2 = ffn(n2, dout, x1, up_all, bias_up, down_all, gains, shift_rows)
    ff_grads = jnp.concatenate(
        [
            d_up.reshape(devices, share, 4, D).transpose(0, 2, 1, 3).reshape(devices, 4 * share, D),
            d_down.reshape(devices, ff_share, D),
        ],
        axis=1,
    )
    ff_shard = lax.psum_scatter(ff_grads, BT, scatter_dimension=0, tiled=False).astype(f32)
    d_wo, d_wq, d_wk, d_wv, de, tail_rows, small1 = attn_bwd(
        dx1b, out_all, q, k, v, o, probs, qkv_all, n1, x0, dx1, gains
    )
    proj_shard = lax.psum_scatter(
        jnp.concatenate([d_wq, d_wk, d_wv, d_wo], axis=1), BT, scatter_dimension=0, tiled=True
    ).astype(f32)

    de_all = lax.all_gather(de, "band", axis=0, tiled=False)
    d_pix, d_ker = pixel_grad(
        block_sensor.reshape(-1), band.reshape(1), de_all.reshape(BANDS * CAP, CHIP, D), kmat, pix_t
    )
    d_ker = (d_ker.reshape(OWN, PIX, D) * valid_own[:, :, None]).astype(bf16)
    d_cols = lax.psum_scatter(d_ker, "tok", scatter_dimension=1, tiled=True)
    d_cols_all = lax.all_gather(d_cols, "band", axis=0, tiled=False).astype(f32)
    d_cols_all = (
        d_cols_all.reshape(BANDS, SENSORS, SLOTS, pix_share * D)
        .transpose(1, 0, 2, 3)
        .reshape(SENSORS * BMAX, pix_share * D)
    )
    d_fc = xmm(h_all.reshape(SENSORS * BMAX, WG), d_cols_all, ((0,), (0,)))
    dh = lax.psum(xmm(d_cols_all, fc_kernel, ((1,), (1,))), "tok")

    block_sums = jnp.sum(de.reshape(CAP, CHIP, D).astype(f32), axis=1)
    pick = (own_sensor[None, :] == sensor_ids[:, None]).astype(f32)
    d_bias = jnp.sum(pick[:, :, None] * block_sums[None], axis=1)
    d_class = jnp.sum(tail_rows[:CAP], axis=0, keepdims=True)
    smalls = lax.psum(
        jnp.concatenate(
            [d_bup[0].reshape(4, D), small1[0:1], small2[0:1], small1[1:2], small2[1:3], d_class, d_bias], axis=0
        ),
        BT,
    )
    dbias_full = jnp.pad(smalls[10:17], ((0, 1), (0, 0)))
    g = gen_bwd(*gen_args, jnp.pad(dh, ((0, 4), (0, 0))), dbias_full)
    bup_shard = lax.dynamic_slice_in_dim(smalls[0:4].reshape(FF), me * ff_share, ff_share, 0)
    gains_shard = lax.dynamic_slice_in_dim(smalls[4:6], me * share, share, 1)
    shifts_shard = lax.dynamic_slice_in_dim(smalls[6:10], me * share, share, 1)
    up_shard = ff_shard[: 4 * share].reshape(4, share, D).transpose(1, 0, 2).reshape(share, FF)
    return (
        out.reshape(1, 1, ROWS, D),
        d_pix.transpose(0, 2, 1).reshape(BANDS, 1, FRAME, width),
        tail_rows[CAP : 2 * CAP].reshape(1, 1, CAP, D),
        proj_shard[:, : 3 * D],
        proj_shard[:, 3 * D :],
        up_shard,
        bup_shard,
        ff_shard[4 * share :],
        gains_shard,
        shifts_shard,
        g[0],
        g[1],
        g[2],
        g[3],
        g[4],
        g[5],
        g[6],
        g[7].reshape(WG),
        d_fc,
        g[8],
    )


def solution(mesh):
    both = ("band", "tok")
    placed = (
        P(None, "tok", None, "band"),
        P(),
        P(),
        P(),
        P(None, "tok", None),
        P(None, "tok", None),
        P("band", "tok", None, None),
        P(both, None),
        P(both, None),
        P(both, None),
        P(both),
        P(both, None),
        P(None, both),
        P(None, both),
        P(),
        P(),
        P(),
        P(),
        P(),
        P(),
        P(),
        P(),
        P(None, "tok"),
        P(),
        P("band", "tok", None, None),
    )
    return jax.shard_map(
        shards,
        mesh=mesh,
        in_specs=placed,
        out_specs=(
            P("band", "tok", None, None),
            P(None, "tok", None, "band"),
            P("band", "tok", None, None),
            P(both, None),
            P(both, None),
            P(both, None),
            P(both),
            P(both, None),
            P(None, both),
            P(None, both),
            P(),
            P(),
            P(),
            P(),
            P(),
            P(),
            P(),
            P(),
            P(None, "tok"),
            P(),
        ),
        check_vma=False,
    )
```

```python
import math

import jax
import jax.numpy as jnp
from jax import lax
from jax.experimental import pallas as pl
from jax.experimental.pallas import tpu as pltpu
from jax.sharding import PartitionSpec as P

D = 768
HEADS = 12
HD = 64
FF = 3072
WG = 128
GHEADS = 4
GHD = 32
GFF = 2048
NLAT = 128
PIX = 64
SENSORS = 7
BMAX = 12
CHIP = 256
CAP = 4
FRAME = 1024
ROWS = 1032
RP = 1040
CH = 208
BANDS = 4
SLOTS = BMAX // BANDS
OWN = SENSORS * SLOTS
HALF = D // 2
QX = 96

f32 = jnp.float32
bf16 = jnp.bfloat16
BT = ("band", "tok")
HIGH = lax.Precision.HIGHEST
EPS = 1e-05
MASKED = -1000000000.0
MIB = 2**20


def mm(a, b):
    return lax.dot_general(a, b, (((1,), (0,)), ((), ())), preferred_element_type=f32)


def mm_nt(a, b):
    return lax.dot_general(a, b, (((1,), (1,)), ((), ())), preferred_element_type=f32)


def mm_tn(a, b):
    return lax.dot_general(a, b, (((0,), (0,)), ((), ())), preferred_element_type=f32)


def xmm(a, b, dims=((1,), (0,))):
    return lax.dot_general(a, b, (dims, ((), ())), precision=HIGH, preferred_element_type=f32)


def whole(shape):
    return pl.BlockSpec(shape, lambda *_: (0,) * len(shape))


def like(shape, dtype):
    return jax.ShapeDtypeStruct(shape, dtype)


def params(mib):
    return pltpu.CompilerParams(vmem_limit_bytes=mib * MIB)


def center(x):
    xc = x - jnp.mean(x, axis=1, keepdims=True)
    r = lax.rsqrt(jnp.mean(xc * xc, axis=1, keepdims=True) + EPS)
    return xc * r, r


def gelu_parts(u):
    phi = 0.5 + 0.5 * lax.erf(u * math.sqrt(0.5))
    slope = phi + u * (math.sqrt(0.5 / math.pi) * jnp.exp(-0.5 * u * u))
    return u * phi, slope


def col8(v):
    return jnp.sum(v.reshape(v.shape[0] // 8, 8, v.shape[1]), axis=0)


def total(v):
    return jnp.sum(v, axis=0, keepdims=True)


def head_lanes(h):
    lane = lax.broadcasted_iota(jnp.int32, (1, WG), 1)
    return (lane // GHD == h).astype(f32)


def gen_forward(x, latent, bias, w_qkv, w_out, ff1, ff2, gains, shifts):
    scale = 1.0 / math.sqrt(GHD)
    qkv = xmm(x, w_qkv)
    kv = xmm(latent, w_qkv[:, WG:])
    q = qkv[:, :WG] * scale
    k = jnp.concatenate([kv[:, :WG], qkv[:, WG : 2 * WG]], axis=0)
    v = jnp.concatenate([kv[:, WG:], qkv[:, 2 * WG :]], axis=0)
    mixed = jnp.zeros((QX, WG), f32)
    probs = []
    for h in range(GHEADS):
        lanes = head_lanes(h)
        s = xmm(q * lanes, k, ((1,), (1,))) + bias
        e = jnp.exp(s - jnp.max(s, axis=1, keepdims=True))
        p = e / jnp.sum(e, axis=1, keepdims=True)
        probs.append(p)
        mixed = mixed + xmm(p, v * lanes)
    hat1, r1 = center(x + xmm(mixed, w_out))
    z1 = hat1 * gains[0:1] + shifts[0:1]
    act, slope = gelu_parts(xmm(z1, ff1))
    hat2, r2 = center(z1 + xmm(act, ff2))
    z2 = hat2 * gains[1:2] + shifts[1:2]
    return z2, (q, k, v, probs, mixed, hat1, r1, z1, act, slope, hat2, r2)


def gen_fwd_kernel(x, latent, bias, w_qkv, w_out, ff1, ff2, gains, shifts, fc_bias, z2_o, bias_o):
    z2, _ = gen_forward(
        x[...], latent[...], bias[...], w_qkv[...], w_out[...], ff1[...], ff2[...], gains[...], shifts[...]
    )
    z2_o[...] = z2
    bias_o[...] = xmm(z2[QX - 8 :], fc_bias[...])


def gen_fwd(x, latent, bias, w_qkv, w_out, ff1, ff2, gains, shifts, fc_bias):
    args = (x, latent, bias, w_qkv, w_out, ff1, ff2, gains, shifts, fc_bias)
    return pl.pallas_call(
        gen_fwd_kernel,
        in_specs=[whole(a.shape) for a in args],
        out_specs=[whole((QX, WG)), whole((8, D))],
        out_shape=[like((QX, WG), f32), like((8, D), f32)],
        compiler_params=params(40),
        name="gen_fwd",
    )(*args)


def norm_back(g, hat, r, gain):
    s = g * gain
    return r * (s - jnp.mean(s, axis=1, keepdims=True) - hat * jnp.mean(s * hat, axis=1, keepdims=True))


def gen_bwd_kernel(
    x, latent, bias, w_qkv, w_out, ff1, ff2, gains, shifts, fc_bias, dh, dbias,
    dqkv_o, dout_o, dff1_o, dff2_o, dgains_o, dshifts_o, dlat_o, dtok_o, dfcb_o,
):
    scale = 1.0 / math.sqrt(GHD)
    xv, lat, gainv = x[...], latent[...], gains[...]
    z2, (q, k, v, probs, mixed, hat1, r1, z1, act, slope, hat2, r2) = gen_forward(
        xv, lat, bias[...], w_qkv[...], w_out[...], ff1[...], ff2[...], gainv, shifts[...]
    )
    db = dbias[...]
    dfcb_o[...] = xmm(z2[QX - 8 :], db, ((0,), (0,)))
    dz2 = jnp.concatenate([dh[...], xmm(db, fc_bias[...], ((1,), (1,)))], axis=0)
    dw2 = norm_back(dz2, hat2, r2, gainv[1:2])
    dff2_o[...] = xmm(act, dw2, ((0,), (0,)))
    du = xmm(dw2, ff2[...], ((1,), (1,))) * slope
    dff1_o[...] = xmm(z1, du, ((0,), (0,)))
    dz1 = dw2 + xmm(du, ff1[...], ((1,), (1,)))
    dw1 = norm_back(dz1, hat1, r1, gainv[0:1])
    dgains_o[...] = jnp.concatenate([total(dz1 * hat1), total(dz2 * hat2)], axis=0)
    dshifts_o[...] = jnp.concatenate([total(dz1), total(dz2)], axis=0)
    dout_o[...] = xmm(mixed, dw1, ((0,), (0,)))
    dmix = xmm(dw1, w_out[...], ((1,), (1,)))
    dq = jnp.zeros((QX, WG), f32)
    dk = jnp.zeros((NLAT + QX, WG), f32)
    dv = jnp.zeros((NLAT + QX, WG), f32)
    for h in range(GHEADS):
        lanes = head_lanes(h)
        p = probs[h]
        dm = dmix * lanes
        dp = xmm(dm, v, ((1,), (1,)))
        ds = p * (dp - jnp.sum(p * dp, axis=1, keepdims=True))
        dv = dv + xmm(p, dm, ((0,), (0,)))
        dq = dq + xmm(ds, k * lanes)
        dk = dk + xmm(ds, q * lanes, ((0,), (0,)))
    dq = dq * scale
    dx = jnp.concatenate([dq, dk[NLAT:], dv[NLAT:]], axis=1)
    dl = jnp.concatenate([dk[:NLAT], dv[:NLAT]], axis=1)
    wv = w_qkv[...]
    from_x = xmm(xv, dx, ((0,), (0,)))
    from_l = xmm(lat, dl, ((0,), (0,)))
    dqkv_o[:, :WG] = from_x[:, :WG]
    dqkv_o[:, WG:] = from_x[:, WG:] + from_l
    dlat_o[...] = xmm(dl, wv[:, WG:], ((1,), (1,)))
    dx_full = dw1 + xmm(dx, wv, ((1,), (1,)))
    dtok_o[...] = total(dx_full[QX - 8 : QX - 8 + SENSORS])


def gen_bwd(x, latent, bias, w_qkv, w_out, ff1, ff2, gains, shifts, fc_bias, dh, dbias):
    args = (x, latent, bias, w_qkv, w_out, ff1, ff2, gains, shifts, fc_bias, dh, dbias)
    shapes = [(WG, 3 * WG), (WG, WG), (WG, GFF), (GFF, WG), (2, WG), (2, WG), (NLAT, WG), (1, WG), (WG, D)]
    return pl.pallas_call(
        gen_bwd_kernel,
        in_specs=[whole(a.shape) for a in args],
        out_specs=[whole(s) for s in shapes],
        out_shape=[like(s, f32) for s in shapes],
        compiler_params=params(48),
        name="gen_bwd",
    )(*args)


def embed_kernel(sens, core, *refs):
    pix = refs[:BANDS]
    own = refs[BANDS : 2 * BANDS]
    other = refs[2 * BANDS : 3 * BANDS]
    bias, extra, gains, shifts, x0_o, n1_o = refs[3 * BANDS :]
    c = pl.program_id(0)
    rows = pl.ds(c * CHIP, CHIP)
    row = bias[pl.ds(sens[c], 1), :]
    for half, ker in ((core[0], own), (1 - core[0], other)):
        acc = mm_tn(pix[0][...], ker[0][0])
        for r in range(1, BANDS):
            acc = acc + mm_tn(pix[r][...], ker[r][0])
        x0_o[rows, pl.ds(pl.multiple_of(half * HALF, HALF), HALF)] = acc
    x = x0_o[rows, :] + row
    x0_o[rows, :] = x
    hat, _ = center(x)
    n1_o[rows, :] = (hat * gains[0:1] + shifts[0:1]).astype(bf16)

    @pl.when(c == CAP - 1)
    def _():
        e = extra[...]
        x0_o[FRAME:, :] = e
        h, _ = center(e)
        n1_o[FRAME:, :] = (h * gains[0:1] + shifts[0:1]).astype(bf16)


def embed(sens, core, pix, own, other, bias, extra, gains, shifts):
    width = SLOTS * PIX
    return pl.pallas_call(
        embed_kernel,
        grid_spec=pltpu.PrefetchScalarGridSpec(
            num_scalar_prefetch=2,
            grid=(CAP,),
            in_specs=[pl.BlockSpec((width, CHIP), lambda c, *_: (0, c))] * BANDS
            + [pl.BlockSpec((1, width, HALF), lambda c, s, _: (s[c], 0, 0))] * (2 * BANDS)
            + [whole((8, D)), whole((RP - FRAME, D)), whole((8, D)), whole((8, D))],
            out_specs=[whole((RP, D)), whole((RP, D))],
        ),
        out_shape=[like((RP, D), f32), like((RP, D), bf16)],
        compiler_params=params(40),
        cost_estimate=pl.CostEstimate(flops=2 * FRAME * D * D, bytes_accessed=14 * MIB, transcendentals=0),
        name="embed",
    )(sens, core, *pix, *own, *other, bias, extra, gains, shifts)


def pixel_grad_kernel(first, sens, frames, core, de, k_own, k_oth, pix, *refs):
    if first:
        dpix_o, dker_o = refs
    else:
        _, before, dpix_o, dker_o = refs
    n = pl.program_id(0)

    @pl.when(n == 0)
    def _():
        dker_o[...] = jnp.zeros_like(dker_o) if first else before[...]

    g = de[0]
    lo = pl.ds(pl.multiple_of(core[0] * HALF, HALF), HALF)
    hi = pl.ds(pl.multiple_of((1 - core[0]) * HALF, HALF), HALF)
    dpix_o[0] = mm_nt(k_own[0], de[0, :, lo]) + mm_nt(k_oth[0], de[0, :, hi])
    s = sens[n]
    dker_o[s] = dker_o[s] + mm(pix[0], g)


def pixel_grad(sens, frames, core, de, k_own, k_oth, pix, before):
    blocks = de.shape[0]
    width = SLOTS * PIX
    first = not before
    here = pl.BlockSpec((1, width, CHIP), lambda n, s, f, c: (f[n // CAP], 0, n % CAP))
    kern = pl.BlockSpec((1, width, HALF), lambda n, s, f, c: (s[n], 0, 0))
    more = [] if first else [pl.BlockSpec(memory_space=pl.ANY), whole((SENSORS, width, D))]
    return pl.pallas_call(
        lambda *refs: pixel_grad_kernel(first, *refs),
        grid_spec=pltpu.PrefetchScalarGridSpec(
            num_scalar_prefetch=3,
            grid=(blocks,),
            in_specs=[pl.BlockSpec((1, CHIP, D), lambda n, s, f, c: (n, 0, 0)), kern, kern, here] + more,
            out_specs=[here, whole((SENSORS, width, D))],
        ),
        out_shape=[like((BANDS, width, FRAME), f32), like((SENSORS, width, D), f32)],
        input_output_aliases={} if first else {7: 0, 8: 1},
        compiler_params=params(40),
        cost_estimate=pl.CostEstimate(
            flops=blocks * 4 * CHIP * D * width, bytes_accessed=blocks * MIB, transcendentals=0
        ),
        name="pixel_grad",
    )(sens, frames, core, de, k_own, k_oth, pix, *before)


GH = 4
GW = GH * HD
GROUPS = HEADS // GH


def attn_fwd_kernel(n1, wq, wk, wv, wo, x0, qa, ka, gains, shifts, q_o, k_o, v_o, o_o, p_o, x1_o, n2_o):
    g = pl.program_id(0)

    @pl.when(g == 0)
    def _():
        x1_o[...] = x0[...]

    for c in range(RP // CH):
        s = pl.ds(c * CH, CH)
        q_o[s, :] = mm(n1[s, :], wq[...]).astype(bf16)
        k_o[s, :] = mm(n1[s, :], wk[...]).astype(bf16)
        v_o[s, :] = mm(n1[s, :], wv[...]).astype(bf16)
    qav = qa[...]
    kav = ka[...]
    for h in range(GH):
        hs = slice(h * HD, (h + 1) * HD)
        kh = jnp.concatenate([k_o[:, hs], kav], axis=1)
        vh = v_o[:, hs]
        for c in range(RP // CH):
            s = pl.ds(c * CH, CH)
            qh = jnp.concatenate([q_o[s, hs] * jnp.bfloat16(0.125), qav[c * CH : (c + 1) * CH]], axis=1)
            sc = mm_nt(qh, kh)
            e = jnp.exp(sc - jnp.max(sc, axis=1, keepdims=True))
            p = (e * (1.0 / jnp.sum(e, axis=1, keepdims=True))).astype(bf16)
            p_o[h, s, :] = p
            o_o[s, hs] = mm(p, vh).astype(bf16)
    for c in range(RP // CH):
        s = pl.ds(c * CH, CH)
        x1_o[s, :] += mm(o_o[s, :], wo[...])

    @pl.when(g == pl.num_programs(0) - 1)
    def _():
        for c in range(RP // CH):
            s = pl.ds(c * CH, CH)
            hat, _ = center(x1_o[s, :])
            n2_o[s, :] = (hat * gains[1:2, :] + shifts[1:2, :]).astype(bf16)


def attn_fwd(n1, weights, x0, qa, ka, gains, shifts):
    return pl.pallas_call(
        attn_fwd_kernel,
        grid=(GROUPS,),
        in_specs=[
            whole((RP, D)),
            pl.BlockSpec((D, GW), lambda g: (0, g)),
            pl.BlockSpec((D, GW), lambda g: (0, GROUPS + g)),
            pl.BlockSpec((D, GW), lambda g: (0, 2 * GROUPS + g)),
            pl.BlockSpec((GW, D), lambda g: (g, 3)),
            whole((RP, D)),
            whole((RP, HD)),
            whole((RP, HD)),
            whole((8, D)),
            whole((8, D)),
        ],
        out_specs=[pl.BlockSpec((RP, GW), lambda g: (0, g))] * 4
        + [pl.BlockSpec((GH, RP, RP), lambda g: (g, 0, 0)), whole((RP, D)), whole((RP, D))],
        out_shape=[like((RP, D), bf16)] * 4
        + [like((HEADS, RP, RP), bf16), like((RP, D), f32), like((RP, D), bf16)],
        compiler_params=params(60),
        cost_estimate=pl.CostEstimate(flops=5 * 10**10, bytes_accessed=50 * MIB, transcendentals=0),
        name="attn_fwd",
    )(n1, weights, weights, weights, weights, x0, qa, ka, gains, shifts)


def attn_bwd_kernel(
    last, dx1b, wo, q, k, v, o, p, wq, wk, wv, n1, before, *refs
):
    if last:
        x0, dx1, gains, dwo, dwq, dwk, dwv, de_o, tail_o, small_o, dn1_s, do_s, dq_s, dk_s, dv_s, ds_s = refs
    else:
        dwo, dwq, dwk, dwv, dn1_s, do_s, dq_s, dk_s, dv_s, ds_s = refs
    g = pl.program_id(0)

    @pl.when(g == 0)
    def _():
        dn1_s[...] = before[...]

    for c in range(RP // CH):
        s = pl.ds(c * CH, CH)
        do_s[s, :] = mm_nt(dx1b[s, :], wo[...]).astype(bf16)
    dwo[...] = mm_tn(o[...], dx1b[...]).astype(bf16)
    for h in range(GH):
        hs = slice(h * HD, (h + 1) * HD)
        vh = v[:, hs]
        kh = k[:, hs]
        qh = q[:, hs]
        doh = do_s[:, hs]
        for c in range(RP // CH):
            s = pl.ds(c * CH, CH)
            dc = do_s[s, hs]
            inner = jnp.sum(dc.astype(f32) * o[s, hs].astype(f32), axis=1, keepdims=True)
            ds = (p[h, s, :].astype(f32) * (mm_nt(dc, vh) - inner)).astype(bf16)
            ds_s[s, :] = ds
            dq_s[s, hs] = (mm(ds, kh) * 0.125).astype(bf16)
        dk_s[:, hs] = (mm_tn(ds_s[...], qh) * 0.125).astype(bf16)
        dv_s[:, hs] = mm_tn(p[h], doh).astype(bf16)
    for c in range(RP // CH):
        s = pl.ds(c * CH, CH)
        dn1_s[s, :] += mm_nt(dq_s[s, :], wq[...]) + mm_nt(dk_s[s, :], wk[...]) + mm_nt(dv_s[s, :], wv[...])
    dwq[...] = mm_tn(n1[...], dq_s[...]).astype(bf16)
    dwk[...] = mm_tn(n1[...], dk_s[...]).astype(bf16)
    dwv[...] = mm_tn(n1[...], dv_s[...]).astype(bf16)
    if not last:
        return

    @pl.when(g == pl.num_programs(0) - 1)
    def _():
        gg = jnp.zeros((8, D), f32)
        gs = jnp.zeros((8, D), f32)
        for c in range(RP // CH):
            s = pl.ds(c * CH, CH)
            hat, r = center(x0[s, :])
            gr = dn1_s[s, :]
            gg = gg + col8(gr * hat)
            gs = gs + col8(gr)
            dn1_s[s, :] = dx1[s, :] + norm_back(gr, hat, r, gains[0:1, :])
        de_o[...] = dn1_s[:FRAME, :].astype(bf16)
        tail_o[...] = dn1_s[FRAME:, :]
        small_o[0:1, :] = total(gg)
        small_o[1:2, :] = total(gs)
        small_o[2:8, :] = jnp.zeros((6, D), f32)


def attn_bwd(start, count, last, dx1b, weights, q, k, v, o, p, n1, before, ends=()):
    col = pl.BlockSpec((RP, GW), lambda g: (0, start + g))
    grads = [like((count * GW, D), bf16)] + [like((D, count * GW), bf16)] * 3
    grad_specs = [pl.BlockSpec((GW, D), lambda g: (g, 0))] + [pl.BlockSpec((D, GW), lambda g: (0, g))] * 3
    work = [pltpu.VMEM((RP, GW), bf16)] * 4 + [pltpu.VMEM((RP, RP), bf16)]
    if last:
        out_shape = grads + [like((FRAME, D), bf16), like((RP - FRAME, D), f32), like((8, D), f32)]
        out_specs = grad_specs + [whole((FRAME, D)), whole((RP - FRAME, D)), whole((8, D))]
        work = [pltpu.VMEM((RP, D), f32)] + work
    else:
        out_shape = grads + [like((RP, D), f32)]
        out_specs = grad_specs + [whole((RP, D))]
    return pl.pallas_call(
        lambda *refs: attn_bwd_kernel(last, *refs),
        grid=(count,),
        in_specs=[
            whole((RP, D)),
            pl.BlockSpec((GW, D), lambda g: (start + g, 3)),
            col,
            col,
            col,
            col,
            pl.BlockSpec((GH, RP, RP), lambda g: (start + g, 0, 0)),
            pl.BlockSpec((D, GW), lambda g: (0, start + g)),
            pl.BlockSpec((D, GW), lambda g: (0, GROUPS + start + g)),
            pl.BlockSpec((D, GW), lambda g: (0, 2 * GROUPS + start + g)),
            whole((RP, D)),
            whole((RP, D)),
        ]
        + ([whole((RP, D)), whole((RP, D)), whole((8, D))] if last else []),
        out_specs=out_specs,
        out_shape=out_shape,
        scratch_shapes=work,
        compiler_params=params(62),
        cost_estimate=pl.CostEstimate(flops=count * 2 * 10**10, bytes_accessed=count * 20 * MIB, transcendentals=0),
        name="attn_bwd",
    )(dx1b, weights, q, k, v, o, p, weights, weights, weights, n1, before, *ends)


FB = 768


def ffn_kernel(
    n2, dout, x1, wup, bup, wdown, gains, shifts,
    out, dw, dbup, dx1_o, dx1b_o, small_o, act_s, du_s, dn2_s, out_s,
):
    j = pl.program_id(0)

    @pl.when(j == 0)
    def _():
        out_s[...] = x1[...] + shifts[2:3, :]
        dn2_s[...] = jnp.zeros_like(dn2_s)

    cs = jnp.zeros((8, FB), f32)
    for c in range(RP // CH):
        s = pl.ds(c * CH, CH)
        u = mm(n2[s, :], wup[...]) + bup[...]
        da = mm_nt(dout[s, :], wdown[...]).astype(bf16).astype(f32)
        act, slope = gelu_parts(u)
        act = act.astype(bf16)
        act_s[s, :] = act
        du = (da * slope).astype(bf16)
        du_s[s, :] = du
        cs = cs + col8(du.astype(f32))
        out_s[s, :] += mm(act, wdown[...])
        dn2_s[s, :] += mm_nt(du, wup[...])
    dbup[...] = jnp.broadcast_to(total(cs), (8, FB))
    dw[:, :FB] = mm_tn(n2[...], du_s[...]).astype(bf16)
    dw[:, FB:] = mm_tn(act_s[...], dout[...]).astype(bf16)

    @pl.when(j == pl.num_programs(0) - 1)
    def _():
        out[...] = out_s[:ROWS, :]
        gg = jnp.zeros((8, D), f32)
        gs = jnp.zeros((8, D), f32)
        gd = jnp.zeros((8, D), f32)
        for c in range(RP // CH):
            s = pl.ds(c * CH, CH)
            hat, r = center(x1[s, :])
            g = dn2_s[s, :]
            do = dout[s, :].astype(f32)
            gg = gg + col8(g * hat)
            gs = gs + col8(g)
            gd = gd + col8(do)
            dx1 = do + norm_back(g, hat, r, gains[1:2, :])
            dx1_o[s, :] = dx1
            dx1b_o[s, :] = dx1.astype(bf16)
        small_o[0:1, :] = total(gg)
        small_o[1:2, :] = total(gs)
        small_o[2:3, :] = total(gd)
        small_o[3:8, :] = jnp.zeros((5, D), f32)


def ffn(n2, dout, x1, weights, b_up, gains, shifts):
    return pl.pallas_call(
        ffn_kernel,
        grid=(FF // FB,),
        in_specs=[
            whole((RP, D)),
            whole((RP, D)),
            whole((RP, D)),
            pl.BlockSpec((D, FB), lambda g: (0, 4 + g)),
            pl.BlockSpec((1, FB), lambda g: (0, g)),
            pl.BlockSpec((FB, D), lambda g: (0, 8 + g)),
            whole((8, D)),
            whole((8, D)),
        ],
        out_specs=[
            whole((ROWS, D)),
            pl.BlockSpec((D, 2 * FB), lambda g: (0, g)),
            pl.BlockSpec((8, FB), lambda g: (0, g)),
            whole((RP, D)),
            whole((RP, D)),
            whole((8, D)),
        ],
        out_shape=[
            like((ROWS, D), f32),
            like((D, 2 * FF), bf16),
            like((8, FF), f32),
            like((RP, D), f32),
            like((RP, D), bf16),
            like((8, D), f32),
        ],
        scratch_shapes=[pltpu.VMEM((RP, FB), bf16)] * 2 + [pltpu.VMEM((RP, D), f32)] * 2,
        compiler_params=params(62),
        cost_estimate=pl.CostEstimate(flops=45 * 10**9, bytes_accessed=30 * MIB, transcendentals=0),
        name="ffn",
    )(n2, dout, x1, weights, b_up, weights, gains, shifts)


def flip(v, axis, bits):
    return lax.ppermute(v, axis, [(i, i ^ bits) for i in range(lax.axis_size(axis))])


def terms(v, axis, step, count):
    return [v] + [flip(v, axis, k * step) for k in range(1, count)]


def tree_sum(parts):
    parts = list(parts)
    while len(parts) > 1:
        parts = [parts[i] + parts[i + 1] for i in range(0, len(parts), 2)]
    return parts[0]


def in_order(parts, place):
    parts = list(parts)
    bit = 1
    while bit < len(parts):
        odd = (place & bit) != 0
        parts = [jnp.where(odd, parts[i ^ bit], parts[i]) for i in range(len(parts))]
        bit *= 2
    return parts


def pick(v, i, axis=0):
    return lax.dynamic_index_in_dim(v, i, axis, keepdims=False)


def sum_low(parts):
    return tree_sum([p.astype(f32) for p in parts])


def scatter_core(v, core):
    got = flip(pick(v, 1 - core, 2), "tok", 1)
    return sum_low([pick(v, core, 2), got]).astype(bf16)


def scatter_band(v, band):
    return sum_low([pick(v, band)] + [flip(pick(v, band ^ r), "band", r) for r in range(1, BANDS)]).astype(bf16)


def scatter_z(v, z):
    return sum_low([pick(v, z)] + [flip(pick(v, z ^ k), "tok", 2 * k) for k in range(1, v.shape[0])])


def sum_tok(v, chips):
    v = v + flip(v, "tok", 1)
    return tree_sum(terms(v, "tok", 2, chips))


def wave_features(wavelengths, wave_index):
    table_size = wavelengths.shape[0]
    picked = (wave_index[..., None] == jnp.arange(table_size, dtype=jnp.int32)).astype(f32)
    wave_values = jnp.sum(picked * wavelengths, axis=-1)
    half_width = WG // 2
    frequency = 1.0 / 10000.0 ** (jnp.arange(half_width, dtype=f32) / half_width)
    angles = 1000.0 * wave_values[..., None] * frequency
    return jnp.concatenate([jnp.sin(angles), jnp.cos(angles)], axis=-1)


def shards(
    pixels, wavelengths, wave_index, band_counts, sensors, chip_lengths, meta_rows,
    w_qkv, w_out, w_up, b_up, w_down, norm_gains, shifts,
    gen_qkv, gen_out, gen_ff1, gen_ff2, gen_gains, gen_shifts, latent_tokens, bias_token,
    fc_kernel, fc_bias, d_out,
):
    band = lax.axis_index("band")
    tok = lax.axis_index("tok")
    toks = lax.axis_size("tok")
    chips = toks // 2
    core = tok % 2
    z = tok // 2
    devices = BANDS * toks
    me = band * toks + tok
    share = D // devices
    ff_share = FF // devices
    pix_share = PIX // toks
    width = SLOTS * PIX

    pix_t = pixels.reshape(BANDS, FRAME, width).transpose(0, 2, 1)
    pix = [pick(pix_t, band)] + [flip(pick(pix_t, band ^ r), "band", r) for r in range(1, BANDS)]

    vectors = jnp.concatenate([norm_gains.T, shifts.T, b_up.reshape(4, share).T], axis=1)
    weights = jnp.concatenate(
        [
            w_qkv,
            w_out,
            w_up.reshape(share, devices, 4, share).transpose(0, 2, 1, 3).reshape(share, FF),
            w_down.reshape(4, share, D).transpose(1, 0, 2).reshape(share, FF),
            jnp.pad(vectors, ((0, 0), (0, WG - vectors.shape[1]))),
        ],
        axis=1,
    )
    weights = lax.all_gather(weights, BT, axis=0, tiled=True)
    rest = weights[:, 12 * D : 12 * D + 10].astype(f32).T
    gains = jnp.pad(rest[:2], ((0, 6), (0, 0)))
    shift_rows = jnp.pad(rest[2:6], ((0, 4), (0, 0)))
    bias_up = rest[6:10].reshape(1, FF)

    features = wave_features(wavelengths, wave_index).reshape(SENSORS * BMAX, WG)
    valid = jnp.arange(BMAX, dtype=jnp.int32)[None, :] < band_counts[:, None]
    seq = jnp.concatenate([features, jnp.zeros((4, WG), f32), jnp.broadcast_to(bias_token, (8, WG))], axis=0)
    sensor_ids = jnp.arange(SENSORS, dtype=jnp.int32)
    row_sensor = jnp.concatenate(
        [jnp.repeat(sensor_ids, BMAX), jnp.full((4,), 8, jnp.int32), sensor_ids, jnp.full((1,), 9, jnp.int32)]
    )
    key_ok = jnp.concatenate([valid.reshape(-1), jnp.zeros((4,), jnp.bool_), jnp.ones((8,), jnp.bool_)])
    allowed = (row_sensor[:, None] == row_sensor[None, :]) & key_ok[None, :]
    gen_bias = jnp.concatenate([jnp.zeros((QX, NLAT), f32), jnp.where(allowed, 0.0, MASKED)], axis=1)
    gen_args = (seq, latent_tokens, gen_bias, gen_qkv, gen_out, gen_ff1, gen_ff2, gen_gains, gen_shifts, fc_bias)
    z2, bias_vec = gen_fwd(*gen_args)
    h_all = (z2[: SENSORS * BMAX] + features).reshape(SENSORS, BMAX, WG)
    valid_f = valid.astype(f32)

    ends = jnp.cumsum(chip_lengths.reshape(BANDS, CAP), axis=-1)
    starts = jnp.arange(CAP, dtype=jnp.int32) * CHIP
    block_segment = jnp.sum((ends[:, None, :] <= starts[None, :, None]).astype(jnp.int32), axis=-1)
    block_sensor = jnp.take_along_axis(sensors.reshape(BANDS, CAP), block_segment, axis=1)
    own_ends = pick(ends, band)
    frame_sensor = [pick(block_sensor, band ^ r) for r in range(BANDS)]
    positions = jnp.arange(FRAME, dtype=jnp.int32)
    patch_segment = jnp.sum((own_ends[None, :] <= positions[:, None]).astype(jnp.int32), axis=-1)
    slot_ids = jnp.arange(CAP, dtype=jnp.int32)
    segment = jnp.concatenate([patch_segment, slot_ids, slot_ids, jnp.full((RP - ROWS,), CAP + 1, jnp.int32)])
    onehot = segment[:, None] == jnp.arange(HD, dtype=jnp.int32)[None, :]
    ka = onehot.astype(bf16)
    qa = jnp.where(onehot, 0.0, -(2.0**30)).astype(bf16)

    h_own = lax.dynamic_slice_in_dim(h_all, band * SLOTS, SLOTS, 1).reshape(OWN, WG)
    valid_own = lax.dynamic_slice_in_dim(valid_f, band * SLOTS, SLOTS, 1).reshape(OWN, 1)
    part = (jnp.dot(h_own, fc_kernel, precision=HIGH) * valid_own).astype(bf16).reshape(OWN, pix_share, 2, HALF)
    mine = pick(part, core, 2)
    got = flip(pick(part, 1 - core, 2), "tok", 1)
    got, *pix = lax.optimization_barrier((got, *pix))
    pair = jnp.where(core == 0, jnp.concatenate([mine, got], axis=1), jnp.concatenate([got, mine], axis=1))
    k_own = jnp.concatenate(in_order(terms(pair, "tok", 2, chips), z), axis=1).reshape(SENSORS, width, HALF)

    ker_own = terms(k_own, "band", 1, BANDS)
    ker_other = [flip(v, "tok", 1) for v in ker_own]
    k_other = ker_other[0]

    extra_rows = jnp.concatenate(
        [
            jnp.broadcast_to(shift_rows[3], (CAP, D)),
            meta_rows.reshape(CAP, D).astype(f32),
            jnp.zeros((RP - ROWS, D), f32),
        ],
        axis=0,
    )
    which = core.reshape(1)
    x0, n1 = embed(frame_sensor[0], which, pix, ker_own, ker_other, bias_vec, extra_rows, gains, shift_rows)
    q, k, v, o, probs, x1, n2 = attn_fwd(n1, weights, x0, qa, ka, gains, shift_rows)
    dout = jnp.pad(d_out.reshape(ROWS, D), ((0, RP - ROWS), (0, 0)))
    out, d_ff, d_bup, dx1, dx1b, small2 = ffn(n2, dout, x1, weights, bias_up, gains, shift_rows)
    d_ff = lax.psum_scatter(d_ff, BT, scatter_dimension=0, tiled=True).astype(f32).reshape(share, 8, D)
    args = (dx1b, weights, q, k, v, o, probs, n1)
    d_wo, d_wq, d_wk, d_wv, de, tail_rows, small1 = attn_bwd(
        0, GROUPS, True, *args, jnp.zeros((RP, D), f32), (x0, dx1, gains)
    )

    de_x = flip(de, "band", 1)
    de_y = flip(de, "band", 2)
    d_proj = jnp.concatenate([d_wq, d_wk, d_wv, d_wo], axis=1).reshape(BANDS, chips, 2, share, 4 * D)
    d_proj = scatter_core(d_proj, core)

    def grads(group, done):
        return pixel_grad(
            jnp.concatenate([frame_sensor[r] for r, _ in group]),
            jnp.stack([band ^ r for r, _ in group]),
            which,
            jnp.concatenate([g.reshape(CAP, CHIP, D) for _, g in group], axis=0),
            k_own,
            k_other,
            pix_t,
            done,
        )

    done = grads(((0, de),), ())
    half = FRAME // 2
    d_proj, de_x, de_y = lax.optimization_barrier((d_proj, de_x, de_y))
    de_xy = jnp.concatenate([flip(de_x[:half], "band", 2), flip(de_y[half:], "band", 1)], axis=0)
    done = grads(((1, de_x), (2, de_y)), done)
    d_proj, de_xy = lax.optimization_barrier((d_proj, de_xy))
    d_proj = scatter_band(d_proj, band)
    done = grads(((3, de_xy),), done)
    d_pix, d_ker = done
    d_ker = (d_ker.reshape(OWN, PIX, D) * valid_own[:, :, None]).astype(bf16)
    d_ker = scatter_core(d_ker.reshape(1, OWN * chips, 2, pix_share, D), core)
    d_ker = d_ker.reshape(OWN, chips, pix_share, D).transpose(1, 0, 2, 3)
    d_cols = scatter_z(d_ker, z).astype(bf16)
    d_proj, d_cols = lax.optimization_barrier((d_proj, d_cols))
    d_proj = scatter_z(d_proj, z)
    d_cols_all = jnp.stack(in_order(terms(d_cols, "band", 1, BANDS), band), axis=0)
    d_cols_all = (
        d_cols_all.reshape(BANDS, SENSORS, SLOTS, pix_share * D)
        .transpose(1, 0, 2, 3)
        .reshape(SENSORS * BMAX, pix_share * D)
        .astype(f32)
    )
    d_fc = xmm(h_all.reshape(SENSORS * BMAX, WG), d_cols_all, ((0,), (0,)))
    dh = sum_tok(xmm(d_cols.reshape(OWN, pix_share * D).astype(f32), fc_kernel, ((1,), (1,))), chips)
    dh = jnp.stack(in_order(terms(dh, "band", 1, BANDS), band)).reshape(BANDS, SENSORS, SLOTS, WG)
    dh = dh.transpose(1, 0, 2, 3).reshape(SENSORS * BMAX, WG)

    block_sums = jnp.sum(de.reshape(CAP, CHIP, D).astype(f32), axis=1)
    which_sensor = (frame_sensor[0][None, :] == sensor_ids[:, None]).astype(f32)
    d_bias = jnp.sum(which_sensor[:, :, None] * block_sums[None], axis=1)
    d_class = jnp.sum(tail_rows[:CAP], axis=0, keepdims=True)
    smalls = jnp.concatenate(
        [d_bup[0].reshape(4, D), small1[0:1], small2[0:1], small1[1:2], small2[1:3], d_class, d_bias], axis=0
    )
    smalls = tree_sum(terms(sum_tok(smalls, chips), "band", 1, BANDS))
    dbias_full = jnp.pad(smalls[10:17], ((0, 1), (0, 0)))
    g = gen_bwd(*gen_args, jnp.pad(dh, ((0, 4), (0, 0))), dbias_full)
    bup_shard = lax.dynamic_slice_in_dim(smalls[0:4], me * share, share, 1).reshape(ff_share)
    gains_shard = lax.dynamic_slice_in_dim(smalls[4:6], me * share, share, 1)
    shifts_shard = lax.dynamic_slice_in_dim(smalls[6:10], me * share, share, 1)
    return (
        out.reshape(1, 1, ROWS, D),
        d_pix.transpose(0, 2, 1).reshape(BANDS, 1, FRAME, width),
        tail_rows[CAP : 2 * CAP].reshape(1, 1, CAP, D),
        d_proj[:, : 3 * D],
        d_proj[:, 3 * D :],
        d_ff[:, 0::2].reshape(share, 4, devices, share).transpose(0, 2, 1, 3).reshape(share, FF),
        bup_shard,
        d_ff[:, 1::2].transpose(1, 0, 2).reshape(ff_share, D),
        gains_shard,
        shifts_shard,
        g[0],
        g[1],
        g[2],
        g[3],
        g[4],
        g[5],
        g[6],
        g[7].reshape(WG),
        d_fc,
        g[8],
    )


def solution(mesh):
    both = ("band", "tok")
    placed = (
        P(None, "tok", None, "band"),
        P(),
        P(),
        P(),
        P(None, "tok", None),
        P(None, "tok", None),
        P("band", "tok", None, None),
        P(both, None),
        P(both, None),
        P(both, None),
        P(both),
        P(both, None),
        P(None, both),
        P(None, both),
        P(),
        P(),
        P(),
        P(),
        P(),
        P(),
        P(),
        P(),
        P(None, "tok"),
        P(),
        P("band", "tok", None, None),
    )
    return jax.shard_map(
        shards,
        mesh=mesh,
        in_specs=placed,
        out_specs=(
            P("band", "tok", None, None),
            P(None, "tok", None, "band"),
            P("band", "tok", None, None),
            P(both, None),
            P(both, None),
            P(both, None),
            P(both),
            P(both, None),
            P(None, both),
            P(None, both),
            P(),
            P(),
            P(),
            P(),
            P(),
            P(),
            P(),
            P(),
            P(None, "tok"),
            P(),
        ),
        check_vma=False,
    )
```

```python
import math

import jax
import jax.numpy as jnp
from jax import lax
from jax.experimental import pallas as pl
from jax.experimental.pallas import tpu as pltpu
from jax.sharding import PartitionSpec as P

D = 768
HEADS = 12
HD = 64
FF = 3072
WG = 128
GHEADS = 4
GHD = 32
GFF = 2048
NLAT = 128
PIX = 64
SENSORS = 7
BMAX = 12
CHIP = 256
CAP = 4
FRAME = 1024
ROWS = 1032
RP = 1040
CH = RP
BACK_ROWS = ((0, 528), (528, 512))
BANDS = 4
SLOTS = BMAX // BANDS
OWN = SENSORS * SLOTS
HALF = D // 2
QX = 96

f32 = jnp.float32
bf16 = jnp.bfloat16
BT = ("band", "tok")
HIGH = lax.Precision.HIGHEST
EPS = 1e-05
MASKED = -1000000000.0
MIB = 2**20
SHORT = pl.CostEstimate(flops=2 * 10**8, bytes_accessed=MIB // 4, transcendentals=0)


def mm(a, b):
    return lax.dot_general(a, b, (((1,), (0,)), ((), ())), preferred_element_type=f32)


def mm_nt(a, b):
    return lax.dot_general(a, b, (((1,), (1,)), ((), ())), preferred_element_type=f32)


def mm_tn(a, b):
    return lax.dot_general(a, b, (((0,), (0,)), ((), ())), preferred_element_type=f32)


def xmm(a, b, dims=((1,), (0,))):
    return lax.dot_general(a, b, (dims, ((), ())), precision=HIGH, preferred_element_type=f32)


def whole(shape):
    return pl.BlockSpec(shape, lambda *_: (0,) * len(shape))


def like(shape, dtype):
    return jax.ShapeDtypeStruct(shape, dtype)


def params(mib):
    return pltpu.CompilerParams(vmem_limit_bytes=mib * MIB)


def center(x):
    xc = x - jnp.mean(x, axis=1, keepdims=True)
    r = lax.rsqrt(jnp.mean(xc * xc, axis=1, keepdims=True) + EPS)
    return xc * r, r


def gelu_parts(u):
    phi = 0.5 + 0.5 * lax.erf(u * math.sqrt(0.5))
    slope = phi + u * (math.sqrt(0.5 / math.pi) * jnp.exp(-0.5 * u * u))
    return u * phi, slope


def col8(v):
    return jnp.sum(v.reshape(v.shape[0] // 8, 8, v.shape[1]), axis=0)


def total(v):
    return jnp.sum(v, axis=0, keepdims=True)


def head_lanes(h):
    lane = lax.broadcasted_iota(jnp.int32, (1, WG), 1)
    return (lane // GHD == h).astype(f32)


def gen_forward(x, latent, bias, w_qkv, w_out, ff1, ff2, gains, shifts):
    scale = 1.0 / math.sqrt(GHD)
    qkv = xmm(x, w_qkv)
    kv = xmm(latent, w_qkv[:, WG:])
    q = qkv[:, :WG] * scale
    k = jnp.concatenate([kv[:, :WG], qkv[:, WG : 2 * WG]], axis=0)
    v = jnp.concatenate([kv[:, WG:], qkv[:, 2 * WG :]], axis=0)
    mixed = jnp.zeros((QX, WG), f32)
    probs = []
    for h in range(GHEADS):
        lanes = head_lanes(h)
        s = xmm(q * lanes, k, ((1,), (1,))) + bias
        e = jnp.exp(s - jnp.max(s, axis=1, keepdims=True))
        p = e / jnp.sum(e, axis=1, keepdims=True)
        probs.append(p)
        mixed = mixed + xmm(p, v * lanes)
    hat1, r1 = center(x + xmm(mixed, w_out))
    z1 = hat1 * gains[0:1] + shifts[0:1]
    act, slope = gelu_parts(xmm(z1, ff1))
    hat2, r2 = center(z1 + xmm(act, ff2))
    z2 = hat2 * gains[1:2] + shifts[1:2]
    return z2, (q, k, v, probs, mixed, hat1, r1, z1, act, slope, hat2, r2)


GEN_KEPT = [(QX, WG)] + [(NLAT + QX, WG)] * 2 + [(GHEADS, QX, NLAT + QX)] + [(QX, WG)] * 4 + [(QX, GFF)] * 2 + [(QX, WG)] * 2


def gen_fwd_kernel(
    x, latent, bias, w_qkv, w_out, ff1, ff2, gains, shifts, fc_bias, chosen, fc_kernel, z2_o, bias_o, part_o, *kept_o
):
    z2, kept = gen_forward(
        x[...], latent[...], bias[...], w_qkv[...], w_out[...], ff1[...], ff2[...], gains[...], shifts[...]
    )
    z2_o[...] = z2
    bias_o[...] = xmm(z2[QX - 8 :], fc_bias[...])
    part_o[...] = xmm(xmm(chosen[...], z2 + x[...]), fc_kernel[...]).astype(bf16)
    for ref, shape, v in zip(kept_o, GEN_KEPT, kept):
        if isinstance(v, list):
            for h in range(GHEADS):
                ref[h] = v[h]
        else:
            ref[...] = jnp.broadcast_to(v, shape)


def gen_fwd(x, latent, bias, w_qkv, w_out, ff1, ff2, gains, shifts, fc_bias, chosen, fc_kernel):
    args = (x, latent, bias, w_qkv, w_out, ff1, ff2, gains, shifts, fc_bias, chosen, fc_kernel)
    part = (chosen.shape[0], fc_kernel.shape[1])
    return pl.pallas_call(
        gen_fwd_kernel,
        in_specs=[whole(a.shape) for a in args],
        out_specs=[whole((QX, WG)), whole((8, D)), whole(part)] + [whole(t) for t in GEN_KEPT],
        out_shape=[like((QX, WG), f32), like((8, D), f32), like(part, bf16)] + [like(t, f32) for t in GEN_KEPT],
        compiler_params=params(62),
        cost_estimate=SHORT,
        name="gen_fwd",
    )(*args)


def norm_back(g, hat, r, gain):
    s = g * gain
    return r * (s - jnp.mean(s, axis=1, keepdims=True) - hat * jnp.mean(s * hat, axis=1, keepdims=True))


def gen_bwd_kernel(
    x, latent, w_qkv, w_out, ff1, ff2, gains, fc_bias, z2, q, k, v, probs, mixed, hat1, r1, z1, act, slope, hat2, r2,
    dh, dbias, dqkv_o, dout_o, dff1_o, dff2_o, dgains_o, dshifts_o, dlat_o, dtok_o, dfcb_o,
):
    scale = 1.0 / math.sqrt(GHD)
    xv, lat, gainv = x[...], latent[...], gains[...]
    z2, q, k, v, mixed, hat1, r1, z1, act, slope, hat2, r2 = (
        ref[...] for ref in (z2, q, k, v, mixed, hat1, r1, z1, act, slope, hat2, r2)
    )
    db = dbias[...]
    dfcb_o[...] = xmm(z2[QX - 8 :], db, ((0,), (0,)))
    dz2 = jnp.concatenate([dh[...], xmm(db, fc_bias[...], ((1,), (1,)))], axis=0)
    dw2 = norm_back(dz2, hat2, r2, gainv[1:2])
    dff2_o[...] = xmm(act, dw2, ((0,), (0,)))
    du = xmm(dw2, ff2[...], ((1,), (1,))) * slope
    dff1_o[...] = xmm(z1, du, ((0,), (0,)))
    dz1 = dw2 + xmm(du, ff1[...], ((1,), (1,)))
    dw1 = norm_back(dz1, hat1, r1, gainv[0:1])
    dgains_o[...] = jnp.concatenate([total(dz1 * hat1), total(dz2 * hat2)], axis=0)
    dshifts_o[...] = jnp.concatenate([total(dz1), total(dz2)], axis=0)
    dout_o[...] = xmm(mixed, dw1, ((0,), (0,)))
    dmix = xmm(dw1, w_out[...], ((1,), (1,)))
    dq = jnp.zeros((QX, WG), f32)
    dk = jnp.zeros((NLAT + QX, WG), f32)
    dv = jnp.zeros((NLAT + QX, WG), f32)
    for h in range(GHEADS):
        lanes = head_lanes(h)
        p = probs[h]
        dm = dmix * lanes
        dp = xmm(dm, v, ((1,), (1,)))
        ds = p * (dp - jnp.sum(p * dp, axis=1, keepdims=True))
        dv = dv + xmm(p, dm, ((0,), (0,)))
        dq = dq + xmm(ds, k * lanes)
        dk = dk + xmm(ds, q * lanes, ((0,), (0,)))
    dq = dq * scale
    dx = jnp.concatenate([dq, dk[NLAT:], dv[NLAT:]], axis=1)
    dl = jnp.concatenate([dk[:NLAT], dv[:NLAT]], axis=1)
    wv = w_qkv[...]
    from_x = xmm(xv, dx, ((0,), (0,)))
    from_l = xmm(lat, dl, ((0,), (0,)))
    dqkv_o[:, :WG] = from_x[:, :WG]
    dqkv_o[:, WG:] = from_x[:, WG:] + from_l
    dlat_o[...] = xmm(dl, wv[:, WG:], ((1,), (1,)))
    dx_full = dw1 + xmm(dx, wv, ((1,), (1,)))
    dtok_o[...] = total(dx_full[QX - 8 : QX - 8 + SENSORS])


def gen_bwd(x, latent, w_qkv, w_out, ff1, ff2, gains, fc_bias, z2, kept, dh, dbias):
    args = (x, latent, w_qkv, w_out, ff1, ff2, gains, fc_bias, z2, *kept, dh, dbias)
    shapes = [(WG, 3 * WG), (WG, WG), (WG, GFF), (GFF, WG), (2, WG), (2, WG), (NLAT, WG), (1, WG), (WG, D)]
    return pl.pallas_call(
        gen_bwd_kernel,
        in_specs=[whole(a.shape) for a in args],
        out_specs=[whole(s) for s in shapes],
        out_shape=[like(s, f32) for s in shapes],
        compiler_params=params(62),
        cost_estimate=SHORT,
        name="gen_bwd",
    )(*args)


def embed_kernel(sens, core, *refs):
    n = len(refs) // 3 - 2
    pix, own, other = refs[:n], refs[n : 2 * n], refs[2 * n : 3 * n]
    bias, extra, gains, shifts, x0_o, n1_o = refs[3 * n :]
    c = pl.program_id(0)
    rows = pl.ds(c * CHIP, CHIP)
    row = bias[pl.ds(sens[c], 1), :]
    for half, ker in ((core[0], own), (1 - core[0], other)):
        acc = mm_tn(pix[0][...], ker[0][0])
        for r in range(1, n):
            acc = acc + mm_tn(pix[r][...], ker[r][0])
        x0_o[rows, pl.ds(pl.multiple_of(half * HALF, HALF), HALF)] = acc
    x = x0_o[rows, :] + row
    x0_o[rows, :] = x
    hat, _ = center(x)
    n1_o[rows, :] = (hat * gains[0:1] + shifts[0:1]).astype(bf16)

    @pl.when(c == CAP - 1)
    def _():
        e = extra[...]
        x0_o[FRAME:, :] = e
        h, _ = center(e)
        n1_o[FRAME:, :] = (h * gains[0:1] + shifts[0:1]).astype(bf16)


def embed(sens, core, pix, own, other, bias, extra, gains, shifts):
    heights = [v.shape[1] for v in own]
    kernels = [pl.BlockSpec((1, n, HALF), lambda c, s, _: (s[c], 0, 0)) for n in heights]
    return pl.pallas_call(
        embed_kernel,
        grid_spec=pltpu.PrefetchScalarGridSpec(
            num_scalar_prefetch=2,
            grid=(CAP,),
            in_specs=[pl.BlockSpec((n, CHIP), lambda c, *_, at=at: (at, c)) for n, (_, at) in zip(heights, pix)]
            + kernels
            + kernels
            + [whole((8, D)), whole((RP - FRAME, D)), whole((8, D)), whole((8, D))],
            out_specs=[whole((RP, D)), whole((RP, D))],
        ),
        out_shape=[like((RP, D), f32), like((RP, D), bf16)],
        compiler_params=params(62),
        cost_estimate=pl.CostEstimate(flops=2 * FRAME * D * D, bytes_accessed=14 * MIB, transcendentals=0),
        name="embed",
    )(sens, core, *[v for v, _ in pix], *own, *other, bias, extra, gains, shifts)


def frame_kernel_grad_kernel(de, *refs):
    g = de[0]
    for pix, out in zip(refs[:BANDS], refs[BANDS:]):
        out[0] = mm(pix[...], g).astype(bf16)


def frame_kernel_grad(de, pix):
    width = SLOTS * PIX
    return pl.pallas_call(
        frame_kernel_grad_kernel,
        grid=(CAP,),
        in_specs=[pl.BlockSpec((1, CHIP, D), lambda c: (c, 0, 0))]
        + [pl.BlockSpec((width, CHIP), lambda c: (0, c))] * BANDS,
        out_specs=[pl.BlockSpec((1, width, D), lambda c: (c, 0, 0))] * BANDS,
        out_shape=[like((CAP, width, D), bf16)] * BANDS,
        compiler_params=params(62),
        cost_estimate=SHORT,
        name="frame_kernel_grad",
    )(de, *pix)


def frame_pixel_grad_kernel(sens, core, de, *refs):
    n = (len(refs) - BANDS) // 2
    own, other, outs = refs[:n], refs[n : 2 * n], refs[2 * n :]
    lo = de[0, :, pl.ds(pl.multiple_of(core[0] * HALF, HALF), HALF)]
    hi = de[0, :, pl.ds(pl.multiple_of((1 - core[0]) * HALF, HALF), HALF)]
    out, at = 0, 0
    for a, b in zip(own, other):
        rows = a.shape[1]
        outs[out][at : at + rows, :] = (mm_nt(a[0], lo) + mm_nt(b[0], hi)).astype(bf16)
        at += rows
        if at == outs[out].shape[0]:
            out, at = out + 1, 0


def frame_pixel_grad(sens, core, de, own, other):
    width = SLOTS * PIX
    kernels = [pl.BlockSpec((1, v.shape[1], HALF), lambda c, s, _: (s[c], 0, 0)) for v in own]
    return pl.pallas_call(
        frame_pixel_grad_kernel,
        grid_spec=pltpu.PrefetchScalarGridSpec(
            num_scalar_prefetch=2,
            grid=(CAP,),
            in_specs=[pl.BlockSpec((1, CHIP, D), lambda c, *_: (c, 0, 0))] + kernels + kernels,
            out_specs=[pl.BlockSpec((width, CHIP), lambda c, *_: (0, c))] * BANDS,
        ),
        out_shape=[like((width, FRAME), bf16)] * BANDS,
        compiler_params=params(62),
        cost_estimate=SHORT,
        name="frame_pixel_grad",
    )(sens, core, de, *own, *other)


def by_sensor_kernel(sens, valid, *refs):
    parts, out, acc = refs[:BANDS], refs[BANDS], refs[BANDS + 1]
    acc[...] = jnp.zeros_like(acc)
    for r in range(BANDS):
        for c in range(CAP):
            s = sens[r * CAP + c]
            acc[s] = acc[s] + parts[r][c].astype(f32)
    for s in range(SENSORS):
        for j in range(SLOTS):
            rows = slice(j * PIX, (j + 1) * PIX)
            keep = (valid[s * SLOTS + j] != 0).astype(f32)
            out[s, rows, :] = (acc[s, rows, :] * keep).astype(bf16)


def by_sensor(sens, valid, parts):
    width = SLOTS * PIX
    return pl.pallas_call(
        by_sensor_kernel,
        grid_spec=pltpu.PrefetchScalarGridSpec(
            num_scalar_prefetch=2,
            grid=(1,),
            in_specs=[whole((CAP, width, D))] * BANDS,
            out_specs=whole((SENSORS, width, D)),
            scratch_shapes=[pltpu.VMEM((SENSORS, width, D), f32)],
        ),
        out_shape=like((SENSORS, width, D), bf16),
        compiler_params=params(62),
        cost_estimate=SHORT,
        name="by_sensor",
    )(sens, valid, *parts)


def small_sums_kernel(sens, d_bup, small1, small2, tail, de, out, acc):
    acc[...] = jnp.zeros_like(acc)
    for c in range(CAP):
        row = pl.ds(sens[c], 1)
        acc[row, :] = acc[row, :] + total(col8(de[c].astype(f32)))
    for a in range(4):
        out[a : a + 1, :] = d_bup[0:1, a * D : (a + 1) * D]
    out[4:5, :] = small1[0:1, :]
    out[5:6, :] = small2[0:1, :]
    out[6:7, :] = small1[1:2, :]
    out[7:9, :] = small2[1:3, :]
    out[9:10, :] = total(tail[0:CAP, :])
    out[10:17, :] = acc[0:SENSORS, :]
    out[17:24, :] = jnp.zeros((7, D), f32)


def small_sums(sens, d_bup, small1, small2, tail, de):
    args = (d_bup, small1, small2, tail, de)
    return pl.pallas_call(
        small_sums_kernel,
        grid_spec=pltpu.PrefetchScalarGridSpec(
            num_scalar_prefetch=1,
            grid=(1,),
            in_specs=[whole(a.shape) for a in args],
            out_specs=whole((24, D)),
            scratch_shapes=[pltpu.VMEM((8, D), f32)],
        ),
        out_shape=like((24, D), f32),
        compiler_params=params(62),
        cost_estimate=SHORT,
        name="small_sums",
    )(sens, *args)


def columns_kernel(fc_kernel, smalls, *refs):
    *parts, cols_o, both_o = refs
    cols = tree_sum([p[...].astype(f32) for p in parts]).astype(bf16)
    cols_o[...] = cols
    cols = cols.astype(f32)
    dh = jnp.zeros((OWN, WG), f32)
    for i in range(cols.shape[1]):
        dh = dh + xmm(cols[:, i, :], fc_kernel[:, i * D : (i + 1) * D], ((1,), (1,)))
    both_o[:, :D] = smalls[...]
    both_o[:, D:] = jnp.concatenate([dh, jnp.zeros((24 - OWN, WG), f32)], axis=0)


def columns(fc_kernel, smalls, parts):
    shape = parts[0].shape
    return pl.pallas_call(
        columns_kernel,
        in_specs=[whole(fc_kernel.shape), whole((24, D))] + [whole(shape)] * len(parts),
        out_specs=[whole(shape), whole((24, D + WG))],
        out_shape=[like(shape, bf16), like((24, D + WG), f32)],
        compiler_params=params(62),
        cost_estimate=SHORT,
        name="columns",
    )(fc_kernel, smalls, *parts)


GH = 4
GW = GH * HD
GROUPS = HEADS // GH


def attn_fwd_kernel(n1, wq, wk, wv, wo, x0, qa, ka, gains, shifts, q_o, k_o, v_o, o_o, p_o, x1_o, n2_o):
    g = pl.program_id(0)

    @pl.when(g == 0)
    def _():
        x1_o[...] = x0[...]

    for c in range(RP // CH):
        s = pl.ds(c * CH, CH)
        q_o[s, :] = mm(n1[s, :], wq[...]).astype(bf16)
        k_o[s, :] = mm(n1[s, :], wk[...]).astype(bf16)
        v_o[s, :] = mm(n1[s, :], wv[...]).astype(bf16)
    qav = qa[...]
    kav = ka[...]
    for h in range(GH):
        hs = slice(h * HD, (h + 1) * HD)
        kh = jnp.concatenate([k_o[:, hs], kav], axis=1)
        vh = v_o[:, hs]
        for c in range(RP // CH):
            s = pl.ds(c * CH, CH)
            qh = jnp.concatenate([q_o[s, hs] * jnp.bfloat16(0.125), qav[c * CH : (c + 1) * CH]], axis=1)
            sc = mm_nt(qh, kh)
            e = jnp.exp(sc - jnp.max(sc, axis=1, keepdims=True))
            p = (e * (1.0 / jnp.sum(e, axis=1, keepdims=True))).astype(bf16)
            p_o[h, s, :] = p
            o_o[s, hs] = mm(p, vh).astype(bf16)
    for c in range(RP // CH):
        s = pl.ds(c * CH, CH)
        x1_o[s, :] += mm(o_o[s, :], wo[...])

    @pl.when(g == pl.num_programs(0) - 1)
    def _():
        for c in range(RP // CH):
            s = pl.ds(c * CH, CH)
            hat, _ = center(x1_o[s, :])
            n2_o[s, :] = (hat * gains[1:2, :] + shifts[1:2, :]).astype(bf16)


def attn_fwd(n1, weights, late, x0, qa, ka, gains, shifts):
    return pl.pallas_call(
        attn_fwd_kernel,
        grid=(GROUPS,),
        in_specs=[
            whole((RP, D)),
            pl.BlockSpec((D, GW), lambda g: (0, g)),
            pl.BlockSpec((D, GW), lambda g: (0, GROUPS + g)),
            pl.BlockSpec((D, GW), lambda g: (0, 2 * GROUPS + g)),
            pl.BlockSpec((GW, D), lambda g: (g, 8)),
            whole((RP, D)),
            whole((RP, HD)),
            whole((RP, HD)),
            whole((8, D)),
            whole((8, D)),
        ],
        out_specs=[pl.BlockSpec((RP, GW), lambda g: (0, g))] * 4
        + [pl.BlockSpec((GH, RP, RP), lambda g: (g, 0, 0)), whole((RP, D)), whole((RP, D))],
        out_shape=[like((RP, D), bf16)] * 4
        + [like((HEADS, RP, RP), bf16), like((RP, D), f32), like((RP, D), bf16)],
        compiler_params=params(60),
        cost_estimate=pl.CostEstimate(flops=5 * 10**10, bytes_accessed=50 * MIB, transcendentals=0),
        name="attn_fwd",
    )(n1, weights, weights, weights, late, x0, qa, ka, gains, shifts)


def attn_bwd_kernel(
    dx1b, wo, q, k, v, o, p, wq, wk, wv, x0, dx1, gains,
    dq_o, dk_o, dv_o, de_o, tail_o, small_o, dn1_s, do_s, ds_s,
):
    g = pl.program_id(0)

    @pl.when(g == 0)
    def _():
        dn1_s[...] = jnp.zeros_like(dn1_s)

    for c0, cn in BACK_ROWS:
        s = pl.ds(c0, cn)
        do_s[s, :] = mm_nt(dx1b[s, :], wo[...]).astype(bf16)
    for h in range(GH):
        hs = slice(h * HD, (h + 1) * HD)
        vh = v[:, hs]
        kh = k[:, hs]
        qh = q[:, hs]
        doh = do_s[:, hs]
        for c0, cn in BACK_ROWS:
            s = pl.ds(c0, cn)
            dc = do_s[s, hs]
            inner = jnp.sum(dc.astype(f32) * o[s, hs].astype(f32), axis=1, keepdims=True)
            ds = (p[h, s, :].astype(f32) * (mm_nt(dc, vh) - inner)).astype(bf16)
            ds_s[s, :] = ds
            dq_o[s, hs] = (mm(ds, kh) * 0.125).astype(bf16)
        dk_o[:, hs] = (mm(qh.T, ds_s[...]) * 0.125).T.astype(bf16)
        dv_o[:, hs] = mm(doh.T, p[h]).T.astype(bf16)
    for c0, cn in BACK_ROWS:
        s = pl.ds(c0, cn)
        dn1_s[s, :] += mm_nt(dq_o[s, :], wq[...]) + mm_nt(dk_o[s, :], wk[...]) + mm_nt(dv_o[s, :], wv[...])

    @pl.when(g == pl.num_programs(0) - 1)
    def _():
        gg = jnp.zeros((8, D), f32)
        gs = jnp.zeros((8, D), f32)
        for c0, cn in BACK_ROWS:
            s = pl.ds(c0, cn)
            hat, r = center(x0[s, :])
            gr = dn1_s[s, :]
            gg = gg + col8(gr * hat)
            gs = gs + col8(gr)
            dn1_s[s, :] = dx1[s, :] + norm_back(gr, hat, r, gains[0:1, :])
        de_o[...] = dn1_s[:FRAME, :].astype(bf16)
        tail_o[...] = dn1_s[FRAME:, :]
        small_o[0:1, :] = total(gg)
        small_o[1:2, :] = total(gs)
        small_o[2:8, :] = jnp.zeros((6, D), f32)


def attn_bwd(dx1b, weights, late, q, k, v, o, p, x0, dx1, gains):
    col = pl.BlockSpec((RP, GW), lambda g: (0, g))
    return pl.pallas_call(
        attn_bwd_kernel,
        grid=(GROUPS,),
        in_specs=[
            whole((RP, D)),
            pl.BlockSpec((GW, D), lambda g: (g, 8)),
            col,
            col,
            col,
            col,
            pl.BlockSpec((GH, RP, RP), lambda g: (g, 0, 0)),
            pl.BlockSpec((D, GW), lambda g: (0, g)),
            pl.BlockSpec((D, GW), lambda g: (0, GROUPS + g)),
            pl.BlockSpec((D, GW), lambda g: (0, 2 * GROUPS + g)),
            whole((RP, D)),
            whole((RP, D)),
            whole((8, D)),
        ],
        out_specs=[col, col, col, whole((FRAME, D)), whole((RP - FRAME, D)), whole((8, D))],
        out_shape=[like((RP, D), bf16)] * 3 + [like((FRAME, D), bf16), like((RP - FRAME, D), f32), like((8, D), f32)],
        scratch_shapes=[pltpu.VMEM((RP, D), f32), pltpu.VMEM((RP, GW), bf16), pltpu.VMEM((RP, RP), bf16)],
        compiler_params=params(62),
        cost_estimate=pl.CostEstimate(flops=5 * 10**10, bytes_accessed=50 * MIB, transcendentals=0),
        name="attn_bwd",
    )(dx1b, late, q, k, v, o, p, weights, weights, weights, x0, dx1, gains)


def proj_grad_kernel(share, core, n1, dq, dk, dv, o, dx1b, own_qkv, own_out, oth_qkv, oth_out):
    def split(v, own, other, columns):
        if share % 8:
            own[:, columns] = v[: v.shape[0] // 2].astype(bf16)
            other[:, columns] = v[v.shape[0] // 2 :].astype(bf16)
            return
        pieces = [v[i * share : (i + 1) * share] for i in range(v.shape[0] // share)]
        first = jnp.concatenate(pieces[0::2], axis=0).astype(bf16)
        second = jnp.concatenate(pieces[1::2], axis=0).astype(bf16)

        @pl.when(core[0] == 0)
        def _():
            own[:, columns] = first
            other[:, columns] = second

        @pl.when(core[0] != 0)
        def _():
            own[:, columns] = second
            other[:, columns] = first

    for i, part in enumerate((dq, dk, dv)):
        split(mm_tn(n1[...], part[...]), own_qkv, oth_qkv, slice(i * GW, (i + 1) * GW))
    split(mm_tn(o[...], dx1b[...]), own_out, oth_out, slice(0, GW))


def proj_grad(share, core, n1, dq, dk, dv, o, dx1b):
    col = pl.BlockSpec((RP, GW), lambda g, c: (0, g))
    qkv = pl.BlockSpec((D // 2, 3 * GW), lambda g, c: (0, g))
    out = pl.BlockSpec((D // 2, GW), lambda g, c: (0, g))
    return pl.pallas_call(
        lambda *refs: proj_grad_kernel(share, *refs),
        grid_spec=pltpu.PrefetchScalarGridSpec(
            num_scalar_prefetch=1,
            grid=(GROUPS,),
            in_specs=[whole((RP, D)), col, col, col, whole((RP, D)), col],
            out_specs=[qkv, out, qkv, out],
        ),
        out_shape=[like((D // 2, 3 * D), bf16), like((D // 2, D), bf16)] * 2,
        compiler_params=params(62),
        cost_estimate=SHORT,
        name="proj_grad",
    )(core, n1, dq, dk, dv, o, dx1b)


FB = 768


def ffn_kernel(
    share, n2, dout, x1, wup, bup, wdown, gains, shifts,
    out, dw, dbup, dx1_o, dx1b_o, small_o, act_s, du_s, dn2_s, out_s, wd_s, dup_s, ddown_s, sems,
):
    j = pl.program_id(0)
    steps = pl.num_programs(0)
    rows = FB // 4
    shards_here = rows // share

    @pl.when(j == 0)
    def _():
        out_s[...] = x1[...] + shifts[2:3, :]
        dn2_s[...] = jnp.zeros_like(dn2_s)

    wd = wdown[...].astype(f32)
    wd_s[...] = jnp.concatenate(
        [wd[i * share : (i + 1) * share, a * D : (a + 1) * D] for i in range(shards_here) for a in range(4)], axis=0
    ).astype(bf16)
    cs = jnp.zeros((8, FB), f32)
    for c in range(RP // CH):
        s = pl.ds(c * CH, CH)
        u = mm(n2[s, :], wup[...]) + bup[...]
        da = mm_nt(dout[s, :], wd_s[...]).astype(bf16).astype(f32)
        act, slope = gelu_parts(u)
        act = act.astype(bf16)
        act_s[s, :] = act
        du = (da * slope).astype(bf16)
        du_s[s, :] = du
        cs = cs + col8(du.astype(f32))
        out_s[s, :] += mm(act, wd_s[...])
        dn2_s[s, :] += mm_nt(du, wup[...])
    dbup[...] = jnp.broadcast_to(total(cs), (8, FB))

    def copies(step):
        slot = lax.rem(step, 2)
        up = pltpu.make_async_copy(
            dup_s.at[slot], dw.at[:, pl.ds(pl.multiple_of(step * FB, FB), FB)], sems.at[0, slot]
        )
        down = pltpu.make_async_copy(
            ddown_s.at[slot], dw.at[pl.ds(pl.multiple_of(step * rows, rows), rows), pl.ds(FF, FF)], sems.at[1, slot]
        )
        return up, down

    @pl.when(j >= 2)
    def _():
        for copy in copies(j - 2):
            copy.wait()

    slot = lax.rem(j, 2)
    dup_s[slot] = mm_tn(n2[...], du_s[...]).astype(bf16)
    dd = mm_tn(act_s[...], dout[...])
    for a in range(4):
        ddown_s[slot, :, a * D : (a + 1) * D] = jnp.concatenate(
            [dd[(4 * i + a) * share : (4 * i + a + 1) * share] for i in range(shards_here)], axis=0
        ).astype(bf16)
    for copy in copies(j):
        copy.start()

    @pl.when(j == steps - 1)
    def _():
        out[...] = out_s[:ROWS, :]
        gg = jnp.zeros((8, D), f32)
        gs = jnp.zeros((8, D), f32)
        gd = jnp.zeros((8, D), f32)
        for c in range(RP // CH):
            s = pl.ds(c * CH, CH)
            hat, r = center(x1[s, :])
            g = dn2_s[s, :]
            do = dout[s, :].astype(f32)
            gg = gg + col8(g * hat)
            gs = gs + col8(g)
            gd = gd + col8(do)
            dx1 = do + norm_back(g, hat, r, gains[1:2, :])
            dx1_o[s, :] = dx1
            dx1b_o[s, :] = dx1.astype(bf16)
        small_o[0:1, :] = total(gg)
        small_o[1:2, :] = total(gs)
        small_o[2:3, :] = total(gd)
        small_o[3:8, :] = jnp.zeros((5, D), f32)
        for step in (steps - 2, steps - 1):
            for copy in copies(step):
                copy.wait()


def ffn(share, n2, dout, x1, weights, b_up, gains, shifts):
    return pl.pallas_call(
        lambda *refs: ffn_kernel(share, *refs),
        grid=(FF // FB,),
        in_specs=[
            whole((RP, D)),
            whole((RP, D)),
            whole((RP, D)),
            pl.BlockSpec((D, FB), lambda g: (0, 4 + g)),
            pl.BlockSpec((1, FB), lambda g: (0, g)),
            pl.BlockSpec((FB // 4, FF), lambda g: (g, 0)),
            whole((8, D)),
            whole((8, D)),
        ],
        out_specs=[
            whole((ROWS, D)),
            pl.BlockSpec(memory_space=pl.ANY),
            pl.BlockSpec((8, FB), lambda g: (0, g)),
            whole((RP, D)),
            whole((RP, D)),
            whole((8, D)),
        ],
        out_shape=[
            like((ROWS, D), f32),
            like((D, 2 * FF), bf16),
            like((8, FF), f32),
            like((RP, D), f32),
            like((RP, D), bf16),
            like((8, D), f32),
        ],
        scratch_shapes=[pltpu.VMEM((RP, FB), bf16)] * 2
        + [pltpu.VMEM((RP, D), f32)] * 2
        + [
            pltpu.VMEM((FB, D), bf16),
            pltpu.VMEM((2, D, FB), bf16),
            pltpu.VMEM((2, FB // 4, FF), bf16),
            pltpu.SemaphoreType.DMA((2, 2)),
        ],
        compiler_params=params(62),
        cost_estimate=pl.CostEstimate(flops=45 * 10**9, bytes_accessed=30 * MIB, transcendentals=0),
        name="ffn",
    )(n2, dout, x1, weights, b_up, weights, gains, shifts)


def flip(v, axis, bits):
    return lax.ppermute(v, axis, [(i, i ^ bits) for i in range(lax.axis_size(axis))])


def terms(v, axis, step, count):
    return [v] + [flip(v, axis, k * step) for k in range(1, count)]


def tree_sum(parts):
    parts = list(parts)
    while len(parts) > 1:
        parts = [parts[i] + parts[i + 1] for i in range(0, len(parts), 2)]
    return parts[0]


def in_order(parts, place):
    parts = list(parts)
    bit = 1
    while bit < len(parts):
        odd = (place & bit) != 0
        parts = [jnp.where(odd, parts[i ^ bit], parts[i]) for i in range(len(parts))]
        bit *= 2
    return parts


def pick(v, i, axis=0):
    return lax.dynamic_index_in_dim(v, i, axis, keepdims=False)


def sum_low(parts):
    return tree_sum([p.astype(f32) for p in parts])


def scatter_core(v, core):
    got = flip(pick(v, 1 - core, 2), "tok", 1)
    return sum_low([pick(v, core, 2), got]).astype(bf16)


def scatter_band(v, band):
    return sum_low([pick(v, band)] + [flip(pick(v, band ^ r), "band", r) for r in range(1, BANDS)]).astype(bf16)


def scatter_z(v, z):
    return sum_low([pick(v, z)] + [flip(pick(v, z ^ k), "tok", 2 * k) for k in range(1, v.shape[0])])


def sum_tok(v, chips):
    v = v + flip(v, "tok", 1)
    return tree_sum(terms(v, "tok", 2, chips))


def wave_features(wavelengths, wave_index):
    table_size = wavelengths.shape[0]
    picked = (wave_index[..., None] == jnp.arange(table_size, dtype=jnp.int32)).astype(f32)
    wave_values = jnp.sum(picked * wavelengths, axis=-1)
    half_width = WG // 2
    frequency = 1.0 / 10000.0 ** (jnp.arange(half_width, dtype=f32) / half_width)
    angles = 1000.0 * wave_values[..., None] * frequency
    return jnp.concatenate([jnp.sin(angles), jnp.cos(angles)], axis=-1)


def shards(
    pixels, wavelengths, wave_index, band_counts, sensors, chip_lengths, meta_rows,
    w_qkv, w_out, w_up, b_up, w_down, norm_gains, shifts,
    gen_qkv, gen_out, gen_ff1, gen_ff2, gen_gains, gen_shifts, latent_tokens, bias_token,
    fc_kernel, fc_bias, d_out,
):
    band = lax.axis_index("band")
    tok = lax.axis_index("tok")
    toks = lax.axis_size("tok")
    chips = toks // 2
    core = tok % 2
    z = tok // 2
    devices = BANDS * toks
    me = band * toks + tok
    share = D // devices
    ff_share = FF // devices
    pix_share = PIX // toks
    width = SLOTS * PIX

    pix_t = pixels.reshape(BANDS, FRAME, width).transpose(0, 2, 1)
    pix = [pick(pix_t, band)] + [flip(pick(pix_t, band ^ r), "band", r) for r in range(1, BANDS)]

    late = jnp.concatenate([w_down.reshape(4, share, D).transpose(1, 0, 2).reshape(share, FF), w_up, w_out], axis=1)
    late = lax.all_gather(late, BT, axis=0, tiled=True)

    vectors = jnp.concatenate([norm_gains.T, shifts.T, b_up.reshape(share, 4)], axis=1)
    vectors = jnp.pad(vectors, ((0, 0), (0, WG - vectors.shape[1])))
    bundle = terms(jnp.concatenate([w_qkv, vectors], axis=1), "tok", 2, chips)

    features = wave_features(wavelengths, wave_index).reshape(SENSORS * BMAX, WG)
    valid = jnp.arange(BMAX, dtype=jnp.int32)[None, :] < band_counts[:, None]
    seq = jnp.concatenate([features, jnp.zeros((4, WG), f32), jnp.broadcast_to(bias_token, (8, WG))], axis=0)
    sensor_ids = jnp.arange(SENSORS, dtype=jnp.int32)
    row_sensor = jnp.concatenate(
        [jnp.repeat(sensor_ids, BMAX), jnp.full((4,), 8, jnp.int32), sensor_ids, jnp.full((1,), 9, jnp.int32)]
    )
    key_ok = jnp.concatenate([valid.reshape(-1), jnp.zeros((4,), jnp.bool_), jnp.ones((8,), jnp.bool_)])
    allowed = (row_sensor[:, None] == row_sensor[None, :]) & key_ok[None, :]
    gen_bias = jnp.concatenate([jnp.zeros((QX, NLAT), f32), jnp.where(allowed, 0.0, MASKED)], axis=1)
    gen_args = (seq, latent_tokens, gen_bias, gen_qkv, gen_out, gen_ff1, gen_ff2, gen_gains, gen_shifts, fc_bias)
    own_row = sensor_ids[:, None] * BMAX + band * SLOTS + jnp.arange(SLOTS, dtype=jnp.int32)[None, :]
    own_valid = lax.dynamic_slice_in_dim(valid, band * SLOTS, SLOTS, 1).reshape(OWN)
    chosen = (own_row.reshape(OWN, 1) == jnp.arange(QX, dtype=jnp.int32)[None, :]) & own_valid[:, None]
    chosen = jnp.pad(chosen.astype(f32), ((0, 3), (0, 0)))
    z2, bias_vec, part, *kept = gen_fwd(*gen_args, chosen, fc_kernel)
    z2, part, pix, bundle = lax.optimization_barrier((z2, part, pix, bundle))
    h_all = (z2[: SENSORS * BMAX] + features).reshape(SENSORS, BMAX, WG)

    ends = jnp.cumsum(chip_lengths.reshape(BANDS, CAP), axis=-1)
    starts = jnp.arange(CAP, dtype=jnp.int32) * CHIP
    block_segment = jnp.sum((ends[:, None, :] <= starts[None, :, None]).astype(jnp.int32), axis=-1)
    block_sensor = jnp.take_along_axis(sensors.reshape(BANDS, CAP), block_segment, axis=1)
    own_ends = pick(ends, band)
    frame_sensor = [pick(block_sensor, band ^ r) for r in range(BANDS)]
    positions = jnp.arange(FRAME, dtype=jnp.int32)
    patch_segment = jnp.sum((own_ends[None, :] <= positions[:, None]).astype(jnp.int32), axis=-1)
    slot_ids = jnp.arange(CAP, dtype=jnp.int32)
    segment = jnp.concatenate([patch_segment, slot_ids, slot_ids, jnp.full((RP - ROWS,), CAP + 1, jnp.int32)])
    onehot = segment[:, None] == jnp.arange(HD, dtype=jnp.int32)[None, :]
    ka = onehot.astype(bf16)
    qa = jnp.where(onehot, 0.0, -(2.0**30)).astype(bf16)

    part = part[:OWN].reshape(OWN, pix_share, 2, HALF)
    mine = pick(part, core, 2)
    got = flip(pick(part, 1 - core, 2), "tok", 1)
    pair = jnp.where(core == 0, jnp.concatenate([mine, got], axis=1), jnp.concatenate([got, mine], axis=1))
    bundle = terms(jnp.stack(in_order(bundle, z)), "band", 1, BANDS)
    pairs = terms(pair, "tok", 2, chips)
    pairs, bundle = lax.optimization_barrier((pairs, bundle))
    k_own = jnp.concatenate(in_order(pairs, z), axis=1).reshape(SENSORS, width, HALF)
    k_x = flip(k_own, "band", 1)
    k_y = flip(k_own, "band", 2)
    bundle = jnp.stack(in_order(bundle, band))
    bundle_other = flip(bundle, "tok", 1)
    half = width // 2
    k_x, k_y, bundle_other = lax.optimization_barrier((k_x, k_y, bundle_other))
    ker_own = [k_own, k_x, k_y, flip(k_x[:, :half], "band", 2), flip(k_y[:, half:], "band", 1)]
    ker_other = [flip(v, "tok", 1) for v in ker_own]
    weights = jnp.where(
        core == 0, jnp.stack([bundle, bundle_other], axis=2), jnp.stack([bundle_other, bundle], axis=2)
    ).reshape(D, 3 * D + WG)
    rest = weights[:, 3 * D : 3 * D + 10].astype(f32)
    bias_up = rest[:, 6:10].reshape(1, FF)
    rest = rest.T
    gains = jnp.pad(rest[:2], ((0, 6), (0, 0)))
    shift_rows = jnp.pad(rest[2:6], ((0, 4), (0, 0)))

    extra_rows = jnp.concatenate(
        [
            jnp.broadcast_to(shift_rows[3], (CAP, D)),
            meta_rows.reshape(CAP, D).astype(f32),
            jnp.zeros((RP - ROWS, D), f32),
        ],
        axis=0,
    )
    which = core.reshape(1)
    parts = [(pix[0], 0), (pix[1], 0), (pix[2], 0), (pix[3], 0), (pix[3], 1)]
    x0, n1 = embed(frame_sensor[0], which, parts, ker_own, ker_other, bias_vec, extra_rows, gains, shift_rows)
    q, k, v, o, probs, x1, n2 = attn_fwd(n1, weights, late, x0, qa, ka, gains, shift_rows)
    dout = jnp.pad(d_out.reshape(ROWS, D), ((0, RP - ROWS), (0, 0)))
    out, d_ff, d_bup, dx1, dx1b, small2 = ffn(share, n2, dout, x1, late, bias_up, gains, shift_rows)
    d_ff = lax.psum_scatter(d_ff, BT, scatter_dimension=0, tiled=True).astype(f32)
    dq, dk, dv, de, tail_rows, small1 = attn_bwd(dx1b, weights, late, q, k, v, o, probs, x0, dx1, gains)

    de_blocks = de.reshape(CAP, CHIP, D)
    ker_grads = frame_kernel_grad(de_blocks, pix)
    ker_grads, n1, o, tail_rows = lax.optimization_barrier((ker_grads, n1, o, tail_rows))
    ker_grads = [ker_grads[0]] + [flip(ker_grads[r], "band", r) for r in range(1, BANDS)]
    proj = proj_grad(share, which, n1, dq, dk, dv, o, dx1b)
    if share % 8:
        proj = [jnp.concatenate([a, b]).reshape(-1, 2, share, a.shape[1]) for a, b in zip(proj[:2], proj[2:])]
        proj = [pick(v, core, 1) for v in proj] + [pick(v, 1 - core, 1) for v in proj]
    proj = [v.reshape(BANDS, chips, share, -1) for v in proj]
    pix_grads = frame_pixel_grad(frame_sensor[0], which, de_blocks, ker_own, ker_other)
    smalls = small_sums(frame_sensor[0], d_bup, small1, small2, tail_rows, de_blocks)

    ker_grads, pix_grads, proj, smalls = lax.optimization_barrier((ker_grads, pix_grads, proj, smalls))
    d_ker = by_sensor(jnp.concatenate(frame_sensor), own_valid.astype(jnp.int32), ker_grads)
    d_ker = scatter_core(d_ker.reshape(1, OWN * chips, 2, pix_share, D), core)
    d_qkv, d_wo = (sum_low([own, flip(other, "tok", 1)]).astype(bf16) for own, other in zip(proj[:2], proj[2:]))
    d_ker, d_qkv, d_wo = lax.optimization_barrier((d_ker, d_qkv, d_wo))
    d_ker = d_ker.reshape(OWN, chips, pix_share, D)
    d_ker = [pick(d_ker, z, 1)] + [flip(pick(d_ker, z ^ c, 1), "tok", 2 * c) for c in range(1, chips)]
    d_proj = scatter_band(jnp.concatenate([d_qkv, d_wo], axis=-1), band)
    d_ker, d_proj = lax.optimization_barrier((d_ker, d_proj))
    d_cols, both = columns(fc_kernel, smalls, d_ker)
    d_proj = scatter_z(d_proj, z)
    d_wqkv = d_proj[:, : 3 * D].reshape(share, GROUPS, 3, GW).transpose(0, 2, 1, 3).reshape(share, 3 * D)
    d_pix = in_order([pix_grads[0]] + [flip(pix_grads[r], "band", r) for r in range(1, BANDS)], band)
    d_pix = jnp.stack(d_pix).astype(f32)
    d_ff_up = d_ff[:, :FF]
    d_ff_down = d_ff[:, FF:].reshape(share, 4, D).transpose(1, 0, 2).reshape(ff_share, D)
    d_cols_all = jnp.stack(in_order(terms(d_cols, "band", 1, BANDS), band), axis=0)
    d_cols_all = (
        d_cols_all.reshape(BANDS, SENSORS, SLOTS, pix_share * D)
        .transpose(1, 0, 2, 3)
        .reshape(SENSORS * BMAX, pix_share * D)
        .astype(f32)
    )
    d_fc = xmm(h_all.reshape(SENSORS * BMAX, WG), d_cols_all, ((0,), (0,)))
    both = terms(sum_tok(both, chips), "band", 1, BANDS)
    smalls = tree_sum([v[:, :D] for v in both])
    dh = jnp.stack(in_order([v[:OWN, D:] for v in both], band)).reshape(BANDS, SENSORS, SLOTS, WG)
    dh = dh.transpose(1, 0, 2, 3).reshape(SENSORS * BMAX, WG)

    dh, d_fc, d_ff_down = lax.optimization_barrier((dh, d_fc, d_ff_down))
    dbias_full = jnp.pad(smalls[10:17], ((0, 1), (0, 0)))
    g = gen_bwd(
        seq, latent_tokens, gen_qkv, gen_out, gen_ff1, gen_ff2, gen_gains, fc_bias, z2, kept,
        jnp.pad(dh, ((0, 4), (0, 0))), dbias_full,
    )
    bup_shard = lax.dynamic_slice_in_dim(smalls[0:4].reshape(FF), me * ff_share, ff_share, 0)
    gains_shard = lax.dynamic_slice_in_dim(smalls[4:6], me * share, share, 1)
    shifts_shard = lax.dynamic_slice_in_dim(smalls[6:10], me * share, share, 1)
    return (
        out.reshape(1, 1, ROWS, D),
        d_pix.transpose(0, 2, 1).reshape(BANDS, 1, FRAME, width),
        tail_rows[CAP : 2 * CAP].reshape(1, 1, CAP, D),
        d_wqkv,
        d_proj[:, 3 * D :],
        d_ff_up,
        bup_shard,
        d_ff_down,
        gains_shard,
        shifts_shard,
        g[0],
        g[1],
        g[2],
        g[3],
        g[4],
        g[5],
        g[6],
        g[7].reshape(WG),
        d_fc,
        g[8],
    )


def solution(mesh):
    both = ("band", "tok")
    placed = (
        P(None, "tok", None, "band"),
        P(),
        P(),
        P(),
        P(None, "tok", None),
        P(None, "tok", None),
        P("band", "tok", None, None),
        P(both, None),
        P(both, None),
        P(both, None),
        P(both),
        P(both, None),
        P(None, both),
        P(None, both),
        P(),
        P(),
        P(),
        P(),
        P(),
        P(),
        P(),
        P(),
        P(None, "tok"),
        P(),
        P("band", "tok", None, None),
    )
    return jax.shard_map(
        shards,
        mesh=mesh,
        in_specs=placed,
        out_specs=(
            P("band", "tok", None, None),
            P(None, "tok", None, "band"),
            P("band", "tok", None, None),
            P(both, None),
            P(both, None),
            P(both, None),
            P(both),
            P(both, None),
            P(None, both),
            P(None, both),
            P(),
            P(),
            P(),
            P(),
            P(),
            P(),
            P(),
            P(),
            P(None, "tok"),
            P(),
        ),
        check_vma=False,
    )
```

```python
import math

import jax
import jax.numpy as jnp
from jax import lax
from jax.experimental import pallas as pl
from jax.experimental.pallas import tpu as pltpu
from jax.sharding import PartitionSpec as P

D = 768
HEADS = 12
HD = 64
FF = 3072
WG = 128
GHEADS = 4
GHD = 32
GFF = 2048
NLAT = 128
PIX = 64
SENSORS = 7
BMAX = 12
CHIP = 256
CAP = 4
FRAME = 1024
ROWS = 1032
RP = 1040
CH = RP
BACK_ROWS = ((0, 528), (528, 512))
BANDS = 4
SLOTS = BMAX // BANDS
OWN = SENSORS * SLOTS
HALF = D // 2
QX = 96

f32 = jnp.float32
bf16 = jnp.bfloat16
BT = ("band", "tok")
HIGH = lax.Precision.HIGHEST
EPS = 1e-05
MASKED = -1000000000.0
MIB = 2**20
SHORT = pl.CostEstimate(flops=2 * 10**8, bytes_accessed=MIB // 4, transcendentals=0)


def mm(a, b):
    return lax.dot_general(a, b, (((1,), (0,)), ((), ())), preferred_element_type=f32)


def mm_nt(a, b):
    return lax.dot_general(a, b, (((1,), (1,)), ((), ())), preferred_element_type=f32)


def mm_tn(a, b):
    return lax.dot_general(a, b, (((0,), (0,)), ((), ())), preferred_element_type=f32)


def xmm(a, b, dims=((1,), (0,))):
    return lax.dot_general(a, b, (dims, ((), ())), precision=HIGH, preferred_element_type=f32)


def whole(shape):
    return pl.BlockSpec(shape, lambda *_: (0,) * len(shape))


def like(shape, dtype):
    return jax.ShapeDtypeStruct(shape, dtype)


def params(mib):
    return pltpu.CompilerParams(vmem_limit_bytes=mib * MIB)


def center(x):
    xc = x - jnp.mean(x, axis=1, keepdims=True)
    r = lax.rsqrt(jnp.mean(xc * xc, axis=1, keepdims=True) + EPS)
    return xc * r, r


def gelu_parts(u):
    phi = 0.5 + 0.5 * lax.erf(u * math.sqrt(0.5))
    slope = phi + u * (math.sqrt(0.5 / math.pi) * jnp.exp(-0.5 * u * u))
    return u * phi, slope


def col8(v):
    return jnp.sum(v.reshape(v.shape[0] // 8, 8, v.shape[1]), axis=0)


def total(v):
    return jnp.sum(v, axis=0, keepdims=True)


def head_lanes(h):
    lane = lax.broadcasted_iota(jnp.int32, (1, WG), 1)
    return (lane // GHD == h).astype(f32)


def gen_forward(x, latent, bias, w_qkv, w_out, ff1, ff2, gains, shifts):
    scale = 1.0 / math.sqrt(GHD)
    qkv = xmm(x, w_qkv)
    kv = xmm(latent, w_qkv[:, WG:])
    q = qkv[:, :WG] * scale
    k = jnp.concatenate([kv[:, :WG], qkv[:, WG : 2 * WG]], axis=0)
    v = jnp.concatenate([kv[:, WG:], qkv[:, 2 * WG :]], axis=0)
    mixed = jnp.zeros((QX, WG), f32)
    probs = []
    for h in range(GHEADS):
        lanes = head_lanes(h)
        s = xmm(q * lanes, k, ((1,), (1,))) + bias
        e = jnp.exp(s - jnp.max(s, axis=1, keepdims=True))
        p = e / jnp.sum(e, axis=1, keepdims=True)
        probs.append(p)
        mixed = mixed + xmm(p, v * lanes)
    hat1, r1 = center(x + xmm(mixed, w_out))
    z1 = hat1 * gains[0:1] + shifts[0:1]
    act, slope = gelu_parts(xmm(z1, ff1))
    hat2, r2 = center(z1 + xmm(act, ff2))
    z2 = hat2 * gains[1:2] + shifts[1:2]
    return z2, (q, k, v, probs, mixed, hat1, r1, z1, act, slope, hat2, r2)


GEN_KEPT = [(QX, WG)] + [(NLAT + QX, WG)] * 2 + [(GHEADS, QX, NLAT + QX)] + [(QX, WG)] * 4 + [(QX, GFF)] * 2 + [(QX, WG)] * 2


def gen_fwd_kernel(
    x, latent, bias, w_qkv, w_out, ff1, ff2, gains, shifts, fc_bias, chosen, fc_kernel, z2_o, bias_o, part_o, *kept_o
):
    z2, kept = gen_forward(
        x[...], latent[...], bias[...], w_qkv[...], w_out[...], ff1[...], ff2[...], gains[...], shifts[...]
    )
    z2_o[...] = z2
    bias_o[...] = xmm(z2[QX - 8 :], fc_bias[...])
    part_o[...] = xmm(xmm(chosen[...], z2 + x[...]), fc_kernel[...]).astype(bf16)
    for ref, shape, v in zip(kept_o, GEN_KEPT, kept):
        if isinstance(v, list):
            for h in range(GHEADS):
                ref[h] = v[h]
        else:
            ref[...] = jnp.broadcast_to(v, shape)


def gen_fwd(x, latent, bias, w_qkv, w_out, ff1, ff2, gains, shifts, fc_bias, chosen, fc_kernel):
    args = (x, latent, bias, w_qkv, w_out, ff1, ff2, gains, shifts, fc_bias, chosen, fc_kernel)
    part = (chosen.shape[0], fc_kernel.shape[1])
    return pl.pallas_call(
        gen_fwd_kernel,
        in_specs=[whole(a.shape) for a in args],
        out_specs=[whole((QX, WG)), whole((8, D)), whole(part)] + [whole(t) for t in GEN_KEPT],
        out_shape=[like((QX, WG), f32), like((8, D), f32), like(part, bf16)] + [like(t, f32) for t in GEN_KEPT],
        compiler_params=params(62),
        cost_estimate=SHORT,
        name="gen_fwd",
    )(*args)


def norm_back(g, hat, r, gain):
    s = g * gain
    return r * (s - jnp.mean(s, axis=1, keepdims=True) - hat * jnp.mean(s * hat, axis=1, keepdims=True))


def gen_bwd_kernel(
    x, latent, w_qkv, w_out, ff1, ff2, gains, fc_bias, z2, q, k, v, probs, mixed, hat1, r1, z1, act, slope, hat2, r2,
    dh, dbias, dqkv_o, dout_o, dff1_o, dff2_o, dgains_o, dshifts_o, dlat_o, dtok_o, dfcb_o,
):
    scale = 1.0 / math.sqrt(GHD)
    xv, lat, gainv = x[...], latent[...], gains[...]
    z2, q, k, v, mixed, hat1, r1, z1, act, slope, hat2, r2 = (
        ref[...] for ref in (z2, q, k, v, mixed, hat1, r1, z1, act, slope, hat2, r2)
    )
    db = dbias[...]
    dfcb_o[...] = xmm(z2[QX - 8 :], db, ((0,), (0,)))
    dz2 = jnp.concatenate([dh[...], xmm(db, fc_bias[...], ((1,), (1,)))], axis=0)
    dw2 = norm_back(dz2, hat2, r2, gainv[1:2])
    dff2_o[...] = xmm(act, dw2, ((0,), (0,)))
    du = xmm(dw2, ff2[...], ((1,), (1,))) * slope
    dff1_o[...] = xmm(z1, du, ((0,), (0,)))
    dz1 = dw2 + xmm(du, ff1[...], ((1,), (1,)))
    dw1 = norm_back(dz1, hat1, r1, gainv[0:1])
    dgains_o[...] = jnp.concatenate([total(dz1 * hat1), total(dz2 * hat2)], axis=0)
    dshifts_o[...] = jnp.concatenate([total(dz1), total(dz2)], axis=0)
    dout_o[...] = xmm(mixed, dw1, ((0,), (0,)))
    dmix = xmm(dw1, w_out[...], ((1,), (1,)))
    dq = jnp.zeros((QX, WG), f32)
    dk = jnp.zeros((NLAT + QX, WG), f32)
    dv = jnp.zeros((NLAT + QX, WG), f32)
    for h in range(GHEADS):
        lanes = head_lanes(h)
        p = probs[h]
        dm = dmix * lanes
        dp = xmm(dm, v, ((1,), (1,)))
        ds = p * (dp - jnp.sum(p * dp, axis=1, keepdims=True))
        dv = dv + xmm(p, dm, ((0,), (0,)))
        dq = dq + xmm(ds, k * lanes)
        dk = dk + xmm(ds, q * lanes, ((0,), (0,)))
    dq = dq * scale
    dx = jnp.concatenate([dq, dk[NLAT:], dv[NLAT:]], axis=1)
    dl = jnp.concatenate([dk[:NLAT], dv[:NLAT]], axis=1)
    wv = w_qkv[...]
    from_x = xmm(xv, dx, ((0,), (0,)))
    from_l = xmm(lat, dl, ((0,), (0,)))
    dqkv_o[:, :WG] = from_x[:, :WG]
    dqkv_o[:, WG:] = from_x[:, WG:] + from_l
    dlat_o[...] = xmm(dl, wv[:, WG:], ((1,), (1,)))
    dx_full = dw1 + xmm(dx, wv, ((1,), (1,)))
    dtok_o[...] = total(dx_full[QX - 8 : QX - 8 + SENSORS])


def gen_bwd(x, latent, w_qkv, w_out, ff1, ff2, gains, fc_bias, z2, kept, dh, dbias):
    args = (x, latent, w_qkv, w_out, ff1, ff2, gains, fc_bias, z2, *kept, dh, dbias)
    shapes = [(WG, 3 * WG), (WG, WG), (WG, GFF), (GFF, WG), (2, WG), (2, WG), (NLAT, WG), (1, WG), (WG, D)]
    return pl.pallas_call(
        gen_bwd_kernel,
        in_specs=[whole(a.shape) for a in args],
        out_specs=[whole(s) for s in shapes],
        out_shape=[like(s, f32) for s in shapes],
        compiler_params=params(62),
        cost_estimate=SHORT,
        name="gen_bwd",
    )(*args)


def embed_kernel(sens, core, *refs):
    n = len(refs) // 3 - 2
    pix, own, other = refs[:n], refs[n : 2 * n], refs[2 * n : 3 * n]
    bias, extra, gains, shifts, x0_o, n1_o = refs[3 * n :]
    c = pl.program_id(0)
    rows = pl.ds(c * CHIP, CHIP)
    row = bias[pl.ds(sens[c], 1), :]
    for half, ker in ((core[0], own), (1 - core[0], other)):
        acc = mm_tn(pix[0][...], ker[0][0])
        for r in range(1, n):
            acc = acc + mm_tn(pix[r][...], ker[r][0])
        x0_o[rows, pl.ds(pl.multiple_of(half * HALF, HALF), HALF)] = acc
    x = x0_o[rows, :] + row
    x0_o[rows, :] = x
    hat, _ = center(x)
    n1_o[rows, :] = (hat * gains[0:1] + shifts[0:1]).astype(bf16)

    @pl.when(c == CAP - 1)
    def _():
        e = extra[...]
        x0_o[FRAME:, :] = e
        h, _ = center(e)
        n1_o[FRAME:, :] = (h * gains[0:1] + shifts[0:1]).astype(bf16)


def embed(sens, core, pix, own, other, bias, extra, gains, shifts):
    heights = [v.shape[1] for v in own]
    kernels = [pl.BlockSpec((1, n, HALF), lambda c, s, _: (s[c], 0, 0)) for n in heights]
    return pl.pallas_call(
        embed_kernel,
        grid_spec=pltpu.PrefetchScalarGridSpec(
            num_scalar_prefetch=2,
            grid=(CAP,),
            in_specs=[pl.BlockSpec((n, CHIP), lambda c, *_, at=at: (at, c)) for n, (_, at) in zip(heights, pix)]
            + kernels
            + kernels
            + [whole((8, D)), whole((RP - FRAME, D)), whole((8, D)), whole((8, D))],
            out_specs=[whole((RP, D)), whole((RP, D))],
        ),
        out_shape=[like((RP, D), f32), like((RP, D), bf16)],
        compiler_params=params(62),
        cost_estimate=pl.CostEstimate(flops=2 * FRAME * D * D, bytes_accessed=14 * MIB, transcendentals=0),
        name="embed",
    )(sens, core, *[v for v, _ in pix], *own, *other, bias, extra, gains, shifts)


def frame_kernel_grad_kernel(de, *refs):
    g = de[0]
    for pix, out in zip(refs[:BANDS], refs[BANDS:]):
        out[0] = mm(pix[...], g).astype(bf16)


def frame_kernel_grad(de, pix):
    width = SLOTS * PIX
    return pl.pallas_call(
        frame_kernel_grad_kernel,
        grid=(CAP,),
        in_specs=[pl.BlockSpec((1, CHIP, D), lambda c: (c, 0, 0))]
        + [pl.BlockSpec((width, CHIP), lambda c: (0, c))] * BANDS,
        out_specs=[pl.BlockSpec((1, width, D), lambda c: (c, 0, 0))] * BANDS,
        out_shape=[like((CAP, width, D), bf16)] * BANDS,
        compiler_params=params(62),
        cost_estimate=SHORT,
        name="frame_kernel_grad",
    )(de, *pix)


def frame_pixel_grad_kernel(sens, core, de, *refs):
    n = (len(refs) - BANDS) // 2
    own, other, outs = refs[:n], refs[n : 2 * n], refs[2 * n :]
    lo = de[0, :, pl.ds(pl.multiple_of(core[0] * HALF, HALF), HALF)]
    hi = de[0, :, pl.ds(pl.multiple_of((1 - core[0]) * HALF, HALF), HALF)]
    out, at = 0, 0
    for a, b in zip(own, other):
        rows = a.shape[1]
        outs[out][at : at + rows, :] = (mm_nt(a[0], lo) + mm_nt(b[0], hi)).astype(bf16)
        at += rows
        if at == outs[out].shape[0]:
            out, at = out + 1, 0


def frame_pixel_grad(sens, core, de, own, other):
    width = SLOTS * PIX
    kernels = [pl.BlockSpec((1, v.shape[1], HALF), lambda c, s, _: (s[c], 0, 0)) for v in own]
    return pl.pallas_call(
        frame_pixel_grad_kernel,
        grid_spec=pltpu.PrefetchScalarGridSpec(
            num_scalar_prefetch=2,
            grid=(CAP,),
            in_specs=[pl.BlockSpec((1, CHIP, D), lambda c, *_: (c, 0, 0))] + kernels + kernels,
            out_specs=[pl.BlockSpec((width, CHIP), lambda c, *_: (0, c))] * BANDS,
        ),
        out_shape=[like((width, FRAME), bf16)] * BANDS,
        compiler_params=params(62),
        cost_estimate=SHORT,
        name="frame_pixel_grad",
    )(sens, core, de, *own, *other)


def by_sensor_kernel(sens, valid, *refs):
    parts, out, acc = refs[:BANDS], refs[BANDS], refs[BANDS + 1]
    acc[...] = jnp.zeros_like(acc)
    for r in range(BANDS):
        for c in range(CAP):
            s = sens[r * CAP + c]
            acc[s] = acc[s] + parts[r][c].astype(f32)
    for s in range(SENSORS):
        for j in range(SLOTS):
            rows = slice(j * PIX, (j + 1) * PIX)
            keep = (valid[s * SLOTS + j] != 0).astype(f32)
            out[s, rows, :] = (acc[s, rows, :] * keep).astype(bf16)


def by_sensor(sens, valid, parts):
    width = SLOTS * PIX
    return pl.pallas_call(
        by_sensor_kernel,
        grid_spec=pltpu.PrefetchScalarGridSpec(
            num_scalar_prefetch=2,
            grid=(1,),
            in_specs=[whole((CAP, width, D))] * BANDS,
            out_specs=whole((SENSORS, width, D)),
            scratch_shapes=[pltpu.VMEM((SENSORS, width, D), f32)],
        ),
        out_shape=like((SENSORS, width, D), bf16),
        compiler_params=params(62),
        cost_estimate=SHORT,
        name="by_sensor",
    )(sens, valid, *parts)


def small_sums_kernel(sens, d_bup, small1, small2, tail, de, out, acc):
    acc[...] = jnp.zeros_like(acc)
    for c in range(CAP):
        row = pl.ds(sens[c], 1)
        acc[row, :] = acc[row, :] + total(col8(de[c].astype(f32)))
    for a in range(4):
        out[a : a + 1, :] = d_bup[0:1, a * D : (a + 1) * D]
    out[4:5, :] = small1[0:1, :]
    out[5:6, :] = small2[0:1, :]
    out[6:7, :] = small1[1:2, :]
    out[7:9, :] = small2[1:3, :]
    out[9:10, :] = total(tail[0:CAP, :])
    out[10:17, :] = acc[0:SENSORS, :]
    out[17:24, :] = jnp.zeros((7, D), f32)


def small_sums(sens, d_bup, small1, small2, tail, de):
    args = (d_bup, small1, small2, tail, de)
    return pl.pallas_call(
        small_sums_kernel,
        grid_spec=pltpu.PrefetchScalarGridSpec(
            num_scalar_prefetch=1,
            grid=(1,),
            in_specs=[whole(a.shape) for a in args],
            out_specs=whole((24, D)),
            scratch_shapes=[pltpu.VMEM((8, D), f32)],
        ),
        out_shape=like((24, D), f32),
        compiler_params=params(62),
        cost_estimate=SHORT,
        name="small_sums",
    )(sens, *args)


def columns_kernel(fc_kernel, smalls, *refs):
    *parts, cols_o, both_o = refs
    cols = tree_sum([p[...].astype(f32) for p in parts]).astype(bf16)
    cols_o[...] = cols
    cols = cols.astype(f32)
    dh = jnp.zeros((OWN, WG), f32)
    for i in range(cols.shape[1]):
        dh = dh + xmm(cols[:, i, :], fc_kernel[:, i * D : (i + 1) * D], ((1,), (1,)))
    both_o[:, :D] = smalls[...]
    both_o[:, D:] = jnp.concatenate([dh, jnp.zeros((24 - OWN, WG), f32)], axis=0)


def columns(fc_kernel, smalls, parts):
    shape = parts[0].shape
    return pl.pallas_call(
        columns_kernel,
        in_specs=[whole(fc_kernel.shape), whole((24, D))] + [whole(shape)] * len(parts),
        out_specs=[whole(shape), whole((24, D + WG))],
        out_shape=[like(shape, bf16), like((24, D + WG), f32)],
        compiler_params=params(62),
        cost_estimate=SHORT,
        name="columns",
    )(fc_kernel, smalls, *parts)


GH = 4
GW = GH * HD
GROUPS = HEADS // GH


def attn_fwd_kernel(n1, wq, wk, wv, wo, x0, qa, ka, gains, shifts, q_o, k_o, v_o, o_o, p_o, x1_o, n2_o):
    g = pl.program_id(0)

    @pl.when(g == 0)
    def _():
        x1_o[...] = x0[...]

    for c in range(RP // CH):
        s = pl.ds(c * CH, CH)
        q_o[s, :] = mm(n1[s, :], wq[...]).astype(bf16)
        k_o[s, :] = mm(n1[s, :], wk[...]).astype(bf16)
        v_o[s, :] = mm(n1[s, :], wv[...]).astype(bf16)
    qav = qa[...]
    kav = ka[...]
    for h in range(GH):
        hs = slice(h * HD, (h + 1) * HD)
        kh = jnp.concatenate([k_o[:, hs], kav], axis=1)
        vh = v_o[:, hs]
        for c in range(RP // CH):
            s = pl.ds(c * CH, CH)
            qh = jnp.concatenate([q_o[s, hs] * jnp.bfloat16(0.125), qav[c * CH : (c + 1) * CH]], axis=1)
            sc = mm_nt(qh, kh)
            e = jnp.exp(sc - jnp.max(sc, axis=1, keepdims=True))
            p = (e * (1.0 / jnp.sum(e, axis=1, keepdims=True))).astype(bf16)
            p_o[h, s, :] = p
            o_o[s, hs] = mm(p, vh).astype(bf16)
    for c in range(RP // CH):
        s = pl.ds(c * CH, CH)
        x1_o[s, :] += mm(o_o[s, :], wo[...])

    @pl.when(g == pl.num_programs(0) - 1)
    def _():
        for c in range(RP // CH):
            s = pl.ds(c * CH, CH)
            hat, _ = center(x1_o[s, :])
            n2_o[s, :] = (hat * gains[1:2, :] + shifts[1:2, :]).astype(bf16)


def attn_fwd(n1, weights, late, x0, qa, ka, gains, shifts):
    return pl.pallas_call(
        attn_fwd_kernel,
        grid=(GROUPS,),
        in_specs=[
            whole((RP, D)),
            pl.BlockSpec((D, GW), lambda g: (0, g)),
            pl.BlockSpec((D, GW), lambda g: (0, GROUPS + g)),
            pl.BlockSpec((D, GW), lambda g: (0, 2 * GROUPS + g)),
            pl.BlockSpec((GW, D), lambda g: (g, 8)),
            whole((RP, D)),
            whole((RP, HD)),
            whole((RP, HD)),
            whole((8, D)),
            whole((8, D)),
        ],
        out_specs=[pl.BlockSpec((RP, GW), lambda g: (0, g))] * 4
        + [pl.BlockSpec((GH, RP, RP), lambda g: (g, 0, 0)), whole((RP, D)), whole((RP, D))],
        out_shape=[like((RP, D), bf16)] * 4
        + [like((HEADS, RP, RP), bf16), like((RP, D), f32), like((RP, D), bf16)],
        compiler_params=params(60),
        cost_estimate=pl.CostEstimate(flops=5 * 10**10, bytes_accessed=50 * MIB, transcendentals=0),
        name="attn_fwd",
    )(n1, weights, weights, weights, late, x0, qa, ka, gains, shifts)


def attn_bwd_kernel(
    dx1b, wo, q, k, v, o, p, wq, wk, wv, x0, dx1, gains,
    dq_o, dk_o, dv_o, de_o, tail_o, small_o, dn1_s, do_s, ds_s,
):
    g = pl.program_id(0)

    @pl.when(g == 0)
    def _():
        dn1_s[...] = jnp.zeros_like(dn1_s)

    for c0, cn in BACK_ROWS:
        s = pl.ds(c0, cn)
        do_s[s, :] = mm_nt(dx1b[s, :], wo[...]).astype(bf16)
    for h in range(GH):
        hs = slice(h * HD, (h + 1) * HD)
        vh = v[:, hs]
        kh = k[:, hs]
        qh = q[:, hs]
        doh = do_s[:, hs]
        for c0, cn in BACK_ROWS:
            s = pl.ds(c0, cn)
            dc = do_s[s, hs]
            inner = jnp.sum(dc.astype(f32) * o[s, hs].astype(f32), axis=1, keepdims=True)
            ds = (p[h, s, :].astype(f32) * (mm_nt(dc, vh) - inner)).astype(bf16)
            ds_s[s, :] = ds
            dq_o[s, hs] = (mm(ds, kh) * 0.125).astype(bf16)
        dk_o[:, hs] = (mm(qh.T, ds_s[...]) * 0.125).T.astype(bf16)
        dv_o[:, hs] = mm(doh.T, p[h]).T.astype(bf16)
    for c0, cn in BACK_ROWS:
        s = pl.ds(c0, cn)
        dn1_s[s, :] += mm_nt(dq_o[s, :], wq[...]) + mm_nt(dk_o[s, :], wk[...]) + mm_nt(dv_o[s, :], wv[...])

    @pl.when(g == pl.num_programs(0) - 1)
    def _():
        gg = jnp.zeros((8, D), f32)
        gs = jnp.zeros((8, D), f32)
        for c0, cn in BACK_ROWS:
            s = pl.ds(c0, cn)
            hat, r = center(x0[s, :])
            gr = dn1_s[s, :]
            gg = gg + col8(gr * hat)
            gs = gs + col8(gr)
            dn1_s[s, :] = dx1[s, :] + norm_back(gr, hat, r, gains[0:1, :])
        de_o[...] = dn1_s[:FRAME, :].astype(bf16)
        tail_o[...] = dn1_s[FRAME:, :]
        small_o[0:1, :] = total(gg)
        small_o[1:2, :] = total(gs)
        small_o[2:8, :] = jnp.zeros((6, D), f32)


def attn_bwd(dx1b, weights, late, q, k, v, o, p, x0, dx1, gains):
    col = pl.BlockSpec((RP, GW), lambda g: (0, g))
    return pl.pallas_call(
        attn_bwd_kernel,
        grid=(GROUPS,),
        in_specs=[
            whole((RP, D)),
            pl.BlockSpec((GW, D), lambda g: (g, 8)),
            col,
            col,
            col,
            col,
            pl.BlockSpec((GH, RP, RP), lambda g: (g, 0, 0)),
            pl.BlockSpec((D, GW), lambda g: (0, g)),
            pl.BlockSpec((D, GW), lambda g: (0, GROUPS + g)),
            pl.BlockSpec((D, GW), lambda g: (0, 2 * GROUPS + g)),
            whole((RP, D)),
            whole((RP, D)),
            whole((8, D)),
        ],
        out_specs=[col, col, col, whole((FRAME, D)), whole((RP - FRAME, D)), whole((8, D))],
        out_shape=[like((RP, D), bf16)] * 3 + [like((FRAME, D), bf16), like((RP - FRAME, D), f32), like((8, D), f32)],
        scratch_shapes=[pltpu.VMEM((RP, D), f32), pltpu.VMEM((RP, GW), bf16), pltpu.VMEM((RP, RP), bf16)],
        compiler_params=params(62),
        cost_estimate=pl.CostEstimate(flops=5 * 10**10, bytes_accessed=50 * MIB, transcendentals=0),
        name="attn_bwd",
    )(dx1b, late, q, k, v, o, p, weights, weights, weights, x0, dx1, gains)


def proj_grad_kernel(share, core, n1, dq, dk, dv, o, dx1b, qkv_o, out_o):
    def split(v, out, columns):
        if share % 8:
            parts = (v[: v.shape[0] // 2], v[v.shape[0] // 2 :])
        else:
            pieces = [v[i * share : (i + 1) * share] for i in range(v.shape[0] // share)]
            parts = (jnp.concatenate(pieces[0::2], axis=0), jnp.concatenate(pieces[1::2], axis=0))
        for parity, part in enumerate(parts):
            slot = parity if share % 8 else core[0] if parity == 0 else 1 - core[0]
            out[slot, :, columns] = part.astype(bf16)

    for i, part in enumerate((dq, dk, dv)):
        split(mm_tn(n1[...], part[...]), qkv_o, slice(i * GW, (i + 1) * GW))
    split(mm_tn(o[...], dx1b[...]), out_o, slice(0, GW))


def proj_grad(share, core, n1, dq, dk, dv, o, dx1b):
    col = pl.BlockSpec((RP, GW), lambda g, c: (0, g))
    return pl.pallas_call(
        lambda *refs: proj_grad_kernel(share, *refs),
        grid_spec=pltpu.PrefetchScalarGridSpec(
            num_scalar_prefetch=1,
            grid=(GROUPS,),
            in_specs=[whole((RP, D)), col, col, col, whole((RP, D)), col],
            out_specs=[
                pl.BlockSpec((2, D // 2, 3 * GW), lambda g, c: (0, 0, g)),
                pl.BlockSpec((2, D // 2, GW), lambda g, c: (0, 0, g)),
            ],
        ),
        out_shape=[like((2, D // 2, 3 * D), bf16), like((2, D // 2, D), bf16)],
        compiler_params=params(62),
        cost_estimate=SHORT,
        name="proj_grad",
    )(core, n1, dq, dk, dv, o, dx1b)


FB = 768


def ffn_kernel(
    share, n2, dout, x1, wup, bup, wdown, gains, shifts,
    out, dw, dbup, dx1_o, dx1b_o, small_o, act_s, du_s, dn2_s, out_s, wd_s, dup_s, ddown_s, sems,
):
    j = pl.program_id(0)
    steps = pl.num_programs(0)
    rows = FB // 4
    shards_here = rows // share

    @pl.when(j == 0)
    def _():
        out_s[...] = x1[...] + shifts[2:3, :]
        dn2_s[...] = jnp.zeros_like(dn2_s)

    wd = wdown[...].astype(f32)
    wd_s[...] = jnp.concatenate(
        [wd[i * share : (i + 1) * share, a * D : (a + 1) * D] for i in range(shards_here) for a in range(4)], axis=0
    ).astype(bf16)
    cs = jnp.zeros((8, FB), f32)
    for c in range(RP // CH):
        s = pl.ds(c * CH, CH)
        u = mm(n2[s, :], wup[...]) + bup[...]
        da = mm_nt(dout[s, :], wd_s[...]).astype(bf16).astype(f32)
        act, slope = gelu_parts(u)
        act = act.astype(bf16)
        act_s[s, :] = act
        du = (da * slope).astype(bf16)
        du_s[s, :] = du
        cs = cs + col8(du.astype(f32))
        out_s[s, :] += mm(act, wd_s[...])
        dn2_s[s, :] += mm_nt(du, wup[...])
    dbup[...] = jnp.broadcast_to(total(cs), (8, FB))

    def copies(step):
        slot = lax.rem(step, 2)
        up = pltpu.make_async_copy(
            dup_s.at[slot], dw.at[:, pl.ds(pl.multiple_of(step * FB, FB), FB)], sems.at[0, slot]
        )
        down = pltpu.make_async_copy(
            ddown_s.at[slot], dw.at[pl.ds(pl.multiple_of(step * rows, rows), rows), pl.ds(FF, FF)], sems.at[1, slot]
        )
        return up, down

    @pl.when(j >= 2)
    def _():
        for copy in copies(j - 2):
            copy.wait()

    slot = lax.rem(j, 2)
    dup_s[slot] = mm_tn(n2[...], du_s[...]).astype(bf16)
    dd = mm_tn(act_s[...], dout[...])
    for a in range(4):
        ddown_s[slot, :, a * D : (a + 1) * D] = jnp.concatenate(
            [dd[(4 * i + a) * share : (4 * i + a + 1) * share] for i in range(shards_here)], axis=0
        ).astype(bf16)
    for copy in copies(j):
        copy.start()

    @pl.when(j == steps - 1)
    def _():
        out[...] = out_s[:ROWS, :]
        gg = jnp.zeros((8, D), f32)
        gs = jnp.zeros((8, D), f32)
        gd = jnp.zeros((8, D), f32)
        for c in range(RP // CH):
            s = pl.ds(c * CH, CH)
            hat, r = center(x1[s, :])
            g = dn2_s[s, :]
            do = dout[s, :].astype(f32)
            gg = gg + col8(g * hat)
            gs = gs + col8(g)
            gd = gd + col8(do)
            dx1 = do + norm_back(g, hat, r, gains[1:2, :])
            dx1_o[s, :] = dx1
            dx1b_o[s, :] = dx1.astype(bf16)
        small_o[0:1, :] = total(gg)
        small_o[1:2, :] = total(gs)
        small_o[2:3, :] = total(gd)
        small_o[3:8, :] = jnp.zeros((5, D), f32)
        for step in (steps - 2, steps - 1):
            for copy in copies(step):
                copy.wait()


def ffn(share, n2, dout, x1, weights, b_up, gains, shifts):
    return pl.pallas_call(
        lambda *refs: ffn_kernel(share, *refs),
        grid=(FF // FB,),
        in_specs=[
            whole((RP, D)),
            whole((RP, D)),
            whole((RP, D)),
            pl.BlockSpec((D, FB), lambda g: (0, 4 + g)),
            pl.BlockSpec((1, FB), lambda g: (0, g)),
            pl.BlockSpec((FB // 4, FF), lambda g: (g, 0)),
            whole((8, D)),
            whole((8, D)),
        ],
        out_specs=[
            whole((ROWS, D)),
            pl.BlockSpec(memory_space=pl.ANY),
            pl.BlockSpec((8, FB), lambda g: (0, g)),
            whole((RP, D)),
            whole((RP, D)),
            whole((8, D)),
        ],
        out_shape=[
            like((ROWS, D), f32),
            like((D, 2 * FF), bf16),
            like((8, FF), f32),
            like((RP, D), f32),
            like((RP, D), bf16),
            like((8, D), f32),
        ],
        scratch_shapes=[pltpu.VMEM((RP, FB), bf16)] * 2
        + [pltpu.VMEM((RP, D), f32)] * 2
        + [
            pltpu.VMEM((FB, D), bf16),
            pltpu.VMEM((2, D, FB), bf16),
            pltpu.VMEM((2, FB // 4, FF), bf16),
            pltpu.SemaphoreType.DMA((2, 2)),
        ],
        compiler_params=params(62),
        cost_estimate=pl.CostEstimate(flops=45 * 10**9, bytes_accessed=30 * MIB, transcendentals=0),
        name="ffn",
    )(n2, dout, x1, weights, b_up, weights, gains, shifts)


def flip(v, axis, bits):
    return lax.ppermute(v, axis, [(i, i ^ bits) for i in range(lax.axis_size(axis))])


def terms(v, axis, step, count):
    return [v] + [flip(v, axis, k * step) for k in range(1, count)]


def tree_sum(parts):
    parts = list(parts)
    while len(parts) > 1:
        parts = [parts[i] + parts[i + 1] for i in range(0, len(parts), 2)]
    return parts[0]


def in_order(parts, place):
    parts = list(parts)
    bit = 1
    while bit < len(parts):
        odd = (place & bit) != 0
        parts = [jnp.where(odd, parts[i ^ bit], parts[i]) for i in range(len(parts))]
        bit *= 2
    return parts


def pick(v, i, axis=0):
    return lax.dynamic_index_in_dim(v, i, axis, keepdims=False)


def sum_low(parts):
    return tree_sum([p.astype(f32) for p in parts])


def scatter_core(v, core):
    got = flip(pick(v, 1 - core, 2), "tok", 1)
    return sum_low([pick(v, core, 2), got]).astype(bf16)


def scatter_band(v, band):
    return sum_low([pick(v, band)] + [flip(pick(v, band ^ r), "band", r) for r in range(1, BANDS)])


def scatter_z(v, z, axis=0):
    return sum_low([pick(v, z, axis)] + [flip(pick(v, z ^ k, axis), "tok", 2 * k) for k in range(1, v.shape[axis])])


def sum_tok(v, chips):
    v = v + flip(v, "tok", 1)
    return tree_sum(terms(v, "tok", 2, chips))


def wave_features(wavelengths, wave_index):
    table_size = wavelengths.shape[0]
    picked = (wave_index[..., None] == jnp.arange(table_size, dtype=jnp.int32)).astype(f32)
    wave_values = jnp.sum(picked * wavelengths, axis=-1)
    half_width = WG // 2
    frequency = 1.0 / 10000.0 ** (jnp.arange(half_width, dtype=f32) / half_width)
    angles = 1000.0 * wave_values[..., None] * frequency
    return jnp.concatenate([jnp.sin(angles), jnp.cos(angles)], axis=-1)


def shards(
    pixels, wavelengths, wave_index, band_counts, sensors, chip_lengths, meta_rows,
    w_qkv, w_out, w_up, b_up, w_down, norm_gains, shifts,
    gen_qkv, gen_out, gen_ff1, gen_ff2, gen_gains, gen_shifts, latent_tokens, bias_token,
    fc_kernel, fc_bias, d_out,
):
    band = lax.axis_index("band")
    tok = lax.axis_index("tok")
    toks = lax.axis_size("tok")
    chips = toks // 2
    core = tok % 2
    z = tok // 2
    devices = BANDS * toks
    me = band * toks + tok
    share = D // devices
    ff_share = FF // devices
    pix_share = PIX // toks
    width = SLOTS * PIX

    pix_t = pixels.reshape(BANDS, FRAME, width).transpose(0, 2, 1)
    pix = [pick(pix_t, band)] + [flip(pick(pix_t, band ^ r), "band", r) for r in range(1, BANDS)]

    late = jnp.concatenate([w_down.reshape(4, share, D).transpose(1, 0, 2).reshape(share, FF), w_up, w_out], axis=1)
    late = lax.all_gather(late, BT, axis=0, tiled=True)

    vectors = jnp.concatenate([norm_gains.T, shifts.T, b_up.reshape(share, 4)], axis=1)
    vectors = jnp.pad(vectors, ((0, 0), (0, WG - vectors.shape[1])))
    bundle = terms(jnp.concatenate([w_qkv, vectors], axis=1), "tok", 2, chips)

    features = wave_features(wavelengths, wave_index).reshape(SENSORS * BMAX, WG)
    valid = jnp.arange(BMAX, dtype=jnp.int32)[None, :] < band_counts[:, None]
    seq = jnp.concatenate([features, jnp.zeros((4, WG), f32), jnp.broadcast_to(bias_token, (8, WG))], axis=0)
    sensor_ids = jnp.arange(SENSORS, dtype=jnp.int32)
    row_sensor = jnp.concatenate(
        [jnp.repeat(sensor_ids, BMAX), jnp.full((4,), 8, jnp.int32), sensor_ids, jnp.full((1,), 9, jnp.int32)]
    )
    key_ok = jnp.concatenate([valid.reshape(-1), jnp.zeros((4,), jnp.bool_), jnp.ones((8,), jnp.bool_)])
    allowed = (row_sensor[:, None] == row_sensor[None, :]) & key_ok[None, :]
    gen_bias = jnp.concatenate([jnp.zeros((QX, NLAT), f32), jnp.where(allowed, 0.0, MASKED)], axis=1)
    gen_args = (seq, latent_tokens, gen_bias, gen_qkv, gen_out, gen_ff1, gen_ff2, gen_gains, gen_shifts, fc_bias)
    own_row = sensor_ids[:, None] * BMAX + band * SLOTS + jnp.arange(SLOTS, dtype=jnp.int32)[None, :]
    own_valid = lax.dynamic_slice_in_dim(valid, band * SLOTS, SLOTS, 1).reshape(OWN)
    chosen = (own_row.reshape(OWN, 1) == jnp.arange(QX, dtype=jnp.int32)[None, :]) & own_valid[:, None]
    chosen = jnp.pad(chosen.astype(f32), ((0, 3), (0, 0)))
    z2, bias_vec, part, *kept = gen_fwd(*gen_args, chosen, fc_kernel)
    z2, part, pix, bundle = lax.optimization_barrier((z2, part, pix, bundle))
    h_all = (z2[: SENSORS * BMAX] + features).reshape(SENSORS, BMAX, WG)

    ends = jnp.cumsum(chip_lengths.reshape(BANDS, CAP), axis=-1)
    starts = jnp.arange(CAP, dtype=jnp.int32) * CHIP
    block_segment = jnp.sum((ends[:, None, :] <= starts[None, :, None]).astype(jnp.int32), axis=-1)
    block_sensor = jnp.take_along_axis(sensors.reshape(BANDS, CAP), block_segment, axis=1)
    own_ends = pick(ends, band)
    frame_sensor = [pick(block_sensor, band ^ r) for r in range(BANDS)]
    positions = jnp.arange(FRAME, dtype=jnp.int32)
    patch_segment = jnp.sum((own_ends[None, :] <= positions[:, None]).astype(jnp.int32), axis=-1)
    slot_ids = jnp.arange(CAP, dtype=jnp.int32)
    segment = jnp.concatenate([patch_segment, slot_ids, slot_ids, jnp.full((RP - ROWS,), CAP + 1, jnp.int32)])
    onehot = segment[:, None] == jnp.arange(HD, dtype=jnp.int32)[None, :]
    ka = onehot.astype(bf16)
    qa = jnp.where(onehot, 0.0, -(2.0**30)).astype(bf16)

    part = part[:OWN].reshape(OWN, pix_share, 2, HALF)
    mine = pick(part, core, 2)
    got = flip(pick(part, 1 - core, 2), "tok", 1)
    pair = jnp.where(core == 0, jnp.concatenate([mine, got], axis=1), jnp.concatenate([got, mine], axis=1))
    bundle = terms(jnp.stack(in_order(bundle, z)), "band", 1, BANDS)
    pairs = terms(pair, "tok", 2, chips)
    pairs, bundle = lax.optimization_barrier((pairs, bundle))
    k_own = jnp.concatenate(in_order(pairs, z), axis=1).reshape(SENSORS, width, HALF)
    k_x = flip(k_own, "band", 1)
    k_y = flip(k_own, "band", 2)
    bundle = jnp.stack(in_order(bundle, band))
    bundle_other = flip(bundle, "tok", 1)
    half = width // 2
    k_x, k_y, bundle_other = lax.optimization_barrier((k_x, k_y, bundle_other))
    ker_own = [k_own, k_x, k_y, flip(k_x[:, :half], "band", 2), flip(k_y[:, half:], "band", 1)]
    ker_other = [flip(v, "tok", 1) for v in ker_own]
    weights = jnp.where(
        core == 0, jnp.stack([bundle, bundle_other], axis=2), jnp.stack([bundle_other, bundle], axis=2)
    ).reshape(D, 3 * D + WG)
    rest = weights[:, 3 * D : 3 * D + 10].astype(f32)
    bias_up = rest[:, 6:10].reshape(1, FF)
    rest = rest.T
    gains = jnp.pad(rest[:2], ((0, 6), (0, 0)))
    shift_rows = jnp.pad(rest[2:6], ((0, 4), (0, 0)))

    extra_rows = jnp.concatenate(
        [
            jnp.broadcast_to(shift_rows[3], (CAP, D)),
            meta_rows.reshape(CAP, D).astype(f32),
            jnp.zeros((RP - ROWS, D), f32),
        ],
        axis=0,
    )
    which = core.reshape(1)
    parts = [(pix[0], 0), (pix[1], 0), (pix[2], 0), (pix[3], 0), (pix[3], 1)]
    x0, n1 = embed(frame_sensor[0], which, parts, ker_own, ker_other, bias_vec, extra_rows, gains, shift_rows)
    q, k, v, o, probs, x1, n2 = attn_fwd(n1, weights, late, x0, qa, ka, gains, shift_rows)
    dout = jnp.pad(d_out.reshape(ROWS, D), ((0, RP - ROWS), (0, 0)))
    out, d_ff, d_bup, dx1, dx1b, small2 = ffn(share, n2, dout, x1, late, bias_up, gains, shift_rows)
    d_ff = lax.psum_scatter(d_ff, BT, scatter_dimension=0, tiled=True).astype(f32)
    dq, dk, dv, de, tail_rows, small1 = attn_bwd(dx1b, weights, late, q, k, v, o, probs, x0, dx1, gains)

    de_blocks = de.reshape(CAP, CHIP, D)
    ker_grads = frame_kernel_grad(de_blocks, pix)
    ker_grads, n1, o, tail_rows = lax.optimization_barrier((ker_grads, n1, o, tail_rows))
    ker_grads = [ker_grads[0]] + [flip(ker_grads[r], "band", r) for r in range(1, BANDS)]
    proj = proj_grad(share, which, n1, dq, dk, dv, o, dx1b)
    if share % 8:
        proj = [v.reshape(D // (2 * share), 2, share, v.shape[2]) for v in proj]
        proj = [jnp.stack([pick(v, core, 1), pick(v, 1 - core, 1)]) for v in proj]
    proj = [v.reshape(2, BANDS, chips, share, -1) for v in proj]
    proj = [sum_low([v[0], flip(v[1], "tok", 1)]).astype(bf16) for v in proj]
    d_proj = scatter_z(jnp.concatenate(proj, axis=-1), z, 1).astype(bf16)
    pix_grads = frame_pixel_grad(frame_sensor[0], which, de_blocks, ker_own, ker_other)
    smalls = small_sums(frame_sensor[0], d_bup, small1, small2, tail_rows, de_blocks)

    ker_grads, pix_grads, d_proj, smalls = lax.optimization_barrier((ker_grads, pix_grads, d_proj, smalls))
    d_ker = by_sensor(jnp.concatenate(frame_sensor), own_valid.astype(jnp.int32), ker_grads)
    d_ker = scatter_core(d_ker.reshape(1, OWN * chips, 2, pix_share, D), core)
    d_ker = d_ker.reshape(OWN, chips, pix_share, D)
    d_ker = [pick(d_ker, z, 1)] + [flip(pick(d_ker, z ^ c, 1), "tok", 2 * c) for c in range(1, chips)]
    d_proj = scatter_band(d_proj, band)
    d_ker, d_proj = lax.optimization_barrier((d_ker, d_proj))
    d_cols, both = columns(fc_kernel, smalls, d_ker)
    d_wqkv = d_proj[:, : 3 * D].reshape(share, GROUPS, 3, GW).transpose(0, 2, 1, 3).reshape(share, 3 * D)
    d_pix = in_order([pix_grads[0]] + [flip(pix_grads[r], "band", r) for r in range(1, BANDS)], band)
    d_pix = jnp.stack(d_pix).astype(f32)
    d_ff_up = d_ff[:, :FF]
    d_ff_down = d_ff[:, FF:].reshape(share, 4, D).transpose(1, 0, 2).reshape(ff_share, D)
    d_cols_all = jnp.stack(in_order(terms(d_cols, "band", 1, BANDS), band), axis=0)
    d_cols_all = (
        d_cols_all.reshape(BANDS, SENSORS, SLOTS, pix_share * D)
        .transpose(1, 0, 2, 3)
        .reshape(SENSORS * BMAX, pix_share * D)
        .astype(f32)
    )
    d_fc = xmm(h_all.reshape(SENSORS * BMAX, WG), d_cols_all, ((0,), (0,)))
    bit = 1
    while bit < toks:
        both = both + flip(both, "tok", bit)
        bit *= 2
    got = flip(both, "band", 1)
    smalls = both[:, :D] + got[:, :D]
    both = jnp.concatenate([smalls, both[:, D:], got[:, D:]], axis=1)
    got = flip(both, "band", 2)
    smalls = smalls + got[:, :D]
    dh = [v[:OWN, at : at + WG] for v in (both, got) for at in (D, D + WG)]
    dh = jnp.stack(in_order(dh, band)).reshape(BANDS, SENSORS, SLOTS, WG)
    dh = dh.transpose(1, 0, 2, 3).reshape(SENSORS * BMAX, WG)

    dh, d_fc, d_ff_down = lax.optimization_barrier((dh, d_fc, d_ff_down))
    dbias_full = jnp.pad(smalls[10:17], ((0, 1), (0, 0)))
    g = gen_bwd(
        seq, latent_tokens, gen_qkv, gen_out, gen_ff1, gen_ff2, gen_gains, fc_bias, z2, kept,
        jnp.pad(dh, ((0, 4), (0, 0))), dbias_full,
    )
    bup_shard = lax.dynamic_slice_in_dim(smalls[0:4].reshape(FF), me * ff_share, ff_share, 0)
    gains_shard = lax.dynamic_slice_in_dim(smalls[4:6], me * share, share, 1)
    shifts_shard = lax.dynamic_slice_in_dim(smalls[6:10], me * share, share, 1)
    return (
        out.reshape(1, 1, ROWS, D),
        d_pix.transpose(0, 2, 1).reshape(BANDS, 1, FRAME, width),
        tail_rows[CAP : 2 * CAP].reshape(1, 1, CAP, D),
        d_wqkv,
        d_proj[:, 3 * D :],
        d_ff_up,
        bup_shard,
        d_ff_down,
        gains_shard,
        shifts_shard,
        g[0],
        g[1],
        g[2],
        g[3],
        g[4],
        g[5],
        g[6],
        g[7].reshape(WG),
        d_fc,
        g[8],
    )


def solution(mesh):
    both = ("band", "tok")
    placed = (
        P(None, "tok", None, "band"),
        P(),
        P(),
        P(),
        P(None, "tok", None),
        P(None, "tok", None),
        P("band", "tok", None, None),
        P(both, None),
        P(both, None),
        P(both, None),
        P(both),
        P(both, None),
        P(None, both),
        P(None, both),
        P(),
        P(),
        P(),
        P(),
        P(),
        P(),
        P(),
        P(),
        P(None, "tok"),
        P(),
        P("band", "tok", None, None),
    )
    return jax.shard_map(
        shards,
        mesh=mesh,
        in_specs=placed,
        out_specs=(
            P("band", "tok", None, None),
            P(None, "tok", None, "band"),
            P("band", "tok", None, None),
            P(both, None),
            P(both, None),
            P(both, None),
            P(both),
            P(both, None),
            P(None, both),
            P(None, both),
            P(),
            P(),
            P(),
            P(),
            P(),
            P(),
            P(),
            P(),
            P(None, "tok"),
            P(),
        ),
        check_vma=False,
    )
```

```python
import math

import jax
import jax.numpy as jnp
from jax import lax
from jax.experimental import pallas as pl
from jax.experimental.pallas import tpu as pltpu
from jax.sharding import PartitionSpec as P

D = 768
HEADS = 12
HD = 64
FF = 3072
WG = 128
GHEADS = 4
GHD = 32
GFF = 2048
NLAT = 128
PIX = 64
SENSORS = 7
BMAX = 12
CHIP = 256
CAP = 4
FRAME = 1024
ROWS = 1032
RP = 1040
CH = RP
BACK_ROWS = ((0, 528), (528, 512))
BANDS = 4
SLOTS = BMAX // BANDS
OWN = SENSORS * SLOTS
HALF = D // 2
QX = 96

f32 = jnp.float32
bf16 = jnp.bfloat16
BT = ("band", "tok")
HIGH = lax.Precision.HIGHEST
EPS = 1e-05
MASKED = -1000000000.0
MIB = 2**20
SHORT = pl.CostEstimate(flops=2 * 10**8, bytes_accessed=MIB // 4, transcendentals=0)


def mm(a, b):
    return lax.dot_general(a, b, (((1,), (0,)), ((), ())), preferred_element_type=f32)


def mm_nt(a, b):
    return lax.dot_general(a, b, (((1,), (1,)), ((), ())), preferred_element_type=f32)


def mm_tn(a, b):
    return lax.dot_general(a, b, (((0,), (0,)), ((), ())), preferred_element_type=f32)


def xmm(a, b, dims=((1,), (0,))):
    return lax.dot_general(a, b, (dims, ((), ())), precision=HIGH, preferred_element_type=f32)


def whole(shape):
    return pl.BlockSpec(shape, lambda *_: (0,) * len(shape))


def like(shape, dtype):
    return jax.ShapeDtypeStruct(shape, dtype)


def params(mib):
    return pltpu.CompilerParams(vmem_limit_bytes=mib * MIB)


def center(x):
    xc = x - jnp.mean(x, axis=1, keepdims=True)
    r = lax.rsqrt(jnp.mean(xc * xc, axis=1, keepdims=True) + EPS)
    return xc * r, r


def gelu_parts(u):
    phi = 0.5 + 0.5 * lax.erf(u * math.sqrt(0.5))
    slope = phi + u * (math.sqrt(0.5 / math.pi) * jnp.exp(-0.5 * u * u))
    return u * phi, slope


def col8(v):
    return jnp.sum(v.reshape(v.shape[0] // 8, 8, v.shape[1]), axis=0)


def total(v):
    return jnp.sum(v, axis=0, keepdims=True)


def head_lanes(h):
    lane = lax.broadcasted_iota(jnp.int32, (1, WG), 1)
    return (lane // GHD == h).astype(f32)


def gen_forward(x, latent, bias, w_qkv, w_out, ff1, ff2, gains, shifts):
    scale = 1.0 / math.sqrt(GHD)
    qkv = xmm(x, w_qkv)
    kv = xmm(latent, w_qkv[:, WG:])
    q = qkv[:, :WG] * scale
    k = jnp.concatenate([kv[:, :WG], qkv[:, WG : 2 * WG]], axis=0)
    v = jnp.concatenate([kv[:, WG:], qkv[:, 2 * WG :]], axis=0)
    mixed = jnp.zeros((QX, WG), f32)
    probs = []
    for h in range(GHEADS):
        lanes = head_lanes(h)
        s = xmm(q * lanes, k, ((1,), (1,))) + bias
        e = jnp.exp(s - jnp.max(s, axis=1, keepdims=True))
        p = e / jnp.sum(e, axis=1, keepdims=True)
        probs.append(p)
        mixed = mixed + xmm(p, v * lanes)
    hat1, r1 = center(x + xmm(mixed, w_out))
    z1 = hat1 * gains[0:1] + shifts[0:1]
    act, slope = gelu_parts(xmm(z1, ff1))
    hat2, r2 = center(z1 + xmm(act, ff2))
    z2 = hat2 * gains[1:2] + shifts[1:2]
    return z2, (q, k, v, probs, mixed, hat1, r1, z1, act, slope, hat2, r2)


GEN_KEPT = [(QX, WG)] + [(NLAT + QX, WG)] * 2 + [(GHEADS, QX, NLAT + QX)] + [(QX, WG)] * 4 + [(QX, GFF)] * 2 + [(QX, WG)] * 2


def gen_fwd_kernel(
    x, latent, bias, w_qkv, w_out, ff1, ff2, gains, shifts, fc_bias, chosen, fc_kernel, z2_o, bias_o, part_o, *kept_o
):
    z2, kept = gen_forward(
        x[...], latent[...], bias[...], w_qkv[...], w_out[...], ff1[...], ff2[...], gains[...], shifts[...]
    )
    z2_o[...] = z2
    bias_o[...] = xmm(z2[QX - 8 :], fc_bias[...])
    part_o[...] = xmm(xmm(chosen[...], z2 + x[...]), fc_kernel[...]).astype(bf16)
    for ref, shape, v in zip(kept_o, GEN_KEPT, kept):
        if isinstance(v, list):
            for h in range(GHEADS):
                ref[h] = v[h]
        else:
            ref[...] = jnp.broadcast_to(v, shape)


def gen_fwd(x, latent, bias, w_qkv, w_out, ff1, ff2, gains, shifts, fc_bias, chosen, fc_kernel):
    args = (x, latent, bias, w_qkv, w_out, ff1, ff2, gains, shifts, fc_bias, chosen, fc_kernel)
    part = (chosen.shape[0], fc_kernel.shape[1])
    return pl.pallas_call(
        gen_fwd_kernel,
        in_specs=[whole(a.shape) for a in args],
        out_specs=[whole((QX, WG)), whole((8, D)), whole(part)] + [whole(t) for t in GEN_KEPT],
        out_shape=[like((QX, WG), f32), like((8, D), f32), like(part, bf16)] + [like(t, f32) for t in GEN_KEPT],
        compiler_params=params(62),
        cost_estimate=SHORT,
        name="gen_fwd",
    )(*args)


def norm_back(g, hat, r, gain):
    s = g * gain
    return r * (s - jnp.mean(s, axis=1, keepdims=True) - hat * jnp.mean(s * hat, axis=1, keepdims=True))


def gen_bwd_kernel(
    x, latent, w_qkv, w_out, ff1, ff2, gains, fc_bias, z2, q, k, v, probs, mixed, hat1, r1, z1, act, slope, hat2, r2,
    dh, dbias, dqkv_o, dout_o, dff1_o, dff2_o, dgains_o, dshifts_o, dlat_o, dtok_o, dfcb_o,
):
    scale = 1.0 / math.sqrt(GHD)
    xv, lat, gainv = x[...], latent[...], gains[...]
    z2, q, k, v, mixed, hat1, r1, z1, act, slope, hat2, r2 = (
        ref[...] for ref in (z2, q, k, v, mixed, hat1, r1, z1, act, slope, hat2, r2)
    )
    db = dbias[...]
    dfcb_o[...] = xmm(z2[QX - 8 :], db, ((0,), (0,)))
    dz2 = jnp.concatenate([dh[...], xmm(db, fc_bias[...], ((1,), (1,)))], axis=0)
    dw2 = norm_back(dz2, hat2, r2, gainv[1:2])
    dff2_o[...] = xmm(act, dw2, ((0,), (0,)))
    du = xmm(dw2, ff2[...], ((1,), (1,))) * slope
    dff1_o[...] = xmm(z1, du, ((0,), (0,)))
    dz1 = dw2 + xmm(du, ff1[...], ((1,), (1,)))
    dw1 = norm_back(dz1, hat1, r1, gainv[0:1])
    dgains_o[...] = jnp.concatenate([total(dz1 * hat1), total(dz2 * hat2)], axis=0)
    dshifts_o[...] = jnp.concatenate([total(dz1), total(dz2)], axis=0)
    dout_o[...] = xmm(mixed, dw1, ((0,), (0,)))
    dmix = xmm(dw1, w_out[...], ((1,), (1,)))
    dq = jnp.zeros((QX, WG), f32)
    dk = jnp.zeros((NLAT + QX, WG), f32)
    dv = jnp.zeros((NLAT + QX, WG), f32)
    for h in range(GHEADS):
        lanes = head_lanes(h)
        p = probs[h]
        dm = dmix * lanes
        dp = xmm(dm, v, ((1,), (1,)))
        ds = p * (dp - jnp.sum(p * dp, axis=1, keepdims=True))
        dv = dv + xmm(p, dm, ((0,), (0,)))
        dq = dq + xmm(ds, k * lanes)
        dk = dk + xmm(ds, q * lanes, ((0,), (0,)))
    dq = dq * scale
    dx = jnp.concatenate([dq, dk[NLAT:], dv[NLAT:]], axis=1)
    dl = jnp.concatenate([dk[:NLAT], dv[:NLAT]], axis=1)
    wv = w_qkv[...]
    from_x = xmm(xv, dx, ((0,), (0,)))
    from_l = xmm(lat, dl, ((0,), (0,)))
    dqkv_o[:, :WG] = from_x[:, :WG]
    dqkv_o[:, WG:] = from_x[:, WG:] + from_l
    dlat_o[...] = xmm(dl, wv[:, WG:], ((1,), (1,)))
    dx_full = dw1 + xmm(dx, wv, ((1,), (1,)))
    dtok_o[...] = total(dx_full[QX - 8 : QX - 8 + SENSORS])


def gen_bwd(x, latent, w_qkv, w_out, ff1, ff2, gains, fc_bias, z2, kept, dh, dbias):
    args = (x, latent, w_qkv, w_out, ff1, ff2, gains, fc_bias, z2, *kept, dh, dbias)
    shapes = [(WG, 3 * WG), (WG, WG), (WG, GFF), (GFF, WG), (2, WG), (2, WG), (NLAT, WG), (1, WG), (WG, D)]
    return pl.pallas_call(
        gen_bwd_kernel,
        in_specs=[whole(a.shape) for a in args],
        out_specs=[whole(s) for s in shapes],
        out_shape=[like(s, f32) for s in shapes],
        compiler_params=params(62),
        cost_estimate=SHORT,
        name="gen_bwd",
    )(*args)


def embed_kernel(sens, core, *refs):
    n = len(refs) // 3 - 2
    pix, own, other = refs[:n], refs[n : 2 * n], refs[2 * n : 3 * n]
    bias, extra, gains, shifts, x0_o, n1_o = refs[3 * n :]
    c = pl.program_id(0)
    rows = pl.ds(c * CHIP, CHIP)
    row = bias[pl.ds(sens[c], 1), :]
    for half, ker in ((core[0], own), (1 - core[0], other)):
        acc = mm_tn(pix[0][...], ker[0][0])
        for r in range(1, n):
            acc = acc + mm_tn(pix[r][...], ker[r][0])
        x0_o[rows, pl.ds(pl.multiple_of(half * HALF, HALF), HALF)] = acc
    x = x0_o[rows, :] + row
    x0_o[rows, :] = x
    hat, _ = center(x)
    n1_o[rows, :] = (hat * gains[0:1] + shifts[0:1]).astype(bf16)

    @pl.when(c == CAP - 1)
    def _():
        e = extra[...]
        x0_o[FRAME:, :] = e
        h, _ = center(e)
        n1_o[FRAME:, :] = (h * gains[0:1] + shifts[0:1]).astype(bf16)


def embed(sens, core, pix, own, other, bias, extra, gains, shifts):
    heights = [v.shape[1] for v in own]
    kernels = [pl.BlockSpec((1, n, HALF), lambda c, s, _: (s[c], 0, 0)) for n in heights]
    return pl.pallas_call(
        embed_kernel,
        grid_spec=pltpu.PrefetchScalarGridSpec(
            num_scalar_prefetch=2,
            grid=(CAP,),
            in_specs=[pl.BlockSpec((n, CHIP), lambda c, *_, at=at: (at, c)) for n, (_, at) in zip(heights, pix)]
            + kernels
            + kernels
            + [whole((8, D)), whole((RP - FRAME, D)), whole((8, D)), whole((8, D))],
            out_specs=[whole((RP, D)), whole((RP, D))],
        ),
        out_shape=[like((RP, D), f32), like((RP, D), bf16)],
        compiler_params=params(62),
        cost_estimate=pl.CostEstimate(flops=2 * FRAME * D * D, bytes_accessed=14 * MIB, transcendentals=0),
        name="embed",
    )(sens, core, *[v for v, _ in pix], *own, *other, bias, extra, gains, shifts)


def frame_kernel_grad_kernel(de, *refs):
    g = de[0]
    for pix, out in zip(refs[:BANDS], refs[BANDS:]):
        out[0] = mm(pix[...], g).astype(bf16)


def frame_kernel_grad(de, pix):
    width = SLOTS * PIX
    return pl.pallas_call(
        frame_kernel_grad_kernel,
        grid=(CAP,),
        in_specs=[pl.BlockSpec((1, CHIP, D), lambda c: (c, 0, 0))]
        + [pl.BlockSpec((width, CHIP), lambda c: (0, c))] * BANDS,
        out_specs=[pl.BlockSpec((1, width, D), lambda c: (c, 0, 0))] * BANDS,
        out_shape=[like((CAP, width, D), bf16)] * BANDS,
        compiler_params=params(62),
        cost_estimate=SHORT,
        name="frame_kernel_grad",
    )(de, *pix)


def frame_pixel_grad_kernel(sens, core, de, *refs):
    n = (len(refs) - BANDS) // 2
    own, other, outs = refs[:n], refs[n : 2 * n], refs[2 * n :]
    lo = de[0, :, pl.ds(pl.multiple_of(core[0] * HALF, HALF), HALF)]
    hi = de[0, :, pl.ds(pl.multiple_of((1 - core[0]) * HALF, HALF), HALF)]
    out, at = 0, 0
    for a, b in zip(own, other):
        rows = a.shape[1]
        outs[out][at : at + rows, :] = (mm_nt(a[0], lo) + mm_nt(b[0], hi)).astype(bf16)
        at += rows
        if at == outs[out].shape[0]:
            out, at = out + 1, 0


def frame_pixel_grad(sens, core, de, own, other):
    width = SLOTS * PIX
    kernels = [pl.BlockSpec((1, v.shape[1], HALF), lambda c, s, _: (s[c], 0, 0)) for v in own]
    return pl.pallas_call(
        frame_pixel_grad_kernel,
        grid_spec=pltpu.PrefetchScalarGridSpec(
            num_scalar_prefetch=2,
            grid=(CAP,),
            in_specs=[pl.BlockSpec((1, CHIP, D), lambda c, *_: (c, 0, 0))] + kernels + kernels,
            out_specs=[pl.BlockSpec((width, CHIP), lambda c, *_: (0, c))] * BANDS,
        ),
        out_shape=[like((width, FRAME), bf16)] * BANDS,
        compiler_params=params(62),
        cost_estimate=SHORT,
        name="frame_pixel_grad",
    )(sens, core, de, *own, *other)


def by_sensor_kernel(sens, valid, *refs):
    parts, out, acc = refs[:BANDS], refs[BANDS], refs[BANDS + 1]
    acc[...] = jnp.zeros_like(acc)
    for r in range(BANDS):
        for c in range(CAP):
            s = sens[r * CAP + c]
            acc[s] = acc[s] + parts[r][c].astype(f32)
    for s in range(SENSORS):
        for j in range(SLOTS):
            rows = slice(j * PIX, (j + 1) * PIX)
            keep = (valid[s * SLOTS + j] != 0).astype(f32)
            out[s, rows, :] = (acc[s, rows, :] * keep).astype(bf16)


def by_sensor(sens, valid, parts):
    width = SLOTS * PIX
    return pl.pallas_call(
        by_sensor_kernel,
        grid_spec=pltpu.PrefetchScalarGridSpec(
            num_scalar_prefetch=2,
            grid=(1,),
            in_specs=[whole((CAP, width, D))] * BANDS,
            out_specs=whole((SENSORS, width, D)),
            scratch_shapes=[pltpu.VMEM((SENSORS, width, D), f32)],
        ),
        out_shape=like((SENSORS, width, D), bf16),
        compiler_params=params(40),
        cost_estimate=SHORT,
        name="by_sensor",
    )(sens, valid, *parts)


def small_sums_kernel(sens, d_bup, small1, small2, tail, de, out, acc):
    acc[...] = jnp.zeros_like(acc)
    for c in range(CAP):
        row = pl.ds(sens[c], 1)
        acc[row, :] = acc[row, :] + total(col8(de[c].astype(f32)))
    for a in range(4):
        out[a : a + 1, :] = d_bup[0:1, a * D : (a + 1) * D]
    out[4:5, :] = small1[0:1, :]
    out[5:6, :] = small2[0:1, :]
    out[6:7, :] = small1[1:2, :]
    out[7:9, :] = small2[1:3, :]
    out[9:10, :] = total(tail[0:CAP, :])
    out[10:17, :] = acc[0:SENSORS, :]
    out[17:24, :] = jnp.zeros((7, D), f32)


def small_sums(sens, d_bup, small1, small2, tail, de):
    args = (d_bup, small1, small2, tail, de)
    return pl.pallas_call(
        small_sums_kernel,
        grid_spec=pltpu.PrefetchScalarGridSpec(
            num_scalar_prefetch=1,
            grid=(1,),
            in_specs=[whole(a.shape) for a in args],
            out_specs=whole((24, D)),
            scratch_shapes=[pltpu.VMEM((8, D), f32)],
        ),
        out_shape=like((24, D), f32),
        compiler_params=params(62),
        cost_estimate=SHORT,
        name="small_sums",
    )(sens, *args)


def columns_kernel(fc_kernel, smalls, *refs):
    *parts, cols_o, both_o = refs
    cols = tree_sum([p[...].astype(f32) for p in parts]).astype(bf16)
    cols_o[...] = cols
    cols = cols.astype(f32)
    dh = jnp.zeros((OWN, WG), f32)
    for i in range(cols.shape[1]):
        dh = dh + xmm(cols[:, i, :], fc_kernel[:, i * D : (i + 1) * D], ((1,), (1,)))
    both_o[:, :D] = smalls[...]
    both_o[:, D:] = jnp.concatenate([dh, jnp.zeros((24 - OWN, WG), f32)], axis=0)


def columns(fc_kernel, smalls, parts):
    shape = parts[0].shape
    return pl.pallas_call(
        columns_kernel,
        in_specs=[whole(fc_kernel.shape), whole((24, D))] + [whole(shape)] * len(parts),
        out_specs=[whole(shape), whole((24, D + WG))],
        out_shape=[like(shape, bf16), like((24, D + WG), f32)],
        compiler_params=params(40),
        cost_estimate=SHORT,
        name="columns",
    )(fc_kernel, smalls, *parts)


GH = 4
GW = GH * HD
GROUPS = HEADS // GH


def attn_fwd_kernel(n1, wq, wk, wv, wo, x0, qa, ka, gains, shifts, q_o, k_o, v_o, o_o, p_o, x1_o, n2_o):
    g = pl.program_id(0)

    @pl.when(g == 0)
    def _():
        x1_o[...] = x0[...]

    for c in range(RP // CH):
        s = pl.ds(c * CH, CH)
        q_o[s, :] = mm(n1[s, :], wq[...]).astype(bf16)
        k_o[s, :] = mm(n1[s, :], wk[...]).astype(bf16)
        v_o[s, :] = mm(n1[s, :], wv[...]).astype(bf16)
    qav = qa[...]
    kav = ka[...]
    for h in range(GH):
        hs = slice(h * HD, (h + 1) * HD)
        kh = jnp.concatenate([k_o[:, hs], kav], axis=1)
        vh = v_o[:, hs]
        for c in range(RP // CH):
            s = pl.ds(c * CH, CH)
            qh = jnp.concatenate([q_o[s, hs] * jnp.bfloat16(0.125), qav[c * CH : (c + 1) * CH]], axis=1)
            sc = mm_nt(qh, kh)
            e = jnp.exp(sc - jnp.max(sc, axis=1, keepdims=True))
            p = (e * (1.0 / jnp.sum(e, axis=1, keepdims=True))).astype(bf16)
            p_o[h, s, :] = p
            o_o[s, hs] = mm(p, vh).astype(bf16)
    for c in range(RP // CH):
        s = pl.ds(c * CH, CH)
        x1_o[s, :] += mm(o_o[s, :], wo[...])

    @pl.when(g == pl.num_programs(0) - 1)
    def _():
        for c in range(RP // CH):
            s = pl.ds(c * CH, CH)
            hat, _ = center(x1_o[s, :])
            n2_o[s, :] = (hat * gains[1:2, :] + shifts[1:2, :]).astype(bf16)


def attn_fwd(n1, weights, late, x0, qa, ka, gains, shifts):
    return pl.pallas_call(
        attn_fwd_kernel,
        grid=(GROUPS,),
        in_specs=[
            whole((RP, D)),
            pl.BlockSpec((D, GW), lambda g: (0, g)),
            pl.BlockSpec((D, GW), lambda g: (0, GROUPS + g)),
            pl.BlockSpec((D, GW), lambda g: (0, 2 * GROUPS + g)),
            pl.BlockSpec((GW, D), lambda g: (g, 8)),
            whole((RP, D)),
            whole((RP, HD)),
            whole((RP, HD)),
            whole((8, D)),
            whole((8, D)),
        ],
        out_specs=[pl.BlockSpec((RP, GW), lambda g: (0, g))] * 4
        + [pl.BlockSpec((GH, RP, RP), lambda g: (g, 0, 0)), whole((RP, D)), whole((RP, D))],
        out_shape=[like((RP, D), bf16)] * 4
        + [like((HEADS, RP, RP), bf16), like((RP, D), f32), like((RP, D), bf16)],
        compiler_params=params(60),
        cost_estimate=pl.CostEstimate(flops=5 * 10**10, bytes_accessed=50 * MIB, transcendentals=0),
        name="attn_fwd",
    )(n1, weights, weights, weights, late, x0, qa, ka, gains, shifts)


def attn_bwd_kernel(
    dx1b, wo, q, k, v, o, p, wq, wk, wv, x0, dx1, gains,
    dq_o, dk_o, dv_o, de_o, tail_o, small_o, dn1_s, do_s, ds_s,
):
    g = pl.program_id(0)

    @pl.when(g == 0)
    def _():
        dn1_s[...] = jnp.zeros_like(dn1_s)

    for c0, cn in BACK_ROWS:
        s = pl.ds(c0, cn)
        do_s[s, :] = mm_nt(dx1b[s, :], wo[...]).astype(bf16)
    for h in range(GH):
        hs = slice(h * HD, (h + 1) * HD)
        vh = v[:, hs]
        kh = k[:, hs]
        qh = q[:, hs]
        doh = do_s[:, hs]
        for c0, cn in BACK_ROWS:
            s = pl.ds(c0, cn)
            dc = do_s[s, hs]
            inner = jnp.sum(dc.astype(f32) * o[s, hs].astype(f32), axis=1, keepdims=True)
            ds = (p[h, s, :].astype(f32) * (mm_nt(dc, vh) - inner)).astype(bf16)
            ds_s[s, :] = ds
            dq_o[s, hs] = (mm(ds, kh) * 0.125).astype(bf16)
        dk_o[:, hs] = (mm(qh.T, ds_s[...]) * 0.125).T.astype(bf16)
        dv_o[:, hs] = mm(doh.T, p[h]).T.astype(bf16)
    for c0, cn in BACK_ROWS:
        s = pl.ds(c0, cn)
        dn1_s[s, :] += mm_nt(dq_o[s, :], wq[...]) + mm_nt(dk_o[s, :], wk[...]) + mm_nt(dv_o[s, :], wv[...])

    @pl.when(g == pl.num_programs(0) - 1)
    def _():
        gg = jnp.zeros((8, D), f32)
        gs = jnp.zeros((8, D), f32)
        for c0, cn in BACK_ROWS:
            s = pl.ds(c0, cn)
            hat, r = center(x0[s, :])
            gr = dn1_s[s, :]
            gg = gg + col8(gr * hat)
            gs = gs + col8(gr)
            dn1_s[s, :] = dx1[s, :] + norm_back(gr, hat, r, gains[0:1, :])
        de_o[...] = dn1_s[:FRAME, :].astype(bf16)
        tail_o[...] = dn1_s[FRAME:, :]
        small_o[0:1, :] = total(gg)
        small_o[1:2, :] = total(gs)
        small_o[2:8, :] = jnp.zeros((6, D), f32)


def attn_bwd(dx1b, weights, late, q, k, v, o, p, x0, dx1, gains):
    col = pl.BlockSpec((RP, GW), lambda g: (0, g))
    return pl.pallas_call(
        attn_bwd_kernel,
        grid=(GROUPS,),
        in_specs=[
            whole((RP, D)),
            pl.BlockSpec((GW, D), lambda g: (g, 8)),
            col,
            col,
            col,
            col,
            pl.BlockSpec((GH, RP, RP), lambda g: (g, 0, 0)),
            pl.BlockSpec((D, GW), lambda g: (0, g)),
            pl.BlockSpec((D, GW), lambda g: (0, GROUPS + g)),
            pl.BlockSpec((D, GW), lambda g: (0, 2 * GROUPS + g)),
            whole((RP, D)),
            whole((RP, D)),
            whole((8, D)),
        ],
        out_specs=[col, col, col, whole((FRAME, D)), whole((RP - FRAME, D)), whole((8, D))],
        out_shape=[like((RP, D), bf16)] * 3 + [like((FRAME, D), bf16), like((RP - FRAME, D), f32), like((8, D), f32)],
        scratch_shapes=[pltpu.VMEM((RP, D), f32), pltpu.VMEM((RP, GW), bf16), pltpu.VMEM((RP, RP), bf16)],
        compiler_params=params(62),
        cost_estimate=pl.CostEstimate(flops=5 * 10**10, bytes_accessed=50 * MIB, transcendentals=0),
        name="attn_bwd",
    )(dx1b, late, q, k, v, o, p, weights, weights, weights, x0, dx1, gains)


def proj_grad_kernel(share, core, n1, dq, dk, dv, o, dx1b, qkv_o, out_o):
    def split(v, out, columns):
        if share % 8:
            parts = (v[: v.shape[0] // 2], v[v.shape[0] // 2 :])
        else:
            pieces = [v[i * share : (i + 1) * share] for i in range(v.shape[0] // share)]
            parts = (jnp.concatenate(pieces[0::2], axis=0), jnp.concatenate(pieces[1::2], axis=0))
        for parity, part in enumerate(parts):
            slot = parity if share % 8 else core[0] if parity == 0 else 1 - core[0]
            out[slot, :, columns] = part.astype(bf16)

    for i, part in enumerate((dq, dk, dv)):
        split(mm_tn(n1[...], part[...]), qkv_o, slice(i * GW, (i + 1) * GW))
    split(mm_tn(o[...], dx1b[...]), out_o, slice(0, GW))


def proj_grad(share, core, n1, dq, dk, dv, o, dx1b):
    col = pl.BlockSpec((RP, GW), lambda g, c: (0, g))
    return pl.pallas_call(
        lambda *refs: proj_grad_kernel(share, *refs),
        grid_spec=pltpu.PrefetchScalarGridSpec(
            num_scalar_prefetch=1,
            grid=(GROUPS,),
            in_specs=[whole((RP, D)), col, col, col, whole((RP, D)), col],
            out_specs=[
                pl.BlockSpec((2, D // 2, 3 * GW), lambda g, c: (0, 0, g)),
                pl.BlockSpec((2, D // 2, GW), lambda g, c: (0, 0, g)),
            ],
        ),
        out_shape=[like((2, D // 2, 3 * D), bf16), like((2, D // 2, D), bf16)],
        compiler_params=params(62),
        cost_estimate=SHORT,
        name="proj_grad",
    )(core, n1, dq, dk, dv, o, dx1b)


FB = 768


def ffn_kernel(
    share, n2, dout, x1, wup, bup, wdown, gains, shifts,
    out, dw, dbup, dx1_o, dx1b_o, small_o, act_s, du_s, dn2_s, out_s, wd_s, dup_s, ddown_s, sems,
):
    j = pl.program_id(0)
    steps = pl.num_programs(0)
    rows = FB // 4
    shards_here = rows // share

    @pl.when(j == 0)
    def _():
        out_s[...] = x1[...] + shifts[2:3, :]
        dn2_s[...] = jnp.zeros_like(dn2_s)

    wd = wdown[...].astype(f32)
    wd_s[...] = jnp.concatenate(
        [wd[i * share : (i + 1) * share, a * D : (a + 1) * D] for i in range(shards_here) for a in range(4)], axis=0
    ).astype(bf16)
    cs = jnp.zeros((8, FB), f32)
    for c in range(RP // CH):
        s = pl.ds(c * CH, CH)
        u = mm(n2[s, :], wup[...]) + bup[...]
        da = mm_nt(dout[s, :], wd_s[...]).astype(bf16).astype(f32)
        act, slope = gelu_parts(u)
        act = act.astype(bf16)
        act_s[s, :] = act
        du = (da * slope).astype(bf16)
        du_s[s, :] = du
        cs = cs + col8(du.astype(f32))
        out_s[s, :] += mm(act, wd_s[...])
        dn2_s[s, :] += mm_nt(du, wup[...])
    dbup[...] = jnp.broadcast_to(total(cs), (8, FB))

    def copies(step):
        slot = lax.rem(step, 2)
        up = pltpu.make_async_copy(
            dup_s.at[slot], dw.at[:, pl.ds(pl.multiple_of(step * FB, FB), FB)], sems.at[0, slot]
        )
        down = pltpu.make_async_copy(
            ddown_s.at[slot], dw.at[pl.ds(pl.multiple_of(step * rows, rows), rows), pl.ds(FF, FF)], sems.at[1, slot]
        )
        return up, down

    @pl.when(j >= 2)
    def _():
        for copy in copies(j - 2):
            copy.wait()

    slot = lax.rem(j, 2)
    dup_s[slot] = mm_tn(n2[...], du_s[...]).astype(bf16)
    dd = mm_tn(act_s[...], dout[...])
    for a in range(4):
        ddown_s[slot, :, a * D : (a + 1) * D] = jnp.concatenate(
            [dd[(4 * i + a) * share : (4 * i + a + 1) * share] for i in range(shards_here)], axis=0
        ).astype(bf16)
    for copy in copies(j):
        copy.start()

    @pl.when(j == steps - 1)
    def _():
        out[...] = out_s[:ROWS, :]
        gg = jnp.zeros((8, D), f32)
        gs = jnp.zeros((8, D), f32)
        gd = jnp.zeros((8, D), f32)
        for c in range(RP // CH):
            s = pl.ds(c * CH, CH)
            hat, r = center(x1[s, :])
            g = dn2_s[s, :]
            do = dout[s, :].astype(f32)
            gg = gg + col8(g * hat)
            gs = gs + col8(g)
            gd = gd + col8(do)
            dx1 = do + norm_back(g, hat, r, gains[1:2, :])
            dx1_o[s, :] = dx1
            dx1b_o[s, :] = dx1.astype(bf16)
        small_o[0:1, :] = total(gg)
        small_o[1:2, :] = total(gs)
        small_o[2:3, :] = total(gd)
        small_o[3:8, :] = jnp.zeros((5, D), f32)
        for step in (steps - 2, steps - 1):
            for copy in copies(step):
                copy.wait()


def ffn(share, n2, dout, x1, weights, b_up, gains, shifts):
    return pl.pallas_call(
        lambda *refs: ffn_kernel(share, *refs),
        grid=(FF // FB,),
        in_specs=[
            whole((RP, D)),
            whole((RP, D)),
            whole((RP, D)),
            pl.BlockSpec((D, FB), lambda g: (0, 4 + g)),
            pl.BlockSpec((1, FB), lambda g: (0, g)),
            pl.BlockSpec((FB // 4, FF), lambda g: (g, 0)),
            whole((8, D)),
            whole((8, D)),
        ],
        out_specs=[
            whole((ROWS, D)),
            pl.BlockSpec(memory_space=pl.ANY),
            pl.BlockSpec((8, FB), lambda g: (0, g)),
            whole((RP, D)),
            whole((RP, D)),
            whole((8, D)),
        ],
        out_shape=[
            like((ROWS, D), f32),
            like((D, 2 * FF), bf16),
            like((8, FF), f32),
            like((RP, D), f32),
            like((RP, D), bf16),
            like((8, D), f32),
        ],
        scratch_shapes=[pltpu.VMEM((RP, FB), bf16)] * 2
        + [pltpu.VMEM((RP, D), f32)] * 2
        + [
            pltpu.VMEM((FB, D), bf16),
            pltpu.VMEM((2, D, FB), bf16),
            pltpu.VMEM((2, FB // 4, FF), bf16),
            pltpu.SemaphoreType.DMA((2, 2)),
        ],
        compiler_params=params(62),
        cost_estimate=pl.CostEstimate(flops=45 * 10**9, bytes_accessed=30 * MIB, transcendentals=0),
        name="ffn",
    )(n2, dout, x1, weights, b_up, weights, gains, shifts)


def flip(v, axis, bits):
    return lax.ppermute(v, axis, [(i, i ^ bits) for i in range(lax.axis_size(axis))])


def terms(v, axis, step, count):
    return [v] + [flip(v, axis, k * step) for k in range(1, count)]


def tree_sum(parts):
    parts = list(parts)
    while len(parts) > 1:
        parts = [parts[i] + parts[i + 1] for i in range(0, len(parts), 2)]
    return parts[0]


def in_order(parts, place):
    parts = list(parts)
    bit = 1
    while bit < len(parts):
        odd = (place & bit) != 0
        parts = [jnp.where(odd, parts[i ^ bit], parts[i]) for i in range(len(parts))]
        bit *= 2
    return parts


def pick(v, i, axis=0):
    return lax.dynamic_index_in_dim(v, i, axis, keepdims=False)


def sum_low(parts):
    return tree_sum([p.astype(f32) for p in parts])


def scatter_core(v, core):
    got = flip(pick(v, 1 - core, 2), "tok", 1)
    return sum_low([pick(v, core, 2), got]).astype(bf16)


def scatter_band(v, band):
    return sum_low([pick(v, band)] + [flip(pick(v, band ^ r), "band", r) for r in range(1, BANDS)])


def scatter_z(v, z, axis=0):
    return sum_low([pick(v, z, axis)] + [flip(pick(v, z ^ k, axis), "tok", 2 * k) for k in range(1, v.shape[axis])])


def sum_tok(v, chips):
    v = v + flip(v, "tok", 1)
    return tree_sum(terms(v, "tok", 2, chips))


def wave_features(wavelengths, wave_index):
    table_size = wavelengths.shape[0]
    picked = (wave_index[..., None] == jnp.arange(table_size, dtype=jnp.int32)).astype(f32)
    wave_values = jnp.sum(picked * wavelengths, axis=-1)
    half_width = WG // 2
    frequency = 1.0 / 10000.0 ** (jnp.arange(half_width, dtype=f32) / half_width)
    angles = 1000.0 * wave_values[..., None] * frequency
    return jnp.concatenate([jnp.sin(angles), jnp.cos(angles)], axis=-1)


def shards(
    pixels, wavelengths, wave_index, band_counts, sensors, chip_lengths, meta_rows,
    w_qkv, w_out, w_up, b_up, w_down, norm_gains, shifts,
    gen_qkv, gen_out, gen_ff1, gen_ff2, gen_gains, gen_shifts, latent_tokens, bias_token,
    fc_kernel, fc_bias, d_out,
):
    band = lax.axis_index("band")
    tok = lax.axis_index("tok")
    toks = lax.axis_size("tok")
    chips = toks // 2
    core = tok % 2
    z = tok // 2
    devices = BANDS * toks
    me = band * toks + tok
    share = D // devices
    ff_share = FF // devices
    pix_share = PIX // toks
    width = SLOTS * PIX

    pix_t = pixels.reshape(BANDS, FRAME, width).transpose(0, 2, 1)
    pix = [pick(pix_t, band)] + [flip(pick(pix_t, band ^ r), "band", r) for r in range(1, BANDS)]

    late = jnp.concatenate([w_down.reshape(4, share, D).transpose(1, 0, 2).reshape(share, FF), w_up, w_out], axis=1)
    late = lax.all_gather(late, BT, axis=0, tiled=True)

    vectors = jnp.concatenate([norm_gains.T, shifts.T, b_up.reshape(share, 4)], axis=1)
    vectors = jnp.pad(vectors, ((0, 0), (0, WG - vectors.shape[1])))
    bundle = terms(jnp.concatenate([w_qkv, vectors], axis=1), "tok", 2, chips)

    features = wave_features(wavelengths, wave_index).reshape(SENSORS * BMAX, WG)
    valid = jnp.arange(BMAX, dtype=jnp.int32)[None, :] < band_counts[:, None]
    seq = jnp.concatenate([features, jnp.zeros((4, WG), f32), jnp.broadcast_to(bias_token, (8, WG))], axis=0)
    sensor_ids = jnp.arange(SENSORS, dtype=jnp.int32)
    row_sensor = jnp.concatenate(
        [jnp.repeat(sensor_ids, BMAX), jnp.full((4,), 8, jnp.int32), sensor_ids, jnp.full((1,), 9, jnp.int32)]
    )
    key_ok = jnp.concatenate([valid.reshape(-1), jnp.zeros((4,), jnp.bool_), jnp.ones((8,), jnp.bool_)])
    allowed = (row_sensor[:, None] == row_sensor[None, :]) & key_ok[None, :]
    gen_bias = jnp.concatenate([jnp.zeros((QX, NLAT), f32), jnp.where(allowed, 0.0, MASKED)], axis=1)
    gen_args = (seq, latent_tokens, gen_bias, gen_qkv, gen_out, gen_ff1, gen_ff2, gen_gains, gen_shifts, fc_bias)
    own_row = sensor_ids[:, None] * BMAX + band * SLOTS + jnp.arange(SLOTS, dtype=jnp.int32)[None, :]
    own_valid = lax.dynamic_slice_in_dim(valid, band * SLOTS, SLOTS, 1).reshape(OWN)
    chosen = (own_row.reshape(OWN, 1) == jnp.arange(QX, dtype=jnp.int32)[None, :]) & own_valid[:, None]
    chosen = jnp.pad(chosen.astype(f32), ((0, 3), (0, 0)))
    z2, bias_vec, part, *kept = gen_fwd(*gen_args, chosen, fc_kernel)
    z2, part, pix, bundle = lax.optimization_barrier((z2, part, pix, bundle))
    h_all = (z2[: SENSORS * BMAX] + features).reshape(SENSORS, BMAX, WG)

    ends = jnp.cumsum(chip_lengths.reshape(BANDS, CAP), axis=-1)
    starts = jnp.arange(CAP, dtype=jnp.int32) * CHIP
    block_segment = jnp.sum((ends[:, None, :] <= starts[None, :, None]).astype(jnp.int32), axis=-1)
    block_sensor = jnp.take_along_axis(sensors.reshape(BANDS, CAP), block_segment, axis=1)
    own_ends = pick(ends, band)
    frame_sensor = [pick(block_sensor, band ^ r) for r in range(BANDS)]
    positions = jnp.arange(FRAME, dtype=jnp.int32)
    patch_segment = jnp.sum((own_ends[None, :] <= positions[:, None]).astype(jnp.int32), axis=-1)
    slot_ids = jnp.arange(CAP, dtype=jnp.int32)
    segment = jnp.concatenate([patch_segment, slot_ids, slot_ids, jnp.full((RP - ROWS,), CAP + 1, jnp.int32)])
    onehot = segment[:, None] == jnp.arange(HD, dtype=jnp.int32)[None, :]
    ka = onehot.astype(bf16)
    qa = jnp.where(onehot, 0.0, -(2.0**30)).astype(bf16)

    part = part[:OWN].reshape(OWN, pix_share, 2, HALF)
    mine = pick(part, core, 2)
    got = flip(pick(part, 1 - core, 2), "tok", 1)
    pair = jnp.where(core == 0, jnp.concatenate([mine, got], axis=1), jnp.concatenate([got, mine], axis=1))
    bundle = terms(jnp.stack(in_order(bundle, z)), "band", 1, BANDS)
    pairs = terms(pair, "tok", 2, chips)
    pairs, bundle = lax.optimization_barrier((pairs, bundle))
    k_own = jnp.concatenate(in_order(pairs, z), axis=1).reshape(SENSORS, width, HALF)
    k_x = flip(k_own, "band", 1)
    k_y = flip(k_own, "band", 2)
    bundle = jnp.stack(in_order(bundle, band))
    bundle_other = flip(bundle, "tok", 1)
    half = width // 2
    k_x, k_y, bundle_other = lax.optimization_barrier((k_x, k_y, bundle_other))
    ker_own = [k_own, k_x, k_y, flip(k_x[:, :half], "band", 2), flip(k_y[:, half:], "band", 1)]
    ker_other = [flip(v, "tok", 1) for v in ker_own]
    weights = jnp.where(
        core == 0, jnp.stack([bundle, bundle_other], axis=2), jnp.stack([bundle_other, bundle], axis=2)
    ).reshape(D, 3 * D + WG)
    rest = weights[:, 3 * D : 3 * D + 10].astype(f32)
    bias_up = rest[:, 6:10].reshape(1, FF)
    rest = rest.T
    gains = jnp.pad(rest[:2], ((0, 6), (0, 0)))
    shift_rows = jnp.pad(rest[2:6], ((0, 4), (0, 0)))

    extra_rows = jnp.concatenate(
        [
            jnp.broadcast_to(shift_rows[3], (CAP, D)),
            meta_rows.reshape(CAP, D).astype(f32),
            jnp.zeros((RP - ROWS, D), f32),
        ],
        axis=0,
    )
    which = core.reshape(1)
    parts = [(pix[0], 0), (pix[1], 0), (pix[2], 0), (pix[3], 0), (pix[3], 1)]
    x0, n1 = embed(frame_sensor[0], which, parts, ker_own, ker_other, bias_vec, extra_rows, gains, shift_rows)
    q, k, v, o, probs, x1, n2 = attn_fwd(n1, weights, late, x0, qa, ka, gains, shift_rows)
    dout = jnp.pad(d_out.reshape(ROWS, D), ((0, RP - ROWS), (0, 0)))
    out, d_ff, d_bup, dx1, dx1b, small2 = ffn(share, n2, dout, x1, late, bias_up, gains, shift_rows)
    d_ff = lax.psum_scatter(d_ff, BT, scatter_dimension=0, tiled=True).astype(f32)
    dq, dk, dv, de, tail_rows, small1 = attn_bwd(dx1b, weights, late, q, k, v, o, probs, x0, dx1, gains)

    de_blocks = de.reshape(CAP, CHIP, D)
    ker_grads = frame_kernel_grad(de_blocks, pix)
    ker_grads, n1, o, tail_rows = lax.optimization_barrier((ker_grads, n1, o, tail_rows))
    ker_grads = [ker_grads[0]] + [flip(ker_grads[r], "band", r) for r in range(1, BANDS)]
    proj = proj_grad(share, which, n1, dq, dk, dv, o, dx1b)
    if share % 8:
        proj = [v.reshape(D // (2 * share), 2, share, v.shape[2]) for v in proj]
        proj = [jnp.stack([pick(v, core, 1), pick(v, 1 - core, 1)]) for v in proj]
    proj = [v.reshape(2, BANDS, chips, share, -1) for v in proj]
    proj = [sum_low([v[0], flip(v[1], "tok", 1)]).astype(bf16) for v in proj]
    d_proj = scatter_z(jnp.concatenate(proj, axis=-1), z, 1).astype(bf16)
    pix_grads = frame_pixel_grad(frame_sensor[0], which, de_blocks, ker_own, ker_other)
    smalls = small_sums(frame_sensor[0], d_bup, small1, small2, tail_rows, de_blocks)

    ker_grads, pix_grads, d_proj, smalls = lax.optimization_barrier((ker_grads, pix_grads, d_proj, smalls))
    d_ker = by_sensor(jnp.concatenate(frame_sensor), own_valid.astype(jnp.int32), ker_grads)
    d_ker = scatter_core(d_ker.reshape(1, OWN * chips, 2, pix_share, D), core)
    d_ker = d_ker.reshape(OWN, chips, pix_share, D)
    d_ker = [pick(d_ker, z, 1)] + [flip(pick(d_ker, z ^ c, 1), "tok", 2 * c) for c in range(1, chips)]
    d_proj = scatter_band(d_proj, band)
    d_ker, d_proj = lax.optimization_barrier((d_ker, d_proj))
    d_cols, both = columns(fc_kernel, smalls, d_ker)
    d_wqkv = d_proj[:, : 3 * D].reshape(share, GROUPS, 3, GW).transpose(0, 2, 1, 3).reshape(share, 3 * D)
    d_pix = in_order([pix_grads[0]] + [flip(pix_grads[r], "band", r) for r in range(1, BANDS)], band)
    d_pix = jnp.stack(d_pix).astype(f32)
    d_ff_up = d_ff[:, :FF]
    d_ff_down = d_ff[:, FF:].reshape(share, 4, D).transpose(1, 0, 2).reshape(ff_share, D)
    d_cols_all = jnp.stack(in_order(terms(d_cols, "band", 1, BANDS), band), axis=0)
    d_cols_all = (
        d_cols_all.reshape(BANDS, SENSORS, SLOTS, pix_share * D)
        .transpose(1, 0, 2, 3)
        .reshape(SENSORS * BMAX, pix_share * D)
        .astype(f32)
    )
    d_fc = xmm(h_all.reshape(SENSORS * BMAX, WG), d_cols_all, ((0,), (0,)))
    bit = 1
    while bit < toks:
        both = both + flip(both, "tok", bit)
        bit *= 2
    got = flip(both, "band", 1)
    smalls = both[:, :D] + got[:, :D]
    both = jnp.concatenate([smalls, both[:, D:], got[:, D:]], axis=1)
    got = flip(both, "band", 2)
    smalls = smalls + got[:, :D]
    dh = [v[:OWN, at : at + WG] for v in (both, got) for at in (D, D + WG)]
    dh = jnp.stack(in_order(dh, band)).reshape(BANDS, SENSORS, SLOTS, WG)
    dh = dh.transpose(1, 0, 2, 3).reshape(SENSORS * BMAX, WG)

    dh, d_fc, d_ff_down = lax.optimization_barrier((dh, d_fc, d_ff_down))
    dbias_full = jnp.pad(smalls[10:17], ((0, 1), (0, 0)))
    g = gen_bwd(
        seq, latent_tokens, gen_qkv, gen_out, gen_ff1, gen_ff2, gen_gains, fc_bias, z2, kept,
        jnp.pad(dh, ((0, 4), (0, 0))), dbias_full,
    )
    bup_shard = lax.dynamic_slice_in_dim(smalls[0:4].reshape(FF), me * ff_share, ff_share, 0)
    gains_shard = lax.dynamic_slice_in_dim(smalls[4:6], me * share, share, 1)
    shifts_shard = lax.dynamic_slice_in_dim(smalls[6:10], me * share, share, 1)
    return (
        out.reshape(1, 1, ROWS, D),
        d_pix.transpose(0, 2, 1).reshape(BANDS, 1, FRAME, width),
        tail_rows[CAP : 2 * CAP].reshape(1, 1, CAP, D),
        d_wqkv,
        d_proj[:, 3 * D :],
        d_ff_up,
        bup_shard,
        d_ff_down,
        gains_shard,
        shifts_shard,
        g[0],
        g[1],
        g[2],
        g[3],
        g[4],
        g[5],
        g[6],
        g[7].reshape(WG),
        d_fc,
        g[8],
    )


def solution(mesh):
    both = ("band", "tok")
    placed = (
        P(None, "tok", None, "band"),
        P(),
        P(),
        P(),
        P(None, "tok", None),
        P(None, "tok", None),
        P("band", "tok", None, None),
        P(both, None),
        P(both, None),
        P(both, None),
        P(both),
        P(both, None),
        P(None, both),
        P(None, both),
        P(),
        P(),
        P(),
        P(),
        P(),
        P(),
        P(),
        P(),
        P(None, "tok"),
        P(),
        P("band", "tok", None, None),
    )
    return jax.shard_map(
        shards,
        mesh=mesh,
        in_specs=placed,
        out_specs=(
            P("band", "tok", None, None),
            P(None, "tok", None, "band"),
            P("band", "tok", None, None),
            P(both, None),
            P(both, None),
            P(both, None),
            P(both),
            P(both, None),
            P(None, both),
            P(None, both),
            P(),
            P(),
            P(),
            P(),
            P(),
            P(),
            P(),
            P(),
            P(None, "tok"),
            P(),
        ),
        check_vma=False,
    )
```
